128 devices in a mesh: section: 2 (over z_hi), dp: 64 (over z_lo, x, y, core).
Axes of the slice: x: 4, y: 4, z: 4 (z_hi: 2, z_lo: 2; z = z_hi * 2 + z_lo), core: 2. Of those that a mesh axis runs over, the one named last changes fastest.
Arguments:
- fields: bfloat16 [16384, 640], P('dp'), may hold values from -6 to 6
- behaviour: bfloat16 [16384, 3200], P('dp'), may hold values from -6 to 6
- lengths: int32 [16384], P('dp'), may hold values from 1 to 200, as said below
- domains: int32 [16384], P('dp'), may hold values from 0 to 1
- validity: int32 [16384], P('dp'), may hold values from 0 to 1, as said below
- cotangent: float32 [16384], P('dp'), may hold values from -6 to 6
- w_query: float32 [16, 16], replicated, may hold values from -1.5 to 1.5
- w_key: float32 [16, 16], replicated, may hold values from -1.5 to 1.5
- w_value: float32 [16, 16], replicated, may hold values from -1.5 to 1.5
- w_proj: bfloat16 [640, 512], replicated, may hold values from -0.25 to 0.25
- b_proj: float32 [512], replicated, may hold values from -0.6 to 0.6
- norm_gain: float32 [512], replicated, may hold values from 0.5 to 1.5
- norm_shift: float32 [512], replicated, may hold values from -0.6 to 0.6
- gate_weight: bfloat16 [512, 7], replicated, may hold values from -0.1875 to 0.1875
- w_in: bfloat16 [6, 512, 1024], replicated, may hold values from -0.25 to 0.25
- b_in: float32 [6, 1024], replicated, may hold values from -0.6 to 0.6
- w_out: bfloat16 [6, 1024, 512], replicated, may hold values from -0.1875 to 0.1875
- b_out: float32 [6, 512], replicated, may hold values from -0.6 to 0.6
- tower_in: bfloat16 [512, 512], replicated, may hold values from -0.25 to 0.25
- tower_bias: float32 [512], replicated, may hold values from -0.6 to 0.6
- tower_out: float32 [512], replicated, may hold values from -0.375 to 0.375
- tower_end: float32 [2], replicated, may hold values from -3 to 3
Outputs:
- predictions: float32 [2, 16384], P('section', 'dp')
- field_grad: float32 [2, 16384, 640], P('section', 'dp')
- behaviour_grad: float32 [2, 16384, 3200], P('section', 'dp')
- query_grad: float32 [2, 16, 16], P('section')
- key_grad: float32 [2, 16, 16], P('section')
- value_grad: float32 [2, 16, 16], P('section')
- proj_grad: float32 [2, 640, 512], P('section')
- proj_bias_grad: float32 [2, 512], P('section')
- gain_grad: float32 [2, 512], P('section')
- shift_grad: float32 [2, 512], P('section')
- gate_grad: float32 [2, 512, 7], P('section')
- in_grad: float32 [2, 6, 512, 1024], P('section')
- in_bias_grad: float32 [2, 6, 1024], P('section')
- out_grad: float32 [2, 6, 1024, 512], P('section')
- out_bias_grad: float32 [2, 6, 512], P('section')
- tower_in_grad: float32 [2, 512, 512], P('section')
- tower_bias_grad: float32 [2, 512], P('section')
- tower_out_grad: float32 [2, 512], P('section')
- tower_end_grad: float32 [2, 2], P('section')
- root_means: float32 [2, 2], P('section')
The draws below stay inside these ranges and needn't reach their ends.
Inputs may be any that keep to these rules, and one draw needn't show every extreme that they name: `lengths`: the first event of every aligned block of 64 events has length 200. `validity`: the first event of every aligned block of 64 events is valid.
All inputs are finite; a program needn't handle non-finite values.
Results may differ from the reference program's by a relative error of at most 0.011.
Values may be sent and summed in bfloat16 or wider, within the bound.
A program may use at most 256 MiB of HBM per device.

```python
import jax
import jax.numpy as jnp
from jax import lax

E = 16
L = 200
H = 512
X = 1024
TW = 256
SHARED = 2
DOMAINS = 2
DEXP = 2
EV_DEV = 64
FE = 640
LE = 3200
EXP = 6
NG = 7
EVENTS = 16384
N_DP = 64


def draw_lengths(key, part):
    key = jax.random.fold_in(key, 11)
    first_key, second_key = jax.random.split(key)
    first_draw = jax.random.randint(first_key, (EVENTS,), 1, L + 1)
    second_draw = jax.random.randint(second_key, (EVENTS,), 1, L + 1)
    places = jnp.arange(EVENTS).astype(jnp.int32)
    return jnp.where(places % EV_DEV == 0, L, jnp.minimum(first_draw, second_draw)).astype(jnp.int32)


def draw_validity(key, part):
    key = jax.random.fold_in(key, 23)
    places = jnp.arange(EVENTS).astype(jnp.int32)
    ticket = jax.random.randint(key, (EVENTS,), 0, 1000)
    threshold = 250 + 650 * places // EVENTS
    return jnp.where((places % EV_DEV == 0) | (ticket < threshold), 1, 0).astype(jnp.int32)


def touch_ends(values, rng, least, top_value):
    longest = values.shape.index(max(values.shape))
    spots = []
    for shift in (0, 1):
        where = [jax.random.randint(jax.random.fold_in(rng, axis), (), 0, length) for axis, length in enumerate(values.shape)]
        where[longest] = (where[longest] + shift) % values.shape[longest]
        spots.append(tuple(where))
    return values.at[spots[0]].set(least).at[spots[1]].set(top_value)


def shard_levels(stream_key, shape, cuts, least, largest):
    gain = 1.0
    for position, shards_of in cuts:
        heights = jax.random.uniform(jax.random.fold_in(jax.random.fold_in(stream_key, 6), position), (shards_of,), jnp.float32, least / len(cuts), largest / len(cuts))
        gain = gain * jnp.repeat(jnp.exp(heights), shape[position] // shards_of).reshape((-1,) + (1,) * (len(shape) - 1 - position))
    return gain


def scatter_about(stream_key, dims, width, most, cuts=(), dtype=jnp.bfloat16):
    values = width * jax.random.normal(stream_key, dims, jnp.float32)
    if cuts:
        values = values * shard_levels(stream_key, dims, cuts, -0.22, 0.18)
    return jnp.clip(values, -most, most).astype(dtype)


def setup_inputs(seed: int = 0) -> dict:
    seeds = jax.random.split(jax.random.key(seed), 23)
    fields = scatter_about(seeds[0], (EVENTS, FE), 1.0, 6.0, ((0, 64),))
    behaviour = scatter_about(seeds[1], (EVENTS, LE), 1.0, 6.0, ((0, 64),))
    lengths = draw_lengths(jax.random.fold_in(seeds[22], 71), 0)
    domains = touch_ends(jax.random.randint(seeds[3], (EVENTS,), 0, DOMAINS), jax.random.fold_in(seeds[3], 1), 0, DOMAINS - 1).astype(jnp.int32)
    validity = draw_validity(jax.random.fold_in(seeds[22], 71), 0)
    cotangent = scatter_about(seeds[5], (EVENTS,), 1.0, 6.0, ((0, 64),), jnp.float32)
    w_query = scatter_about(seeds[6], (E, E), E ** -0.5, 1.5, (), jnp.float32)
    w_key = scatter_about(seeds[7], (E, E), E ** -0.5, 1.5, (), jnp.float32)
    w_value = scatter_about(seeds[8], (E, E), E ** -0.5, 1.5, (), jnp.float32)
    w_proj = scatter_about(seeds[9], (FE, H), FE ** -0.5, 0.25)
    b_proj = scatter_about(seeds[10], (H,), 0.1, 0.6, (), jnp.float32)
    norm_gain = jnp.clip(1.0 + 0.1 * jax.random.normal(seeds[11], (H,), jnp.float32), 0.5, 1.5)
    norm_shift = scatter_about(seeds[12], (H,), 0.1, 0.6, (), jnp.float32)
    gate_weight = scatter_about(seeds[13], (H, NG), (2 * H) ** -0.5, 0.1875)
    w_in = scatter_about(seeds[14], (EXP, H, X), H ** -0.5, 0.25)
    b_in = scatter_about(seeds[15], (EXP, X), 0.1, 0.6, (), jnp.float32)
    w_out = scatter_about(seeds[16], (EXP, X, H), X ** -0.5, 0.1875)
    b_out = scatter_about(seeds[17], (EXP, H), 0.1, 0.6, (), jnp.float32)
    tower_in = scatter_about(seeds[18], (H, DOMAINS * TW), H ** -0.5, 0.25)
    tower_bias = scatter_about(seeds[19], (DOMAINS * TW,), 0.1, 0.6, (), jnp.float32)
    tower_out = scatter_about(seeds[20], (DOMAINS * TW,), TW ** -0.5, 0.375, (), jnp.float32)
    tower_end = scatter_about(seeds[21], (DOMAINS,), 0.5, 3.0, (), jnp.float32)
    return dict(fields=fields, behaviour=behaviour, lengths=lengths, domains=domains, validity=validity, cotangent=cotangent, w_query=w_query, w_key=w_key, w_value=w_value, w_proj=w_proj, b_proj=b_proj, norm_gain=norm_gain, norm_shift=norm_shift, gate_weight=gate_weight, w_in=w_in, b_in=b_in, w_out=w_out, b_out=b_out, tower_in=tower_in, tower_bias=tower_bias, tower_out=tower_out, tower_end=tower_end)


PRECISE = lax.Precision.HIGHEST
EPSILON = 1e-05

@jax.custom_vjp
def low(v):
    return lax.optimization_barrier(v.astype(jnp.bfloat16)).astype(jnp.float32)

@jax.custom_vjp
def low_back(v):
    return v

def low_keep(v):
    return (low(v), None)

def low_pass(kept, grad):
    return (grad,)

def back_keep(v):
    return (v, None)

def back_low(kept, grad):
    return (low(grad),)
low.defvjp(low_keep, low_pass)
low_back.defvjp(back_keep, back_low)

def soft_max(values):
    peak = lax.optimization_barrier(jnp.max(values, axis=-1, keepdims=True))
    raised = jnp.exp(values - peak)
    return raised / lax.optimization_barrier(jnp.sum(raised, axis=-1, keepdims=True))

def layer_norm(values, norm_gain, norm_shift):
    centred = values - lax.optimization_barrier(jnp.mean(values, axis=1, keepdims=True))
    spread = lax.optimization_barrier(jnp.mean(centred * centred, axis=1, keepdims=True))
    return centred * lax.rsqrt(spread + EPSILON) * norm_gain + norm_shift

def mix_gates(logits, onehot):
    row_count = logits.shape[0]
    shared = soft_max(logits[:, :SHARED])
    level_gate = jax.nn.sigmoid(logits[:, -1:])
    domain_logits = logits[:, SHARED:SHARED + DOMAINS * DEXP].reshape(row_count, DOMAINS, DEXP)
    chosen = soft_max(domain_logits) * onehot[:, :, None]
    return jnp.concatenate([level_gate * shared, (1.0 - level_gate) * chosen.reshape(row_count, DOMAINS * DEXP)], axis=1)

def forward(fields, behaviour, w_query, w_key, w_value, w_proj, b_proj, norm_gain, norm_shift, gate_weight, w_in, b_in, w_out, b_out, tower_in, tower_bias, tower_out, tower_end, lengths, domains):
    row_count = fields.shape[0]
    target = fields[:, :E]
    sequence = behaviour.reshape(row_count, L, E)
    query_vec = jnp.dot(target, w_query, precision=PRECISE)
    key_probe = jnp.dot(query_vec, w_key.T, precision=PRECISE)
    scores = 0.5 * jnp.einsum('rle,re->rl', sequence, key_probe, precision=PRECISE)
    inside = lax.broadcasted_iota(jnp.int32, scores.shape, 1) < lengths[:, None]
    attn = soft_max(jnp.where(inside, scores, -1e+30))
    pooled = jnp.einsum('rl,rle->re', attn, sequence, precision=PRECISE)
    joined = low(jnp.concatenate([fields[:, E:], jnp.dot(pooled, w_value, precision=PRECISE)], axis=1))
    projected = low_back(jnp.dot(joined, w_proj, precision=PRECISE) + b_proj)
    activation = low_back(low(jax.nn.gelu(projected)))
    normed = low(layer_norm(activation, norm_gain, norm_shift))
    onehot = (domains[:, None] == lax.broadcasted_iota(jnp.int32, (row_count, DOMAINS), 1)).astype(jnp.float32)
    mixing = mix_gates(low_back(jnp.dot(normed, gate_weight, precision=PRECISE)), onehot)
    expert_pre = low_back(jnp.einsum('rh,ehx->erx', normed, w_in, precision=PRECISE) + b_in[:, None, :])
    active = low(jax.nn.gelu(expert_pre))
    expert = low_back(jnp.einsum('erx,exh->erh', active, w_out, precision=PRECISE) + b_out[:, None, :])
    branch = lax.optimization_barrier(jnp.sum(mixing.T[:, :, None] * expert, axis=0))
    residual = activation + branch
    tower_pre = low_back(jnp.dot(low(residual), tower_in, precision=PRECISE) + tower_bias)
    per_domain = lax.optimization_barrier(jnp.sum((jax.nn.gelu(tower_pre) * tower_out).reshape(row_count, DOMAINS, TW), axis=2))
    predict = jax.nn.sigmoid(lax.optimization_barrier(jnp.sum(onehot * (per_domain + tower_end), axis=1)))
    return (predict, (residual, branch))

def to_wide(array):
    return array.astype(jnp.float32)

def zeros_of(array):
    return jnp.zeros(array.shape, jnp.float32)

def first_only(array):
    return jnp.stack([array, jnp.zeros_like(array)])

def second_only(array):
    return jnp.stack([jnp.zeros_like(array), array])

def reference(fields, behaviour, lengths, domains, validity, cotangent, w_query, w_key, w_value, w_proj, b_proj, norm_gain, norm_shift, gate_weight, w_in, b_in, w_out, b_out, tower_in, tower_bias, tower_out, tower_end):
    params = jax.tree.map(to_wide, (w_query, w_key, w_value, w_proj, b_proj, norm_gain, norm_shift, gate_weight, w_in, b_in, w_out, b_out, tower_in, tower_bias, tower_out, tower_end))
    block_rows = EVENTS // N_DP
    pieces = (fields.astype(jnp.float32).reshape(N_DP, block_rows, FE), behaviour.astype(jnp.float32).reshape(N_DP, block_rows, LE), lengths.reshape(N_DP, block_rows), domains.reshape(N_DP, block_rows), validity.reshape(N_DP, block_rows), cotangent.astype(jnp.float32).reshape(N_DP, block_rows))

    def one_block(totals, piece):
        part_fields, part_seq, part_len, part_dom, part_valid, part_cot = piece

        def local_forward(field_rows, seq_rows, *weights):
            return forward(field_rows, seq_rows, *weights, part_len, part_dom)
        predict, pull_back, extra = jax.vjp(local_forward, part_fields, part_seq, *params, has_aux=True)
        residual, branch = extra
        kept = part_valid.astype(jnp.float32)
        gradient = pull_back(predict * 0.0 + part_cot * kept)
        statistics = jnp.stack([jnp.sum(kept * lax.optimization_barrier(jnp.sum(residual * residual, axis=1))), jnp.sum(kept * lax.optimization_barrier(jnp.sum(branch * branch, axis=1))), jnp.sum(kept)])
        totals = jax.tree.map(jnp.add, totals, (tuple(gradient[2:]), statistics))
        return (totals, (predict, gradient[0], gradient[1]))
    start_totals = (jax.tree.map(zeros_of, params), jnp.zeros((3,), jnp.float32))
    totals, outputs = lax.scan(one_block, start_totals, pieces)
    weight_grads, statistics = totals
    predict = outputs[0].reshape(EVENTS)
    field_rows = outputs[1].reshape(EVENTS, FE)
    seq_rows = outputs[2].reshape(EVENTS, LE)
    root_means = jnp.sqrt(statistics[:2] / (H * statistics[2]) + EPSILON)
    return (second_only(predict), first_only(field_rows), first_only(seq_rows), first_only(weight_grads[0]), first_only(weight_grads[1]), first_only(weight_grads[2]), first_only(weight_grads[3]), first_only(weight_grads[4]), second_only(weight_grads[5]), second_only(weight_grads[6]), second_only(weight_grads[7]), second_only(weight_grads[8]), second_only(weight_grads[9]), second_only(weight_grads[10]), second_only(weight_grads[11]), second_only(weight_grads[12]), second_only(weight_grads[13]), second_only(weight_grads[14]), second_only(weight_grads[15]), second_only(root_means))
```

```python
from functools import partial

import jax
import jax.numpy as jnp
from jax import lax
from jax.experimental import pallas as pl
from jax.experimental.pallas import tpu as pltpu
from jax.sharding import PartitionSpec as P

SHARED = 2
DEXP = 2
PRECISE = lax.Precision.HIGHEST
EPSILON = 1e-05
MESH = pl.DeviceIdType.MESH
LANES = 128
PARTS = 6
HALVINGS = 3
CHUNKS = 4
MID_ROWS = 384
SMALL_ROWS = 128
F32 = jnp.float32
BF16 = jnp.bfloat16


def coords():
    section, place = lax.axis_index("section"), lax.axis_index("dp")
    return 2 * section + place // 32, (place // 8) % 4, (place // 2) % 4, place % 2


def device_at(z, x, y, core):
    return {"section": z // 2, "dp": (((z % 2) * 4 + x) * 4 + y) * 2 + core}


def hop(r, kind):
    near, far = 1 - 2 * (r % 2), 3 - 2 * r
    return near + kind * (far - near)


def side(r, kind):
    near = (r + r // 2) % 2
    return near + kind * (r // 2 - near)


def picks(dim):
    a = dim % 3
    return (1 - a) * (2 - a) // 2, a * (2 - a), a * (a - 1) // 2, dim // 3


def neighbour(dim):
    z, x, y, core = coords()
    ex, ey, ez, kind = picks(dim)
    return device_at(z + ez * hop(z, kind), x + ex * hop(x, kind), y + ey * hop(y, kind), core)


def which_half(dim):
    z, x, y, core = coords()
    ex, ey, ez, kind = picks(dim)
    return ex * side(x, kind) + ey * side(y, kind) + ez * side(z, kind)


class Family:
    def __init__(self, rows, refs):
        self.rows = rows
        self.share = rows >> HALVINGS
        (
            self.source,
            self.kept,
            self.from_core,
            self.arrived,
            self.doubled,
            self.total,
            self.send_sem,
            self.recv_sem,
        ) = refs

    def remote(self, unit, slot, src, dst, to):
        return pltpu.make_async_remote_copy(
            src_ref=src,
            dst_ref=dst,
            send_sem=self.send_sem.at[unit, slot],
            recv_sem=self.recv_sem.at[unit, slot],
            device_id=to,
            device_id_type=MESH,
        )

    def start_of(self, part, step):
        start = 0
        for k in range(step):
            start = start + which_half((part + k) % 6) * (self.rows >> (k + 1))
        return start

    def span(self, start, size):
        return pl.ds(pl.multiple_of(start, size), size)

    def across(self, unit):
        z, x, y, core = coords()
        return self.remote(
            unit, 0, self.source.at[unit, 1 - core], self.from_core.at[unit], device_at(z, x, y, 1 - core)
        )

    def halve(self, unit, part, k):
        size = self.rows >> (k + 1)
        dim = (part + k) % 6
        start = self.start_of(part, k) + (1 - which_half(dim)) * size
        return self.remote(
            unit,
            1 + k,
            self.kept.at[unit, self.span(start, size)],
            self.arrived.at[unit, pl.ds(self.rows - 2 * size, size)],
            neighbour(dim),
        )

    def double(self, unit, part, j):
        dim = (part + HALVINGS + j) % 6
        if j == 0:
            src = self.kept.at[unit, self.span(self.start_of(part, HALVINGS), self.share)]
        else:
            src = self.doubled.at[unit, j - 1]
        return self.remote(
            unit,
            1 + HALVINGS + j,
            src,
            self.arrived.at[unit, pl.ds(self.rows - self.share + j * self.share, self.share)],
            neighbour(dim),
        )

    def spread(self, unit, part, k):
        size = self.rows >> (k + 1)
        core = coords()[3]
        region = self.total.at[unit, core, self.span(self.start_of(part, k + 1), size)]
        return self.remote(unit, 7 + k, region, region, neighbour((part + k) % 6))

    def back(self, unit):
        z, x, y, core = coords()
        region = self.total.at[unit, core]
        return self.remote(unit, 7 + HALVINGS, region, region, device_at(z, x, y, 1 - core))

    def task(self, unit, part, t):
        core = coords()[3]
        dtype = self.kept.dtype
        if t == 0:
            self.across(unit).start()
        elif t == 1:
            self.across(unit).wait_recv()
            mine = self.source[unit, core].astype(F32) + self.from_core[unit].astype(F32)
            self.kept[unit] = mine.astype(dtype)
            self.halve(unit, part, 0).start()
        elif t < 2 + HALVINGS:
            k = t - 2
            size = self.rows >> (k + 1)
            self.halve(unit, part, k).wait_recv()
            region = self.span(self.start_of(part, k + 1), size)
            came = self.arrived[unit, pl.ds(self.rows - 2 * size, size)]
            self.kept[unit, region] = (self.kept[unit, region].astype(F32) + came.astype(F32)).astype(dtype)
            if k + 1 < HALVINGS:
                self.halve(unit, part, k + 1).start()
            else:
                self.double(unit, part, 0).start()
        elif t < 8:
            j = t - 2 - HALVINGS
            self.double(unit, part, j).wait_recv()
            region = self.span(self.start_of(part, HALVINGS), self.share)
            old = self.kept[unit, region] if j == 0 else self.doubled[unit, j - 1]
            came = self.arrived[unit, pl.ds(self.rows - self.share + j * self.share, self.share)]
            new = (old.astype(F32) + came.astype(F32)).astype(dtype)
            if j < 5 - HALVINGS:
                self.doubled[unit, j] = new
                self.double(unit, part, j + 1).start()
            else:
                self.total[unit, core, region] = new
                self.spread(unit, part, HALVINGS - 1).start()
        elif t < 8 + HALVINGS:
            k = HALVINGS - 1 - (t - 8)
            self.spread(unit, part, k).wait_recv()
            if k > 0:
                self.spread(unit, part, k - 1).start()
            else:
                self.back(unit).start()
        else:
            self.back(unit).wait_recv()

    def drain(self, unit, part):
        self.across(unit).wait_send()
        for k in range(HALVINGS):
            self.halve(unit, part, k).wait_send()
        for j in range(6 - HALVINGS):
            self.double(unit, part, j).wait_send()
        for k in range(HALVINGS):
            self.spread(unit, part, k).wait_send()
        self.back(unit).wait_send()


TASKS = 9 + HALVINGS


def family_scratch(units, rows, dtype):
    share = rows >> HALVINGS
    return [
        pltpu.VMEM((units, rows, LANES), dtype),
        pltpu.VMEM((units, rows, LANES), dtype),
        pltpu.VMEM((units, rows - share + (6 - HALVINGS) * share, LANES), dtype),
        pltpu.VMEM((units, 5 - HALVINGS, share, LANES), dtype),
        pltpu.VMEM((units, 2, rows, LANES), dtype),
        pltpu.SemaphoreType.DMA((units, 8 + HALVINGS)),
        pltpu.SemaphoreType.DMA((units, 8 + HALVINGS)),
    ]


FAMILIES = ((PARTS * CHUNKS, 1024, BF16), (PARTS, MID_ROWS, BF16), (1, SMALL_ROWS, F32))


def sum_kernel(*refs):
    sources, outs, rest = refs[:3], refs[3:6], refs[6:]
    families = [
        Family(rows, (source, *rest[7 * i : 7 * i + 7]))
        for i, ((_, rows, _), source) in enumerate(zip(FAMILIES, sources))
    ]
    out_sem = rest[21]
    z, x, y, core = coords()
    barrier = pltpu.get_barrier_semaphore()
    for dim in range(6):
        pl.semaphore_signal(barrier, inc=1, device_id=neighbour(dim), device_id_type=MESH)
    pl.semaphore_signal(barrier, inc=1, device_id=device_at(z, x, y, 1 - core), device_id_type=MESH)
    pl.semaphore_wait(barrier, 7)
    chunks = [(families[0], n * PARTS, PARTS) for n in range(CHUNKS)]
    chunks += [(families[1], 0, PARTS), (families[2], 0, 1)]
    for tick in range(TASKS + len(chunks) - 1):
        for n in reversed(range(len(chunks))):
            t = tick - n
            if 0 <= t < TASKS:
                family, base, parts = chunks[n]

                def one(part, _, family=family, base=base, t=t):
                    family.task(base + part, part, t)
                    return 0

                lax.fori_loop(0, parts, one, 0)
    copies = []
    for i, family in enumerate(families):
        copies.append(pltpu.make_async_copy(family.total, outs[i], out_sem.at[i]))
        copies[-1].start()
    for family, base, parts in chunks:

        def finish(part, _, family=family, base=base):
            family.drain(base + part, part)
            return 0

        lax.fori_loop(0, parts, finish, 0)
    for copy in copies:
        copy.wait()


def sum_everywhere(big, mid, small):
    scratch = []
    for family in FAMILIES:
        scratch += family_scratch(*family)
    return pl.pallas_call(
        sum_kernel,
        out_shape=[jax.ShapeDtypeStruct((units, 2, rows, LANES), dtype) for units, rows, dtype in FAMILIES],
        in_specs=[pl.BlockSpec(memory_space=pltpu.VMEM)] * 3,
        out_specs=[pl.BlockSpec(memory_space=pl.ANY)] * 3,
        scratch_shapes=scratch + [pltpu.SemaphoreType.DMA((3,))],
        compiler_params=pltpu.CompilerParams(
            collective_id=0, has_side_effects=True, vmem_limit_bytes=62 << 20
        ),
        name="sum_everywhere",
    )(big, mid, small)


def place_kernel(
    out_units,
    in_units,
    mid,
    small,
    out_grad,
    in_grad,
    proj,
    tower,
    b_proj,
    gain,
    shift,
    tower_b,
    tower_o,
    tower_e,
    roots,
    gate,
    in_b,
    out_b,
    query,
    key,
    value,
):
    second = (lax.axis_index("section") == 1).astype(F32)
    first = 1.0 - second
    for core in range(2):
        for j in range(2):
            column = 2 * core + j
            out_grad[0, 0, :, column * LANES : (column + 1) * LANES] = out_units[j, core].astype(F32) * second
            for i in range(2):
                column = 4 * core + 2 * j + i
                block = in_units[j, core, i * 512 : (i + 1) * 512].astype(F32)
                in_grad[0, 0, :, column * LANES : (column + 1) * LANES] = block * second

    @pl.when(pl.program_id(0) == 0)
    def _():
        for core in range(2):
            for i in range(PARTS):
                column = core * 2 + i // 3
                lanes = slice(column * LANES, (column + 1) * LANES)
                block = mid[i, core].astype(F32)
                if i % 3 == 0:
                    tower[0, :384, lanes] = block * second
                elif i % 3 == 1:
                    tower[0, 384:, lanes] = block[:128] * second
                    proj[0, :256, lanes] = block[128:] * first
                else:
                    proj[0, 256:, lanes] = block * first

        def rows(start, count):
            return jnp.concatenate(
                [small[core, j * 64 + start : j * 64 + start + count] for core in range(2) for j in range(2)],
                axis=1,
            )

        head = rows(0, 8)
        b_proj[...] = head[0:1] * first
        gain[...] = head[1:2] * second
        shift[...] = head[2:3] * second
        tower_b[...] = head[3:4] * second
        tower_o[...] = head[4:5] * second
        tower_e[...] = head[5:6, 0:2] * second
        count = head[5:6, 4:5]
        squares = head[5:6, 2:4] / (512.0 * jnp.maximum(count, 1.0)) + EPSILON
        roots[...] = jnp.where(count > 0.0, jnp.sqrt(squares), 0.0) * second
        gate[0] = jnp.transpose(rows(8, 8))[:, :7] * second
        in_b[0, :, :512] = rows(16, 6) * second
        in_b[0, :, 512:] = rows(24, 6) * second
        out_b[0] = rows(32, 6) * second
        three = rows(48, 16)
        query[0] = three[:, 0:16] * first
        key[0] = three[:, 16:32] * first
        value[0] = three[:, 32:48] * first


def place(big, mid, small):
    def whole(*shape):
        return jax.ShapeDtypeStruct(shape, F32), pl.BlockSpec(shape, lambda i: (0,) * len(shape))

    shapes, specs = zip(
        (jax.ShapeDtypeStruct((1, 6, 1024, 512), F32), pl.BlockSpec((1, 1, 1024, 512), lambda i: (0, i, 0, 0))),
        (jax.ShapeDtypeStruct((1, 6, 512, 1024), F32), pl.BlockSpec((1, 1, 512, 1024), lambda i: (0, i, 0, 0))),
        whole(1, 640, 512),
        whole(1, 512, 512),
        whole(1, 512),
        whole(1, 512),
        whole(1, 512),
        whole(1, 512),
        whole(1, 512),
        whole(1, 2),
        whole(1, 2),
        whole(1, 512, 7),
        whole(1, 6, 1024),
        whole(1, 6, 512),
        whole(1, 16, 16),
        whole(1, 16, 16),
        whole(1, 16, 16),
    )
    return pl.pallas_call(
        place_kernel,
        grid=(6,),
        out_shape=shapes,
        in_specs=[
            pl.BlockSpec((2, 2, 1024, LANES), lambda i: (i, 0, 0, 0)),
            pl.BlockSpec((2, 2, 1024, LANES), lambda i: (i + 6, 0, 0, 0)),
            pl.BlockSpec((PARTS, 2, MID_ROWS, LANES), lambda i: (0, 0, 0, 0)),
            pl.BlockSpec((2, SMALL_ROWS, LANES), lambda i: (0, 0, 0)),
        ],
        out_specs=specs,
        compiler_params=pltpu.CompilerParams(vmem_limit_bytes=56 << 20),
        name="place",
    )(big, big, mid, small)


def soft_max(values):
    peak = jnp.max(values, axis=-1, keepdims=True)
    raised = jnp.exp(values - peak)
    return raised / jnp.sum(raised, axis=-1, keepdims=True)


def layer_norm(values, norm_gain, norm_shift):
    centred = values - jnp.mean(values, axis=1, keepdims=True)
    spread = jnp.mean(centred * centred, axis=1, keepdims=True)
    return centred * lax.rsqrt(spread + EPSILON) * norm_gain + norm_shift


def mix_gates(logits, onehot):
    row_count = logits.shape[0]
    domain_count = onehot.shape[1]
    shared = soft_max(logits[:, :SHARED])
    level_gate = jax.nn.sigmoid(logits[:, -1:])
    domain_logits = logits[:, SHARED : SHARED + domain_count * DEXP].reshape(
        row_count, domain_count, DEXP
    )
    chosen = soft_max(domain_logits) * onehot[:, :, None]
    return jnp.concatenate(
        [level_gate * shared, (1.0 - level_gate) * chosen.reshape(row_count, domain_count * DEXP)],
        axis=1,
    )


def contract_rows(left, right):
    return lax.dot_general(left, right, (((0,), (0,)), ((), ())), preferred_element_type=F32)


def contract_cols(left, right):
    return lax.dot_general(left, right, (((1,), (1,)), ((), ())), preferred_element_type=F32)


def exact(left, right):
    return jnp.dot(left, right, precision=PRECISE)


def attend(target, sequence, row_lengths, w_query, w_key, w_value, gather, tile):
    query_vec = exact(target, w_query)
    key_probe = exact(query_vec, w_key.T)
    scores = 0.5 * exact(sequence * exact(key_probe, tile), gather)
    inside = lax.broadcasted_iota(jnp.int32, scores.shape, 1) < row_lengths[:, None]
    attn = soft_max(jnp.where(inside, scores, -1e30))
    pooled = exact(exact(attn, gather.T) * sequence, tile.T)
    return exact(pooled, w_value)


def body(
    fields,
    behaviour,
    lengths,
    domains,
    validity,
    cotangent,
    w_query,
    w_key,
    w_value,
    w_proj,
    b_proj,
    norm_gain,
    norm_shift,
    gate_weight,
    w_in,
    b_in,
    w_out,
    b_out,
    tower_in,
    tower_bias,
    tower_out,
    tower_end,
):
    section = lax.axis_index("section")
    all_rows = fields.shape[0]
    batch_rows = all_rows // 2
    field_width = w_query.shape[0]
    all_width = fields.shape[1]
    seq_width = behaviour.shape[1]
    hidden = norm_gain.shape[0]
    domain_count = tower_end.shape[0]
    tower_width = tower_in.shape[1] // domain_count
    positions = seq_width // field_width

    def own(array):
        return lax.dynamic_slice_in_dim(array, section * batch_rows, batch_rows, 0)

    def both(array):
        other = lax.ppermute(array, "section", [(0, 1), (1, 0)])
        return jnp.where(
            section == 0, jnp.concatenate([array, other], axis=0), jnp.concatenate([other, array], axis=0)
        )

    spot = lax.broadcasted_iota(jnp.int32, (seq_width, positions), 0) // field_width
    gather = (spot == lax.broadcasted_iota(jnp.int32, (seq_width, positions), 1)).astype(F32)
    feature = lax.broadcasted_iota(jnp.int32, (field_width, seq_width), 1) % field_width
    tile = (feature == lax.broadcasted_iota(jnp.int32, (field_width, seq_width), 0)).astype(F32)

    target = fields[:, :field_width].astype(F32)
    sequence = behaviour.astype(F32)

    def attend_local(target_in, sequence_in, query_w, key_w, value_w):
        return attend(target_in, sequence_in, lengths, query_w, key_w, value_w, gather, tile)

    value_part, attend_back = jax.vjp(attend_local, target, sequence, w_query, w_key, w_value)
    joined = own(jnp.concatenate([fields[:, field_width:], value_part.astype(BF16)], axis=1))
    projected = jnp.dot(joined, w_proj, preferred_element_type=F32) + b_proj
    activation, gelu_back = jax.vjp(jax.nn.gelu, projected)
    activation = activation.astype(BF16).astype(F32)

    domain_ids, is_valid, cot_rows = own(domains), own(validity).astype(F32), own(cotangent)
    onehot = (
        domain_ids[:, None] == lax.broadcasted_iota(jnp.int32, (batch_rows, domain_count), 1)
    ).astype(F32)
    normed, norm_back = jax.vjp(layer_norm, activation, norm_gain, norm_shift)
    normed_low = normed.astype(BF16)
    logits = jnp.dot(normed_low, gate_weight, preferred_element_type=F32)
    mixing, mix_back = jax.vjp(partial(mix_gates, onehot=onehot), logits)
    expert_pre = (
        jnp.einsum("rh,ehx->erx", normed_low, w_in, preferred_element_type=F32) + b_in[:, None, :]
    )
    active, active_back = jax.vjp(jax.nn.gelu, expert_pre)
    active_low = active.astype(BF16)
    expert = (
        jnp.einsum("erx,exh->erh", active_low, w_out, preferred_element_type=F32) + b_out[:, None, :]
    )
    branch = jnp.sum(mixing.T[:, :, None] * expert, axis=0)
    residual = activation + branch
    statistics = jnp.stack(
        [
            jnp.sum(is_valid * jnp.sum(residual * residual, axis=1)),
            jnp.sum(is_valid * jnp.sum(branch * branch, axis=1)),
            jnp.sum(is_valid),
        ]
    )
    residual_low = residual.astype(BF16)
    tower_pre = jnp.dot(residual_low, tower_in, preferred_element_type=F32) + tower_bias
    tower_act, tower_back = jax.vjp(jax.nn.gelu, tower_pre)
    per_domain = jnp.sum((tower_act * tower_out).reshape(batch_rows, domain_count, tower_width), axis=2)
    predict = jax.nn.sigmoid(jnp.sum(onehot * (per_domain + tower_end), axis=1))
    d_logit = cot_rows * is_valid * predict * (1.0 - predict)
    d_domain = onehot * d_logit[:, None]
    d_tower_end = jnp.sum(d_domain, axis=0)
    d_spread = jnp.broadcast_to(
        d_domain[:, :, None], (batch_rows, domain_count, tower_width)
    ).reshape(batch_rows, domain_count * tower_width)
    d_tower_out = jnp.sum(tower_act * d_spread, axis=0)
    d_tower_pre = tower_back(d_spread * tower_out)[0].astype(BF16)
    d_tower_in = contract_rows(residual_low, d_tower_pre)
    d_tower_bias = jnp.sum(d_tower_pre.astype(F32), axis=0)
    d_residual = contract_cols(d_tower_pre, tower_in)
    d_expert = (mixing.T[:, :, None] * d_residual[None]).astype(BF16)
    d_mixing = jnp.sum(expert * d_residual[None], axis=2).T
    d_w_out = jnp.einsum("erx,erh->exh", active_low, d_expert, preferred_element_type=F32)
    d_b_out = jnp.sum(d_expert.astype(F32), axis=1)
    d_active = jnp.einsum("erh,exh->erx", d_expert, w_out, preferred_element_type=F32)
    d_expert_pre = active_back(d_active)[0].astype(BF16)
    d_w_in = jnp.einsum("rh,erx->ehx", normed_low, d_expert_pre, preferred_element_type=F32)
    d_b_in = jnp.sum(d_expert_pre.astype(F32), axis=1)
    d_normed = jnp.einsum("erx,ehx->rh", d_expert_pre, w_in, preferred_element_type=F32)
    d_logits = mix_back(d_mixing)[0].astype(BF16)
    d_gate = contract_rows(normed_low, d_logits)
    d_normed = d_normed + contract_cols(d_logits, gate_weight)
    d_activation, d_gain, d_shift = norm_back(d_normed)
    d_activation = (d_activation + d_residual).astype(BF16).astype(F32)

    d_projected = gelu_back(d_activation)[0].astype(BF16)
    d_proj = contract_rows(joined, d_projected)
    d_bias = jnp.sum(d_projected.astype(F32), axis=0)
    d_joined = contract_cols(both(d_projected), w_proj)
    d_target, d_sequence, d_query, d_key, d_value = attend_back(d_joined[:, all_width - field_width :])
    d_fields = jnp.concatenate([d_target, d_joined[:, : all_width - field_width]], axis=1)
    predicted = both(predict)

    first = (section == 0).astype(F32)
    experts = w_in.shape[0]
    out_units = d_w_out.reshape(experts, 1024, 2, 2, LANES).transpose(0, 3, 2, 1, 4)
    in_units = d_w_in.reshape(experts, 512, 2, 2, 2, LANES).transpose(0, 3, 2, 4, 1, 5)
    big = jnp.concatenate(
        [out_units.reshape(12, 2, 1024, LANES), in_units.reshape(12, 2, 1024, LANES)], axis=0
    ).astype(BF16)
    mid = jnp.concatenate([d_tower_in, d_proj], axis=0).astype(BF16)
    mid = mid.reshape(3, MID_ROWS, 2, 2, LANES).transpose(3, 0, 2, 1, 4).reshape(PARTS, 2, MID_ROWS, LANES)

    def rows(array, count):
        array = array.reshape(-1, array.shape[-1])
        return jnp.pad(array, ((0, count - array.shape[0]), (0, 512 - array.shape[1])))

    small = jnp.concatenate(
        [
            rows(d_bias, 1),
            rows(d_gain, 1),
            rows(d_shift, 1),
            rows(d_tower_bias, 1),
            rows(d_tower_out, 1),
            rows(jnp.concatenate([d_tower_end, statistics]), 3),
            rows(d_gate.T, 8),
            rows(d_b_in[:, :512], 8),
            rows(d_b_in[:, 512:], 8),
            rows(d_b_out, 16),
            rows(jnp.concatenate([d_query, d_key, d_value], axis=1) * first, 16),
        ],
        axis=0,
    )
    small = small.reshape(64, 2, 2, LANES).transpose(1, 2, 0, 3).reshape(1, 2, SMALL_ROWS, LANES)
    big, mid, small = sum_everywhere(big, mid, small)
    (
        out_grad,
        in_grad,
        proj,
        tower,
        g_b_proj,
        gain,
        shift,
        tower_b,
        tower_o,
        tower_e,
        roots,
        gate,
        in_b,
        out_b,
        query,
        key,
        value,
    ) = place(big, mid, small.reshape(2, SMALL_ROWS, LANES))
    return (
        (predicted * (1.0 - first))[None],
        (d_fields * first)[None],
        (d_sequence * first)[None],
        query,
        key,
        value,
        proj,
        g_b_proj,
        gain,
        shift,
        gate,
        in_grad,
        in_b,
        out_grad,
        out_b,
        tower,
        tower_b,
        tower_o,
        tower_e,
        roots,
    )


def solution(mesh):
    each = (P("dp", None), P("dp", None), P("dp"), P("dp"), P("dp"), P("dp"))
    ranks = (2, 3, 3, 3, 3, 3, 3, 2, 2, 2, 3, 4, 3, 4, 3, 3, 2, 2, 2, 2)
    outs = tuple(
        P("section", "dp", *(None,) * (rank - 2)) if i < 3 else P("section", *(None,) * (rank - 1))
        for i, rank in enumerate(ranks)
    )
    return jax.shard_map(
        body, mesh=mesh, in_specs=each + (P(),) * 16, out_specs=outs, check_vma=False
    )
```

```python
import jax
import jax.numpy as jnp
from jax import lax
from jax.experimental import pallas as pl
from jax.experimental.pallas import tpu as pltpu
from jax.sharding import PartitionSpec as P

EPSILON = 1e-05
MESH = pl.DeviceIdType.MESH
F32 = jnp.float32
BF16 = jnp.bfloat16

LANES = 128
PARTS = 6
HALVINGS = 3
TASKS = 9 + HALVINGS
ROWS = 128
EXPERTS = 6
HIDDEN = 512
WIDE = 1024
FIELDS = 640
EMBED = 16
SEQ = 3200
SPOTS = 256
PIECES = tuple((at, 512) for at in range(0, 3072, 512)) + ((3072, 128),)
MID_ROWS = 384
SMALL_ROWS = 128
BLOCK = 64


def coords():
    section, place = lax.axis_index("section"), lax.axis_index("dp")
    return 2 * section + place // 32, (place // 8) % 4, (place // 2) % 4, place % 2


def device_at(z, x, y, core):
    return {"section": z // 2, "dp": (((z % 2) * 4 + x) * 4 + y) * 2 + core}


def hop(r, kind):
    near, far = 1 - 2 * (r % 2), 3 - 2 * r
    return near + kind * (far - near)


def side(r, kind):
    near = (r + r // 2) % 2
    return near + kind * (r // 2 - near)


def picks(dim):
    a = dim % 3
    return (1 - a) * (2 - a) // 2, a * (2 - a), a * (a - 1) // 2, dim // 3


def neighbour(dim):
    z, x, y, core = coords()
    ex, ey, ez, kind = picks(dim)
    return device_at(z + ez * hop(z, kind), x + ex * hop(x, kind), y + ey * hop(y, kind), core)


def which_half(dim):
    z, x, y, core = coords()
    ex, ey, ez, kind = picks(dim)
    return ex * side(x, kind) + ey * side(y, kind) + ez * side(z, kind)


def sibling():
    z, x, y, core = coords()
    return device_at(z, x, y, 1 - core)


def opposite():
    return {"section": 1 - lax.axis_index("section"), "dp": lax.axis_index("dp")}


class Family:
    def __init__(self, rows, out, refs, other_half, own_half):
        self.rows = rows
        self.share = rows >> HALVINGS
        self.out = out
        self.other_half = other_half
        self.own_half = own_half
        (
            self.sent,
            self.kept,
            self.from_core,
            self.arrived,
            self.doubled,
            self.send_sem,
            self.recv_sem,
            self.out_sem,
        ) = refs
        self.total = self.sent

    def remote(self, unit, slot, src, dst, to):
        return pltpu.make_async_remote_copy(
            src_ref=src,
            dst_ref=dst,
            send_sem=self.send_sem.at[unit, slot],
            recv_sem=self.recv_sem.at[unit, slot],
            device_id=to,
            device_id_type=MESH,
        )

    def start_of(self, part, step):
        start = 0
        for k in range(step):
            start = start + which_half((part + k) % 6) * (self.rows >> (k + 1))
        return start

    def span(self, start, size):
        return pl.ds(pl.multiple_of(start, size), size)

    def across(self, unit):
        return self.remote(unit, 0, self.sent.at[unit], self.from_core.at[unit], sibling())

    def halve(self, unit, part, k):
        size = self.rows >> (k + 1)
        dim = (part + k) % 6
        start = self.start_of(part, k) + (1 - which_half(dim)) * size
        return self.remote(
            unit,
            1 + k,
            self.kept.at[unit, self.span(start, size)],
            self.arrived.at[unit, pl.ds(self.rows - 2 * size, size)],
            neighbour(dim),
        )

    def double(self, unit, part, j):
        dim = (part + HALVINGS + j) % 6
        if j == 0:
            src = self.kept.at[unit, self.span(self.start_of(part, HALVINGS), self.share)]
        else:
            src = self.doubled.at[unit, j - 1]
        return self.remote(
            unit,
            1 + HALVINGS + j,
            src,
            self.arrived.at[unit, pl.ds(self.rows - self.share + j * self.share, self.share)],
            neighbour(dim),
        )

    def spread(self, unit, part, k):
        size = self.rows >> (k + 1)
        region = self.total.at[unit, self.span(self.start_of(part, k + 1), size)]
        return self.remote(unit, 7 + k, region, region, neighbour((part + k) % 6))

    def back(self, unit):
        core = coords()[3]
        return self.remote(unit, 7 + HALVINGS, self.total.at[unit], self.out.at[unit, core], sibling())

    def keep(self, unit):
        core = coords()[3]
        return pltpu.make_async_copy(self.total.at[unit], self.out.at[unit, core], self.out_sem.at[unit])

    def take(self, unit, part, own):
        self.across(unit).wait_send()
        self.across(unit).wait_recv()
        self.kept[unit] = (own + self.from_core[unit].astype(F32)).astype(self.kept.dtype)
        self.halve(unit, part, 0).start()

    def task(self, unit, part, t):
        dtype = self.kept.dtype
        if t < 2 + HALVINGS:
            k = t - 2
            size = self.rows >> (k + 1)
            self.halve(unit, part, k).wait_recv()
            region = self.span(self.start_of(part, k + 1), size)
            came = self.arrived[unit, pl.ds(self.rows - 2 * size, size)]
            self.kept[unit, region] = (self.kept[unit, region].astype(F32) + came.astype(F32)).astype(dtype)
            if k + 1 < HALVINGS:
                self.halve(unit, part, k + 1).start()
            else:
                self.double(unit, part, 0).start()
        elif t < 8:
            j = t - 2 - HALVINGS
            self.double(unit, part, j).wait_recv()
            region = self.span(self.start_of(part, HALVINGS), self.share)
            old = self.kept[unit, region] if j == 0 else self.doubled[unit, j - 1]
            came = self.arrived[unit, pl.ds(self.rows - self.share + j * self.share, self.share)]
            new = (old.astype(F32) + came.astype(F32)).astype(dtype)
            if j < 5 - HALVINGS:
                self.doubled[unit, j] = new
                self.double(unit, part, j + 1).start()
            else:
                self.total[unit, region] = new
                self.spread(unit, part, HALVINGS - 1).start()
        elif t < 8 + HALVINGS:
            k = HALVINGS - 1 - (t - 8)
            self.spread(unit, part, k).wait_recv()
            if k > 0:
                self.spread(unit, part, k - 1).start()
            else:
                self.back(unit).start()
                self.keep(unit).start()
        else:
            self.back(unit).wait_recv()

    def run(self, base, parts, t):
        if t == 0:
            self.other_half(self, base)
        elif t == 1:
            self.own_half(self, base)
        else:

            def one(part, _):
                self.task(base + part, part, t)
                return 0

            lax.fori_loop(0, parts, one, 0)

    def drain(self, base, parts):
        def one(part, _):
            unit = base + part
            for k in range(HALVINGS):
                self.halve(unit, part, k).wait_send()
            for j in range(6 - HALVINGS):
                self.double(unit, part, j).wait_send()
            for k in range(HALVINGS):
                self.spread(unit, part, k).wait_send()
            self.back(unit).wait_send()
            self.keep(unit).wait()
            return 0

        lax.fori_loop(0, parts, one, 0)


def family_scratch(units, rows, dtype):
    share = rows >> HALVINGS
    return [
        pltpu.VMEM((units, rows, LANES), dtype),
        pltpu.VMEM((units, rows, LANES), dtype),
        pltpu.VMEM((units, rows, LANES), dtype),
        pltpu.VMEM((units, rows - share + (6 - HALVINGS) * share, LANES), dtype),
        pltpu.VMEM((units, 5 - HALVINGS, share, LANES), dtype),
        pltpu.SemaphoreType.DMA((units, 8 + HALVINGS)),
        pltpu.SemaphoreType.DMA((units, 8 + HALVINGS)),
        pltpu.SemaphoreType.DMA((units,)),
    ]


FAMILIES = ((24, 1024, BF16), (PARTS, MID_ROWS, BF16), (1, SMALL_ROWS, F32))


def exact(left, right):
    return jnp.dot(left, right, precision=lax.Precision.HIGHEST, preferred_element_type=F32)


def exact_cols(left, right):
    return lax.dot_general(
        left, right, (((1,), (1,)), ((), ())), precision=lax.Precision.HIGHEST, preferred_element_type=F32
    )


def exact_rows(left, right):
    return lax.dot_general(
        left, right, (((0,), (0,)), ((), ())), precision=lax.Precision.HIGHEST, preferred_element_type=F32
    )


def product(left, right):
    return jnp.dot(left, right, preferred_element_type=F32)


def contract_rows(left, right):
    return lax.dot_general(left, right, (((0,), (0,)), ((), ())), preferred_element_type=F32)


def contract_cols(left, right):
    return lax.dot_general(left, right, (((1,), (1,)), ((), ())), preferred_element_type=F32)


def split(value, terms):
    out = []
    for _ in range(terms):
        out.append(value.astype(BF16))
        value = value - out[-1].astype(F32)
    return out


def sigmoid(v):
    return 1.0 / (1.0 + jnp.exp(-v))


ROOT = 0.7978845608028654
CUBE = 0.044715


def gelu_both(v):
    square = v * v
    bent = jnp.tanh(v * (ROOT + ROOT * CUBE * square))
    half = 0.5 + 0.5 * bent
    slope = half + 0.5 * v * (1.0 - bent * bent) * (ROOT + 3.0 * ROOT * CUBE * square)
    return v * half, slope


def column_sum(array):
    return jnp.sum(array, axis=0, keepdims=True)


def row_sum(array):
    return jnp.sum(array, axis=1, keepdims=True)


def lanes(shape):
    return lax.broadcasted_iota(jnp.int32, shape, 1)


def lane_match(rows, columns, period, shift=0):
    place = lax.broadcasted_iota(jnp.int32, (rows, columns), 1) - shift
    if period:
        place = place % period
    return (place == lax.broadcasted_iota(jnp.int32, (rows, columns), 0)).astype(F32)


def kernel(
    fields,
    packed,
    w_query,
    w_key,
    w_value,
    w_proj,
    gate_weight,
    b_in,
    b_out,
    tower_in,
    behaviour_hbm,
    w_in_hbm,
    w_out_hbm,
    big_out,
    mid_out,
    small_out,
    pred_all,
    d_fields,
    d_seq_hbm,
    behaviour,
    w_in,
    w_out,
    gather,
    proj_turned,
    info,
    joined,
    activation,
    proj_slope,
    normed,
    standard,
    active,
    slope,
    expert,
    d_expert,
    d_normed,
    d_residual,
    mixing,
    d_mixing,
    gates,
    residual_low,
    d_tower,
    d_proj_all,
    small,
    d_seq,
    load_sem,
    seq_sem,
    pair_send,
    pair_recv,
    *family_refs,
):
    section = lax.axis_index("section")
    core = coords()[3]
    own = pl.ds(pl.multiple_of(section * ROWS, ROWS), ROWS)
    rest = pl.ds(pl.multiple_of((1 - section) * ROWS, ROWS), ROWS)

    own_seq = pltpu.make_async_copy(behaviour_hbm.at[own], behaviour.at[own], load_sem.at[12])
    rest_seq = pltpu.make_async_copy(behaviour_hbm.at[rest], behaviour.at[rest], load_sem.at[13])

    def load_in(e):
        return pltpu.make_async_copy(w_in_hbm.at[e], w_in.at[e], load_sem.at[e])

    def load_out(e):
        return pltpu.make_async_copy(w_out_hbm.at[e], w_out.at[e], load_sem.at[6 + e])

    own_seq.start()
    for e in range(EXPERTS):
        load_in(e).start()
        load_out(e).start()
    rest_seq.start()

    barrier = pltpu.get_barrier_semaphore()
    for dim in range(6):
        pl.semaphore_signal(barrier, inc=1, device_id=neighbour(dim), device_id_type=MESH)
    pl.semaphore_signal(barrier, inc=1, device_id=sibling(), device_id_type=MESH)
    pl.semaphore_signal(barrier, inc=1, device_id=opposite(), device_id_type=MESH)

    for at, width in PIECES:
        spot = (lax.broadcasted_iota(jnp.int32, (width, SPOTS), 0) + at) // EMBED
        gather[at : at + width] = (spot == lanes((width, SPOTS))).astype(F32).astype(BF16)
    tile = lane_match(EMBED, 512, EMBED)
    proj_turned[:EMBED] = w_proj[FIELDS - EMBED :]
    proj_turned[EMBED:] = w_proj[: FIELDS - EMBED]
    info[...] = jnp.transpose(packed[8:16, :256])
    small[...] = jnp.zeros_like(small)

    def attention(rows):
        target = fields[rows, 0:LANES].astype(F32)[:, :EMBED]
        query = exact(target, w_query[...])
        probe = exact_cols(query, w_key[...])
        probe_tiled = exact(probe, tile)
        scores = 0.0
        for at, width in PIECES:
            terms = split(behaviour[rows, at : at + width].astype(F32) * probe_tiled[:, :width], 3)
            for term in terms:
                scores = scores + product(term, gather[at : at + width])
        scores = jnp.where(lanes(scores.shape).astype(F32) < info[rows, 0:1], 0.5 * scores, -1e30)
        raised = jnp.exp(scores - jnp.max(scores, axis=1, keepdims=True))
        attn = raised / row_sum(raised)
        return target, query, probe_tiled, attn

    def spread_spots(terms, at, width):
        return sum(contract_cols(term, gather[at : at + width]) for term in terms)

    def fold(pieces):
        wide = sum(pieces[:-1])
        return exact_cols(wide, tile) + exact_cols(pieces[-1], tile[:, :LANES])

    def pool(rows, attn):
        terms = split(attn, 2)
        weights = [spread_spots(terms, at, width) for at, width in PIECES]
        pooled = fold([w * behaviour[rows, at : at + width].astype(F32) for w, (at, width) in zip(weights, PIECES)])
        return weights, pooled

    own_seq.wait()
    _, _, _, attn = attention(own)
    _, pooled = pool(own, attn)
    value = exact(exact(pooled, w_value[...]), lane_match(EMBED, LANES, 0))
    joined[...] = fields[own]
    head = joined[:, :LANES]
    joined[:, :LANES] = jnp.where(lanes(head.shape) < EMBED, value.astype(BF16), head)
    projected = product(joined[...], proj_turned[...]) + packed[0:1]
    act, slope_proj = gelu_both(projected)
    act = act.astype(BF16).astype(F32)
    activation[...] = act
    proj_slope[...] = slope_proj
    centred = act - row_sum(act) * (1.0 / HIDDEN)
    scale = lax.rsqrt(row_sum(centred * centred) * (1.0 / HIDDEN) + EPSILON)
    standard[...] = centred * scale
    normed[...] = (centred * scale * packed[1:2] + packed[2:3]).astype(BF16)
    gates[:, 0:1] = scale

    logits = product(normed[...], gate_weight[...])
    domain = info[own, 1:2]
    in_first = domain == 0.0
    level = sigmoid(logits[:, 6:7])
    shared_a = sigmoid(logits[:, 0:1] - logits[:, 1:2])
    shared_b = sigmoid(logits[:, 1:2] - logits[:, 0:1])
    lead = jnp.where(in_first, logits[:, 2:3] - logits[:, 3:4], logits[:, 4:5] - logits[:, 5:6])
    chosen_a, chosen_b = sigmoid(lead), sigmoid(-lead)
    zero = jnp.zeros_like(level)
    columns = [
        level * shared_a,
        level * shared_b,
        jnp.where(in_first, (1.0 - level) * chosen_a, zero),
        jnp.where(in_first, (1.0 - level) * chosen_b, zero),
        jnp.where(in_first, zero, (1.0 - level) * chosen_a),
        jnp.where(in_first, zero, (1.0 - level) * chosen_b),
    ]
    for e in range(EXPERTS):
        mixing[e] = jnp.broadcast_to(columns[e], (ROWS, LANES))
    for i, column in enumerate((level, shared_a, shared_b, chosen_a, chosen_b)):
        gates[:, i + 1 : i + 2] = column

    d_residual[...] = jnp.zeros_like(d_residual)

    def forward(e, _):
        load_in(e).wait()
        load_out(e).wait()
        pre = product(normed[...], w_in[e]) + b_in[pl.ds(e, 1)]
        out, grade = gelu_both(pre)
        active[e] = out.astype(BF16)
        slope[e] = grade.astype(BF16)
        rows = product(active[e], w_out[e]) + b_out[pl.ds(e, 1)]
        expert[e] = rows
        d_residual[...] += mixing[e][:, 0:1] * rows
        return 0

    lax.fori_loop(0, EXPERTS, forward, 0)
    branch = d_residual[...]
    residual = act + branch
    valid = info[own, 2:3]
    residual_low[...] = residual.astype(BF16)
    tower_act, tower_slope = gelu_both(product(residual_low[...], tower_in[...]) + packed[3:4])
    chosen = jnp.where(in_first, 0, 1) == lanes((ROWS, HIDDEN)) // 256
    ends = packed[5:6]
    end = jnp.where(in_first, ends[:, 0:1], ends[:, 1:2])
    predict = sigmoid(row_sum(jnp.where(chosen, tower_act * packed[4:5], 0.0)) + end)
    d_logit = info[own, 3:4] * valid * predict * (1.0 - predict)
    spread_logit = jnp.where(chosen, d_logit, 0.0)
    d_tower[...] = (spread_logit * packed[4:5] * tower_slope).astype(BF16)
    small[3:4] = column_sum(d_tower[...].astype(F32))
    small[4:5] = column_sum(tower_act * spread_logit)
    spots = lanes((1, HIDDEN))
    parts = (
        column_sum(jnp.where(in_first, d_logit, 0.0)),
        column_sum(jnp.where(in_first, 0.0, d_logit)),
        column_sum(valid * row_sum(residual * residual)),
        column_sum(valid * row_sum(branch * branch)),
        column_sum(valid),
    )
    small[5:6] = sum(jnp.where(spots == i, part, 0.0) for i, part in enumerate(parts))
    pred_all[section] = jnp.transpose(jnp.broadcast_to(predict, (ROWS, LANES)))[:8]
    d_res = contract_cols(d_tower[...], tower_in[...])
    d_residual[...] = d_res
    for e in range(EXPERTS):
        low = (mixing[e][:, 0:1] * d_res).astype(BF16)
        d_expert[e] = low
        small[32 + e : 33 + e] = column_sum(low.astype(F32))
        d_mixing[e] = jnp.broadcast_to(row_sum(expert[e] * d_res), (ROWS, LANES))
    d_normed[...] = jnp.zeros_like(d_normed)

    def backward(e, _):
        grade = contract_cols(d_expert[e], w_out[e]) * slope[e].astype(F32)
        low = grade.astype(BF16)
        slope[e] = low
        sums = column_sum(low.astype(F32))
        small[pl.ds(16 + e, 1)] = sums[:, :512]
        small[pl.ds(24 + e, 1)] = sums[:, 512:]
        d_normed[...] += contract_cols(low, w_in[e])
        return 0

    def finish_backward():
        level, shared_a, shared_b, chosen_a, chosen_b = (gates[:, i : i + 1] for i in range(1, 6))
        in_first = info[own, 1:2] == 0.0
        grads = [d_mixing[e][:, 0:1] for e in range(EXPERTS)]
        grad_a = jnp.where(in_first, grads[2], grads[4])
        grad_b = jnp.where(in_first, grads[3], grads[5])
        d_level = grads[0] * shared_a + grads[1] * shared_b - grad_a * chosen_a - grad_b * chosen_b
        d_shared = level * shared_a * shared_b * (grads[0] - grads[1])
        d_lead = (1.0 - level) * chosen_a * chosen_b * (grad_a - grad_b)
        zero = jnp.zeros_like(d_lead)
        d_first = jnp.where(in_first, d_lead, zero)
        d_second = jnp.where(in_first, zero, d_lead)
        columns = (d_shared, -d_shared, d_first, -d_first, d_second, -d_second, d_level * level * (1.0 - level))
        place = lanes((ROWS, LANES))
        d_logits = sum(jnp.where(place == i, column, 0.0) for i, column in enumerate(columns)).astype(BF16)
        small[8:16] = jnp.transpose(contract_rows(normed[...], d_logits))[:8]
        total = d_normed[...] + contract_cols(d_logits[:, :7], gate_weight[...])
        std = standard[...]
        small[1:2] = column_sum(total * std)
        small[2:3] = column_sum(total)
        scaled = total * packed[1:2]
        inner = scaled - row_sum(scaled) * (1.0 / HIDDEN) - std * (row_sum(scaled * std) * (1.0 / HIDDEN))
        d_act = (inner * gates[:, 0:1] + d_residual[...]).astype(BF16).astype(F32)
        d_projected = (d_act * proj_slope[...]).astype(BF16)
        small[0:1] = column_sum(d_projected.astype(F32))
        d_proj_all[own] = d_projected

    def pair_copy(slot, ref):
        return pltpu.make_async_remote_copy(
            src_ref=ref,
            dst_ref=ref,
            send_sem=pair_send.at[slot],
            recv_sem=pair_recv.at[slot],
            device_id=opposite(),
            device_id_type=MESH,
        )

    gradient_copy = pair_copy(0, d_proj_all.at[pl.ds(ROWS, ROWS)])
    predict_copy = pair_copy(1, pred_all.at[0])

    def store_seq(block):
        rows = pl.ds(block * BLOCK, BLOCK)
        return pltpu.make_async_copy(d_seq, d_seq_hbm.at[rows], seq_sem.at[block])

    def attention_back(block):
        rows = pl.ds(block * BLOCK, BLOCK)
        target, query, probe_tiled, attn = attention(rows)
        weights, pooled = pool(rows, attn)
        d_joined = contract_cols(d_proj_all[rows], proj_turned[...])
        d_value = d_joined[:, :LANES][:, :EMBED]
        value_grad = exact_rows(pooled, d_value)
        d_pooled = exact(exact_cols(d_value, w_value[...]), tile)
        d_attn = 0.0
        for at, width in PIECES:
            for term in split(behaviour[rows, at : at + width].astype(F32) * d_pooled[:, :width], 3):
                d_attn = d_attn + product(term, gather[at : at + width])
        d_scores = attn * (d_attn - row_sum(attn * d_attn))
        terms = split(0.5 * d_scores, 2)
        pieces = []
        if block:
            store_seq(block - 1).wait()
        for (at, width), weight in zip(PIECES, weights):
            grade = spread_spots(terms, at, width)
            pieces.append(grade * behaviour[rows, at : at + width].astype(F32))
            d_seq[:, at : at + width] = (weight * d_pooled[:, :width] + grade * probe_tiled[:, :width]).astype(BF16)
        store_seq(block).start()
        d_probe = fold(pieces)
        key_grad = exact_rows(d_probe, query)
        d_query = exact(d_probe, w_key[...])
        query_grad = exact_rows(target, d_query)
        d_target = exact(exact_cols(d_query, w_query[...]), lane_match(EMBED, LANES, 0))
        d_fields[rows] = d_joined
        d_fields[rows, :LANES] = jnp.where(
            lanes((BLOCK, LANES)) < EMBED, d_target, d_joined[:, :LANES]
        )
        for i, grad in enumerate((query_grad, key_grad, value_grad)):
            small[48:64] += exact(grad, lane_match(EMBED, HIDDEN, 0, EMBED * i))

    def on_first(work):
        pl.when(section == 0)(work)

    def on_second(work):
        pl.when(section == 1)(work)

    def out_half(family, base, half, e, use):
        grad = contract_rows(active[e], d_expert[e, :, pl.ds(pl.multiple_of(half * 256, 256), 256)])
        for j in range(2):
            use(2 * e + j, grad[:, j * LANES : (j + 1) * LANES])

    def in_half(family, base, half, e, use):
        grad = contract_rows(normed[...], slope[e, :, pl.ds(pl.multiple_of(half * 512, 512), 512)])
        for j in range(2):
            pair = [grad[:, (2 * j + i) * LANES : (2 * j + i + 1) * LANES] for i in range(2)]
            use(12 + 2 * e + j, jnp.concatenate(pair, axis=0))

    def big_other(family, base):
        make = out_half if base < 12 else in_half

        def one(i, _):
            def use(unit, rows):
                family.sent[unit] = rows.astype(BF16)
                family.across(unit).start()

            make(family, base, 1 - core, (base % 12) // 2 + i, use)
            return 0

        lax.fori_loop(0, 3, one, 0)

    def big_own(family, base):
        make = out_half if base < 12 else in_half

        def one(i, _):
            def use(unit, rows):
                family.take(unit, unit % 6, rows)

            make(family, base, core, (base % 12) // 2 + i, use)
            return 0

        lax.fori_loop(0, 3, one, 0)

    def mid_half(half):
        pick = pl.ds(pl.multiple_of(half * 256, 256), 256)
        tower = contract_rows(residual_low[...], d_tower[:, pick])
        own_rows = pl.ds(pl.multiple_of(section * ROWS, ROWS), ROWS)
        proj = contract_rows(joined[...], d_proj_all[own_rows, pick])
        for j in range(2):
            at = slice(j * LANES, (j + 1) * LANES)
            yield 3 * j, tower[:384, at]
            yield 3 * j + 1, jnp.concatenate([tower[384:, at], proj[16:272, at]], axis=0)
            yield 3 * j + 2, jnp.concatenate([proj[272:, at], proj[:16, at]], axis=0)

    def mid_other(family, base):
        for unit, rows in mid_half(1 - core):
            family.sent[unit] = rows.astype(BF16)
            family.across(unit).start()

    def mid_own(family, base):
        for unit, rows in mid_half(core):
            family.take(unit, unit, rows)

    def small_half(half):
        columns = [small[:, pl.ds(pl.multiple_of(half * 256 + j * LANES, LANES), LANES)] for j in range(2)]
        return jnp.concatenate(columns, axis=0)

    def small_other(family, base):
        family.sent[0] = small_half(1 - core)
        family.across(0).start()

    def small_own(family, base):
        family.take(0, 0, small_half(core))

    makers = ((big_other, big_own), (mid_other, mid_own), (small_other, small_own))
    families = [
        Family(FAMILIES[i][1], (big_out, mid_out, small_out)[i], family_refs[8 * i : 8 * i + 8], *makers[i])
        for i in range(3)
    ]
    chunks = [(families[0], 6 * n, PARTS) for n in range(4)] + [(families[1], 0, PARTS), (families[2], 0, 1)]
    done = [0] * len(chunks)

    def step(*which):
        for n in which:
            if done[n] < TASKS:
                family, base, count = chunks[n]
                family.run(base, count, done[n])
                done[n] += 1

    pl.semaphore_wait(barrier, 8)
    on_first(predict_copy.start)
    step(0, 1)
    step(0)
    lax.fori_loop(0, 3, backward, 0)
    step(2, 1, 0)
    lax.fori_loop(3, 6, backward, 0)
    step(3, 2, 1, 0)
    finish_backward()
    on_second(gradient_copy.start)
    step(4, 3, 2, 1, 0)
    rest_seq.wait()
    on_first(lambda: attention_back(0))
    step(4, 3, 2, 1, 0)
    on_first(lambda: attention_back(1))
    step(4, 3, 2, 1, 0)
    on_first(gradient_copy.wait_recv)
    on_first(lambda: attention_back(2))
    step(4, 3, 2, 1, 0)
    on_first(lambda: attention_back(3))
    while min(done) < TASKS:
        step(5, 4, 3, 2, 1, 0)
    for family, base, count in chunks:
        family.drain(base, count)
    on_first(predict_copy.wait_send)
    on_second(predict_copy.wait_recv)
    on_second(gradient_copy.wait_send)
    on_first(store_seq(3).wait)


def run(fields, behaviour, packed, w_query, w_key, w_value, w_proj, gate_weight, w_in, b_in, w_out, b_out, tower_in):
    here = pl.BlockSpec(memory_space=pltpu.VMEM)
    far = pl.BlockSpec(memory_space=pl.ANY)

    def keep(*shape, dtype=F32):
        return pltpu.VMEM(shape, dtype)

    scratch = [
        keep(2 * ROWS, SEQ, dtype=BF16),
        keep(EXPERTS, HIDDEN, WIDE, dtype=BF16),
        keep(EXPERTS, WIDE, HIDDEN, dtype=BF16),
        keep(SEQ, SPOTS, dtype=BF16),
        keep(FIELDS, HIDDEN, dtype=BF16),
        keep(2 * ROWS, 8),
        keep(ROWS, FIELDS, dtype=BF16),
        keep(ROWS, HIDDEN),
        keep(ROWS, HIDDEN),
        keep(ROWS, HIDDEN, dtype=BF16),
        keep(ROWS, HIDDEN),
        keep(EXPERTS, ROWS, WIDE, dtype=BF16),
        keep(EXPERTS, ROWS, WIDE, dtype=BF16),
        keep(EXPERTS, ROWS, HIDDEN),
        keep(EXPERTS, ROWS, HIDDEN, dtype=BF16),
        keep(ROWS, HIDDEN),
        keep(ROWS, HIDDEN),
        keep(EXPERTS, ROWS, LANES),
        keep(EXPERTS, ROWS, LANES),
        keep(ROWS, 8),
        keep(ROWS, HIDDEN, dtype=BF16),
        keep(ROWS, HIDDEN, dtype=BF16),
        keep(2 * ROWS, HIDDEN, dtype=BF16),
        keep(64, HIDDEN),
        keep(BLOCK, SEQ, dtype=BF16),
        pltpu.SemaphoreType.DMA((14,)),
        pltpu.SemaphoreType.DMA((4,)),
        pltpu.SemaphoreType.DMA((2,)),
        pltpu.SemaphoreType.DMA((2,)),
    ]
    for family in FAMILIES:
        scratch += family_scratch(*family)
    outs = [jax.ShapeDtypeStruct((units, 2, rows, LANES), dtype) for units, rows, dtype in FAMILIES]
    outs += [
        jax.ShapeDtypeStruct((2, 8, LANES), F32),
        jax.ShapeDtypeStruct((2 * ROWS, FIELDS), F32),
        jax.ShapeDtypeStruct((2 * ROWS, SEQ), BF16),
    ]
    return pl.pallas_call(
        kernel,
        out_shape=outs,
        in_specs=[here] * 10 + [far] * 3,
        out_specs=[far] * 3 + [here] * 2 + [far],
        scratch_shapes=scratch,
        compiler_params=pltpu.CompilerParams(
            collective_id=0, has_side_effects=True, vmem_limit_bytes=64 << 20
        ),
        name="rank_and_sum",
    )(
        fields, packed, w_query, w_key, w_value, w_proj, gate_weight, b_in, b_out, tower_in, behaviour, w_in, w_out
    )


def place_kernel(
    out_units,
    in_units,
    mid,
    small,
    pred_all,
    field_rows,
    seq_rows,
    out_grad,
    in_grad,
    predictions,
    field_grad,
    seq_grad,
    proj,
    tower,
    b_proj,
    gain,
    shift,
    tower_b,
    tower_o,
    tower_e,
    roots,
    gate,
    in_b,
    out_b,
    query,
    key,
    value,
):
    step = pl.program_id(0)
    section = lax.axis_index("section")
    second = (section == 1).astype(F32)
    first = 1.0 - second
    for core in range(2):
        for j in range(2):
            column = 2 * core + j
            out_grad[0, 0, :, column * LANES : (column + 1) * LANES] = out_units[j, core].astype(F32) * second
            for i in range(2):
                column = 4 * core + 2 * j + i
                block = in_units[j, core, i * 512 : (i + 1) * 512].astype(F32)
                in_grad[0, 0, :, column * LANES : (column + 1) * LANES] = block * second

    @pl.when(step < 4)
    def _():
        field_grad[0] = jnp.where(section == 0, field_rows[...], 0.0)
        seq_grad[0] = jnp.where(section == 0, seq_rows[...].astype(F32), 0.0)

    @pl.when(step == 0)
    def _():
        predictions[:, :LANES] = pred_all[0, 0:1] * second
        predictions[:, LANES:] = jnp.where(section == 1, pred_all[1, 0:1], 0.0)
        for core in range(2):
            for i in range(PARTS):
                column = core * 2 + i // 3
                at = slice(column * LANES, (column + 1) * LANES)
                block = mid[i, core].astype(F32)
                if i % 3 == 0:
                    tower[0, :384, at] = block * second
                elif i % 3 == 1:
                    tower[0, 384:, at] = block[:128] * second
                    proj[0, :256, at] = block[128:] * first
                else:
                    proj[0, 256:, at] = block * first

        def rows(start, count):
            return jnp.concatenate(
                [small[core, j * 64 + start : j * 64 + start + count] for core in range(2) for j in range(2)],
                axis=1,
            )

        head = rows(0, 8)
        b_proj[...] = head[0:1] * first
        gain[...] = head[1:2] * second
        shift[...] = head[2:3] * second
        tower_b[...] = head[3:4] * second
        tower_o[...] = head[4:5] * second
        tower_e[...] = head[5:6, 0:2] * second
        count = head[5:6, 4:5]
        squares = head[5:6, 2:4] / (float(HIDDEN) * jnp.maximum(count, 1.0)) + EPSILON
        roots[...] = jnp.where(count > 0.0, jnp.sqrt(squares), 0.0) * second
        gate[0] = jnp.transpose(rows(8, 8))[:, :7] * second
        in_b[0, :, :512] = rows(16, 6) * second
        in_b[0, :, 512:] = rows(24, 6) * second
        out_b[0] = rows(32, 6) * second
        three = rows(48, 16)
        query[0] = three[:, 0:16] * first
        key[0] = three[:, 16:32] * first
        value[0] = three[:, 32:48] * first


def place(big, mid, small, pred_all, field_rows, seq_rows):
    def whole(*shape):
        return jax.ShapeDtypeStruct(shape, F32), pl.BlockSpec(shape, lambda i: (0,) * len(shape))

    def strip(width):
        return (
            jax.ShapeDtypeStruct((1, 2 * ROWS, width), F32),
            pl.BlockSpec((1, BLOCK, width), lambda i: (0, jnp.minimum(i, 3), 0)),
        )

    shapes, specs = zip(
        (jax.ShapeDtypeStruct((1, 6, 1024, 512), F32), pl.BlockSpec((1, 1, 1024, 512), lambda i: (0, i, 0, 0))),
        (jax.ShapeDtypeStruct((1, 6, 512, 1024), F32), pl.BlockSpec((1, 1, 512, 1024), lambda i: (0, i, 0, 0))),
        whole(1, 2 * ROWS),
        strip(FIELDS),
        strip(SEQ),
        whole(1, 640, 512),
        whole(1, 512, 512),
        whole(1, 512),
        whole(1, 512),
        whole(1, 512),
        whole(1, 512),
        whole(1, 512),
        whole(1, 2),
        whole(1, 2),
        whole(1, 512, 7),
        whole(1, 6, 1024),
        whole(1, 6, 512),
        whole(1, 16, 16),
        whole(1, 16, 16),
        whole(1, 16, 16),
    )
    return pl.pallas_call(
        place_kernel,
        grid=(6,),
        out_shape=shapes,
        in_specs=[
            pl.BlockSpec((2, 2, 1024, LANES), lambda i: (i, 0, 0, 0)),
            pl.BlockSpec((2, 2, 1024, LANES), lambda i: (i + 6, 0, 0, 0)),
            pl.BlockSpec((PARTS, 2, MID_ROWS, LANES), lambda i: (0, 0, 0, 0)),
            pl.BlockSpec((2, SMALL_ROWS, LANES), lambda i: (0, 0, 0)),
            pl.BlockSpec((2, 8, LANES), lambda i: (0, 0, 0)),
            pl.BlockSpec((BLOCK, FIELDS), lambda i: (jnp.minimum(i, 3), 0)),
            pl.BlockSpec((BLOCK, SEQ), lambda i: (jnp.minimum(i, 3), 0)),
        ],
        out_specs=specs,
        compiler_params=pltpu.CompilerParams(vmem_limit_bytes=56 << 20),
        name="place",
    )(big, big, mid, small, pred_all, field_rows, seq_rows)


def body(
    fields,
    behaviour,
    lengths,
    domains,
    validity,
    cotangent,
    w_query,
    w_key,
    w_value,
    w_proj,
    b_proj,
    norm_gain,
    norm_shift,
    gate_weight,
    w_in,
    b_in,
    w_out,
    b_out,
    tower_in,
    tower_bias,
    tower_out,
    tower_end,
):
    def line(array):
        return jnp.pad(array.astype(F32), (0, HIDDEN - array.shape[0]))[None]

    blank = jnp.zeros((1, HIDDEN), F32)
    packed = jnp.concatenate(
        [line(a) for a in (b_proj, norm_gain, norm_shift, tower_bias, tower_out, tower_end)]
        + [blank] * 2
        + [line(a) for a in (lengths, domains, validity, cotangent)]
        + [blank] * 4,
        axis=0,
    )
    big, mid, small, pred_all, field_rows, seq_rows = run(
        fields, behaviour, packed, w_query, w_key, w_value, w_proj, gate_weight, w_in, b_in, w_out, b_out, tower_in
    )
    (
        out_grad,
        in_grad,
        predictions,
        field_grad,
        seq_grad,
        proj,
        tower,
        b_proj_grad,
        gain,
        shift,
        tower_b,
        tower_o,
        tower_e,
        roots,
        gate,
        in_b,
        out_b,
        query,
        key,
        value,
    ) = place(big, mid, small.reshape(2, SMALL_ROWS, LANES), pred_all, field_rows, seq_rows)
    return (
        predictions,
        field_grad,
        seq_grad,
        query,
        key,
        value,
        proj,
        b_proj_grad,
        gain,
        shift,
        gate,
        in_grad,
        in_b,
        out_grad,
        out_b,
        tower,
        tower_b,
        tower_o,
        tower_e,
        roots,
    )


def solution(mesh):
    each = (P("dp", None), P("dp", None), P("dp"), P("dp"), P("dp"), P("dp"))
    ranks = (2, 3, 3, 3, 3, 3, 3, 2, 2, 2, 3, 4, 3, 4, 3, 3, 2, 2, 2, 2)
    outs = tuple(
        P("section", "dp", *(None,) * (rank - 2)) if i < 3 else P("section", *(None,) * (rank - 1))
        for i, rank in enumerate(ranks)
    )
    return jax.shard_map(
        body, mesh=mesh, in_specs=each + (P(),) * 16, out_specs=outs, check_vma=False
    )
```

```python
import jax
import jax.numpy as jnp
from jax import lax
from jax.experimental import pallas as pl
from jax.experimental.pallas import tpu as pltpu
from jax.sharding import PartitionSpec as P

EPSILON = 1e-05
MESH = pl.DeviceIdType.MESH
F32 = jnp.float32
BF16 = jnp.bfloat16

LANES = 128
DIMS = 5
HALVINGS = 3
SLOTS = 7 + HALVINGS
ROWS = 256
EXPERTS = 6
HIDDEN = 512
WIDE = 1024
FIELDS = 640
EMBED = 16
SEQ = 3200
SPAN = 256
PIECES = tuple((at, SPAN) for at in range(0, 3072, SPAN)) + ((3072, LANES),)
PROJ_ROWS = 256
SMALL_ROWS = 128
BLOCK = 64


def coords():
    section, place = lax.axis_index("section"), lax.axis_index("dp")
    return 2 * section + place // 32, (place // 8) % 4, (place // 2) % 4, place % 2


def device_at(z, x, y, core):
    return {"section": z // 2, "dp": (((z % 2) * 4 + x) * 4 + y) * 2 + core}


def hop(r, kind):
    near, far = 1 - 2 * (r % 2), 3 - 2 * r
    return near + kind * (far - near)


def side(r, kind):
    near = (r + r // 2) % 2
    return near + kind * (r // 2 - near)


def picks(dim):
    a = dim % 3
    return (1 - a) * (2 - a) // 2, a * (2 - a), a * (a - 1) // 2, dim // 3


def neighbour(dim):
    z, x, y, core = coords()
    ex, ey, ez, kind = picks(dim)
    return device_at(z + ez * hop(z, kind), x + ex * hop(x, kind), y + ey * hop(y, kind), core)


def which_half(dim):
    z, x, y, core = coords()
    ex, ey, ez, kind = picks(dim)
    return ex * side(x, kind) + ey * side(y, kind) + ez * side(z, kind)


def sibling():
    z, x, y, core = coords()
    return device_at(z, x, y, 1 - core)


def cross():
    z, x, y, core = coords()
    return device_at(3 - z, x, y, core)


class Family:
    def __init__(self, rows, out, refs, first, to_other=False):
        self.rows = rows
        self.share = rows >> HALVINGS
        self.out = out
        self.first = first
        self.to_other = to_other
        (
            self.sent,
            self.kept,
            self.arrived,
            self.doubled,
            self.pair_send,
            self.pair_recv,
            self.send_sem,
            self.recv_sem,
            self.out_sem,
        ) = refs
        self.total = self.sent

    def remote(self, unit, slot, src, dst, to):
        return pltpu.make_async_remote_copy(
            src_ref=src,
            dst_ref=dst,
            send_sem=self.send_sem.at[slot],
            recv_sem=self.recv_sem.at[unit // DIMS, slot],
            device_id=to,
            device_id_type=MESH,
        )

    def start_of(self, part, step):
        start = 0
        for k in range(step):
            start = start + which_half((part + k) % DIMS) * (self.rows >> (k + 1))
        return start

    def span(self, start, size):
        return pl.ds(pl.multiple_of(start, size), size)

    def own_share(self, unit):
        return self.span(self.start_of(unit % DIMS, HALVINGS), self.share)

    def across(self, group, unit, count):
        return pltpu.make_async_remote_copy(
            src_ref=self.sent.at[pl.ds(unit, count)],
            dst_ref=self.kept.at[pl.ds(unit - self.first, count)],
            send_sem=self.pair_send.at[group],
            recv_sem=self.pair_recv.at[group],
            device_id=sibling(),
            device_id_type=MESH,
        )

    def halve(self, unit, k):
        size = self.rows >> (k + 1)
        dim = (unit + k) % DIMS
        start = self.start_of(unit % DIMS, k) + (1 - which_half(dim)) * size
        local = unit - self.first
        return self.remote(
            unit,
            k,
            self.kept.at[local, self.span(start, size)],
            self.arrived.at[local, pl.ds(self.rows - 2 * size, size)],
            neighbour(dim),
        )

    def double(self, unit, j):
        local = unit - self.first
        src = self.kept.at[local, self.own_share(unit)] if j == 0 else self.doubled.at[local, j - 1]
        return self.remote(
            unit,
            HALVINGS + j,
            src,
            self.arrived.at[local, pl.ds(self.rows - self.share + j * self.share, self.share)],
            neighbour((unit + HALVINGS + j) % DIMS),
        )

    def over(self, unit):
        region = self.total.at[unit, self.own_share(unit)]
        return self.remote(unit, DIMS, region, region, cross())

    def spread(self, unit, k):
        size = self.rows >> (k + 1)
        region = self.total.at[unit, self.span(self.start_of(unit % DIMS, k + 1), size)]
        return self.remote(unit, DIMS + 1 + k, region, region, neighbour((unit + k) % DIMS))

    def back(self, unit):
        region = self.total.at[unit]
        return self.remote(unit, DIMS + 1 + HALVINGS, region, self.out.at[unit, coords()[3]], sibling())

    def keep(self, unit):
        return pltpu.make_async_copy(self.total.at[unit], self.out.at[unit, coords()[3]], self.out_sem.at[0])

    def send(self, group, unit, halves):
        for i, rows in enumerate(halves):
            self.sent[unit + i] = rows.astype(self.sent.dtype)
        self.across(group, unit, len(halves)).start()

    def take(self, group, unit, halves):
        pair = self.across(group, unit, len(halves))
        pair.wait_send()
        pair.wait_recv()
        for i, rows in enumerate(halves):
            local = unit + i - self.first
            self.kept[local] = (rows + self.kept[local].astype(F32)).astype(self.kept.dtype)
            self.halve(unit + i, 0).start()

    def await_chunk(self, slot, base, ref):
        pltpu.make_async_copy(ref, ref, self.recv_sem.at[base // DIMS, slot]).wait()

    def each(self, base, count, work):
        def one(i, _):
            work(base + i)
            return 0

        lax.fori_loop(0, count, one, 0)

    def reduce(self, base, count, step):
        dtype = self.kept.dtype
        local = pl.ds(base - self.first, count)
        if step < HALVINGS:
            size = self.rows >> (step + 1)
            arrivals = pl.ds(self.rows - 2 * size, size)
        else:
            size = self.share
            arrivals = pl.ds(self.rows - size + (step - HALVINGS) * size, size)
        self.await_chunk(step, base, self.arrived.at[local, arrivals])

        def one(unit):
            here = unit - self.first
            came = self.arrived[here, arrivals].astype(F32)
            if step < HALVINGS:
                region = self.span(self.start_of(unit % DIMS, step + 1), size)
                self.kept[here, region] = (self.kept[here, region].astype(F32) + came).astype(dtype)
                if step + 1 < HALVINGS:
                    self.halve(unit, step + 1).start()
                else:
                    self.double(unit, 0).start()
                return
            j = step - HALVINGS
            region = self.own_share(unit)
            old = self.kept[here, region] if j == 0 else self.doubled[here, j - 1]
            new = (old.astype(F32) + came).astype(dtype)
            if step + 1 < DIMS:
                self.doubled[here, j] = new
                self.double(unit, j + 1).start()
            else:
                self.total[unit, region] = new
                if self.to_other:
                    self.over(unit).start()
                else:
                    self.spread(unit, HALVINGS - 1).start()

        self.each(base, count, one)

    def gather(self, base, count, step):
        units = pl.ds(base, count)
        if step == 0:
            self.await_chunk(DIMS, base, self.total.at[units, pl.ds(0, self.share)])
            self.each(base, count, lambda unit: self.spread(unit, HALVINGS - 1).start())
        elif step <= HALVINGS:
            k = HALVINGS - step
            self.await_chunk(DIMS + 1 + k, base, self.total.at[units, pl.ds(0, self.rows >> (k + 1))])

            def one(unit):
                if k > 0:
                    self.spread(unit, k - 1).start()
                else:
                    self.back(unit).start()
                    self.keep(unit).start()

            self.each(base, count, one)
        else:
            self.await_chunk(DIMS + 1 + HALVINGS, base, self.out.at[units, 1 - coords()[3]])

    def drain(self, reduced, gathered):
        def sent(slot, ref):
            pltpu.make_async_copy(ref, ref, self.send_sem.at[slot]).wait()

        for step in range(DIMS):
            size = self.rows >> (step + 1) if step < HALVINGS else self.share
            sent(step, self.kept.at[pl.ds(0, reduced), pl.ds(0, size)])
        if self.to_other:
            sent(DIMS, self.kept.at[pl.ds(0, reduced), pl.ds(0, self.share)])
        if gathered:
            for k in range(HALVINGS):
                sent(DIMS + 1 + k, self.total.at[pl.ds(0, gathered), pl.ds(0, self.rows >> (k + 1))])
            sent(DIMS + 1 + HALVINGS, self.total.at[pl.ds(0, gathered)])
            whole = self.total.at[pl.ds(0, gathered)]
            pltpu.make_async_copy(whole, whole, self.out_sem.at[0]).wait()


def family_scratch(units, reduced, groups, rows, dtype):
    share = rows >> HALVINGS
    chunks = pl.cdiv(units, DIMS)
    return [
        pltpu.VMEM((units, rows, LANES), dtype),
        pltpu.VMEM((reduced, rows, LANES), dtype),
        pltpu.VMEM((reduced, rows - share + (DIMS - HALVINGS) * share, LANES), dtype),
        pltpu.VMEM((reduced, max(1, DIMS - HALVINGS - 1), share, LANES), dtype),
        pltpu.SemaphoreType.DMA((groups,)),
        pltpu.SemaphoreType.DMA((groups,)),
        pltpu.SemaphoreType.DMA((SLOTS,)),
        pltpu.SemaphoreType.DMA((chunks, SLOTS)),
        pltpu.SemaphoreType.DMA((1,)),
    ]


FAMILIES = ((25, 15, 13, 1024, BF16), (DIMS, DIMS, 1, PROJ_ROWS, BF16), (1, 1, 1, SMALL_ROWS, F32))
SPLIT = 5
TINY_ROWS = 24


PLAN_FIRST = (
    ("send", 5), ("send", 12), ("back", 0), ("take", 5), ("take", 12), ("send", 6), ("back", 1), ("take", 6), ("send", 7),
    ("back", 2), ("take", 7), ("send", 8), ("back", 3), ("take", 8), ("send", 9), ("sum", 2, 0), ("back", 4), ("take", 9),
    ("send", 10), ("sum", 2, 1), ("back", 5), ("send", 11), ("take", 10), ("sum", 3, 0), ("sum", 2, 2), ("take", 11),
    ("sum", 3, 1), ("sum", 2, 3), ("front",), ("sum", 2, 4), ("sum", 3, 2), ("sum", 4, 0), ("send_p",), ("sum", 3, 3),
    ("sum", 4, 1), ("take_p",), ("sum", 3, 4), ("sum", 4, 2), ("seq", 0), ("sum", 4, 3), ("sum_p", 0), ("seq", 1),
    ("sum", 4, 4), ("sum_p", 1), ("seq", 2), ("sum_p", 2), ("seq", 3), ("sum_p", 3), ("weights",), ("tiny", 0),
    ("sum_p", 4), ("tiny", 1), ("all_p", 1), ("tiny", 2), ("all_p", 2), ("tiny", 3), ("all_p", 3), ("tiny", 4),
    ("all_p", 4), ("tiny", 5), ("tiny", 6),
)
PLAN_SECOND = (
    ("send", 0), ("send", 1), ("send", 2), ("take", 0), ("take", 1), ("send", 3), ("take", 2), ("send", 4), ("take", 3),
    ("take", 4), ("back", 0), ("back", 1), ("back", 2), ("sum", 0, 0), ("back", 3), ("back", 4), ("sum", 1, 0),
    ("sum", 0, 1), ("back", 5), ("front",), ("sum", 0, 2), ("sum", 1, 1), ("send_v",), ("take_v",), ("sum", 0, 3),
    ("sum", 1, 2), ("sum_v", 0), ("sum", 0, 4), ("sum", 1, 3), ("sum_v", 1), ("all", 0, 1), ("sum", 1, 4), ("sum_v", 2),
    ("all", 0, 2), ("all", 1, 1), ("sum_v", 3), ("all", 2, 0), ("all", 0, 3), ("all", 1, 2), ("sum_v", 4), ("all", 3, 0),
    ("all", 2, 1), ("all", 1, 3), ("all_v", 1), ("all", 4, 0), ("all", 3, 1), ("all", 2, 2), ("all_v", 2), ("all", 0, 4),
    ("all", 4, 1), ("all", 3, 2), ("all", 2, 3), ("all_v", 3), ("all", 1, 4), ("all", 4, 2), ("all", 3, 3), ("all_v", 4),
    ("all", 2, 4), ("all", 4, 3), ("all", 3, 4), ("all", 4, 4),
)


def exact(left, right):
    return jnp.dot(left, right, precision=lax.Precision.HIGHEST, preferred_element_type=F32)


def exact_cols(left, right):
    return lax.dot_general(
        left, right, (((1,), (1,)), ((), ())), precision=lax.Precision.HIGHEST, preferred_element_type=F32
    )


def exact_rows(left, right):
    return lax.dot_general(
        left, right, (((0,), (0,)), ((), ())), precision=lax.Precision.HIGHEST, preferred_element_type=F32
    )


def product(left, right):
    return jnp.dot(left, right, preferred_element_type=F32)


def contract_rows(left, right):
    return lax.dot_general(left, right, (((0,), (0,)), ((), ())), preferred_element_type=F32)


def contract_cols(left, right):
    return lax.dot_general(left, right, (((1,), (1,)), ((), ())), preferred_element_type=F32)


def split(value, terms):
    out = []
    for _ in range(terms):
        out.append(value.astype(BF16))
        value = value - out[-1].astype(F32)
    return out


def sigmoid(v):
    return 1.0 / (1.0 + jnp.exp(-v))


ROOT = 0.7978845608028654
CUBE = 0.044715


def gelu_both(v):
    square = v * v
    bent = jnp.tanh(v * (ROOT + ROOT * CUBE * square))
    half = 0.5 + 0.5 * bent
    slope = half + 0.5 * v * (1.0 - bent * bent) * (ROOT + 3.0 * ROOT * CUBE * square)
    return v * half, slope


def column_sum(array):
    return jnp.sum(array, axis=0, keepdims=True)


def row_sum(array):
    return jnp.sum(array, axis=1, keepdims=True)


def lanes(shape):
    return lax.broadcasted_iota(jnp.int32, shape, 1)


def lane_match(rows, columns, period, shift=0):
    place = lax.broadcasted_iota(jnp.int32, (rows, columns), 1) - shift
    if period:
        place = place % period
    return (place == lax.broadcasted_iota(jnp.int32, (rows, columns), 0)).astype(F32)


def kernel(
    fields,
    lengths,
    domains,
    validity,
    cotangent,
    w_query,
    w_key,
    w_value,
    w_proj,
    b_proj,
    norm_gain,
    norm_shift,
    gate_turned,
    b_in,
    b_out,
    tower_in,
    tower_bias,
    tower_out,
    tower_end,
    behaviour_hbm,
    w_in_hbm,
    w_out_hbm,
    big_out,
    proj_out,
    small_out,
    tiny_out,
    pred_all,
    d_fields,
    d_seq_hbm,
    behaviour,
    w_in,
    w_out,
    groups,
    probe_w,
    value_w,
    pooled_w,
    back_w,
    target_w,
    proj_turned,
    gate_rows,
    info,
    joined,
    activation,
    proj_slope,
    normed,
    standard,
    active,
    slope,
    expert,
    d_expert,
    d_normed,
    d_residual,
    mixing,
    d_mixing,
    gates,
    residual_low,
    d_tower,
    d_proj_low,
    pooled_rows,
    d_value_rows,
    d_probe_rows,
    small,
    tiny,
    tiny_arrived,
    d_seq,
    load_sem,
    seq_sem,
    tiny_send,
    tiny_recv,
    *family_refs,
):
    section = lax.axis_index("section")
    core = coords()[3]

    barrier = pltpu.get_barrier_semaphore()
    for dim in range(DIMS):
        pl.semaphore_signal(barrier, inc=1, device_id=neighbour(dim), device_id_type=MESH)
    for other in (sibling(), cross()):
        pl.semaphore_signal(barrier, inc=1, device_id=other, device_id_type=MESH)

    seq_copy = pltpu.make_async_copy(behaviour_hbm, behaviour, load_sem.at[12])

    def load_in(e):
        return pltpu.make_async_copy(w_in_hbm.at[e], w_in.at[e], load_sem.at[e])

    def load_out(e):
        return pltpu.make_async_copy(w_out_hbm.at[e], w_out.at[e], load_sem.at[6 + e])

    tile = lane_match(EMBED, SPAN, EMBED)

    def prepare():
        seq_copy.start()
        for e in range(EXPERTS):
            load_in(e).start()
            load_out(e).start()
        group = lax.broadcasted_iota(jnp.int32, (SPAN, SPAN), 0) // EMBED
        groups[...] = (group == lanes((SPAN, SPAN)) // EMBED).astype(F32).astype(BF16)
        eye = lane_match(EMBED, LANES, 0)
        probe_w[...] = exact(w_query[...], exact_rows(w_key[...], tile))
        value_w[...] = exact_rows(tile, exact(w_value[...], eye))
        pooled_w[...] = exact_rows(tile, eye)
        back_w[...] = exact_rows(w_value[...], tile)
        target_w[...] = exact_rows(tile, exact(exact_cols(w_key[...], w_query[...]), eye))
        proj_turned[:EMBED] = w_proj[FIELDS - EMBED :]
        proj_turned[EMBED:] = w_proj[: FIELDS - EMBED]
        rows = [lengths[...].astype(F32), domains[...].astype(F32), validity[...].astype(F32), cotangent[...]]
        info[...] = jnp.transpose(jnp.concatenate(rows + [jnp.zeros((4, ROWS), F32)], axis=0))
        gate_rows[...] = jnp.zeros_like(gate_rows)
        gate_rows[:7] = gate_turned[...]
        small[...] = jnp.zeros_like(small)
        tiny[0] = jnp.zeros((TINY_ROWS, LANES), F32)
        seq_copy.wait()

    def group_sum(value, terms):
        count, width = value.shape
        stacked = jnp.concatenate(split(value, terms), axis=0)
        sums = product(stacked, groups[:width, :width])
        return sum(sums[i * count : (i + 1) * count] for i in range(terms))

    def narrow_sum(pieces):
        wide = sum(pieces[:-1])
        return jnp.concatenate([wide[:, :LANES] + pieces[-1], wide[:, LANES:]], axis=1)

    def stretch(rows, at, width):
        return behaviour[rows, at : at + width].astype(F32)

    def attention(rows):
        target = fields[rows, 0:LANES].astype(F32)[:, :EMBED]
        probe = exact(target, probe_w[...])
        length = info[rows, 0:1]
        scores = []
        for at, width in PIECES:
            sums = group_sum(stretch(rows, at, width) * probe[:, :width], 3)
            place = ((lanes((1, width)) + at) // EMBED).astype(F32)
            scores.append(jnp.where(place < length, 0.5 * sums, -1e30))
        peak = scores[0]
        for piece in scores[1:-1]:
            peak = jnp.maximum(peak, piece)
        peak = jnp.maximum(jnp.max(peak, axis=1, keepdims=True), jnp.max(scores[-1], axis=1, keepdims=True))
        raised = [jnp.exp(piece - peak) for piece in scores]
        scale = float(EMBED) / row_sum(narrow_sum(raised))
        return probe, [piece * scale for piece in raised]

    def pool(rows, attn):
        return narrow_sum([w * stretch(rows, at, width) for w, (at, width) in zip(attn, PIECES)])

    def attention_forward(block, _):
        rows = pl.ds(pl.multiple_of(block * BLOCK, BLOCK), BLOCK)
        _, attn = attention(rows)
        value = exact(pool(rows, attn), value_w[...])
        joined[rows, LANES:] = fields[rows, LANES:]
        head = fields[rows, :LANES]
        joined[rows, :LANES] = jnp.where(lanes(head.shape) < EMBED, value.astype(BF16), head)
        return 0

    def gate_columns():
        return [gates[:, i : i + 1] for i in range(6)]

    def front_forward():
        projected = product(joined[...], proj_turned[...]) + b_proj[...]
        act, slope_proj = gelu_both(projected)
        act = act.astype(BF16).astype(F32)
        activation[...] = act
        proj_slope[...] = slope_proj
        centred = act - row_sum(act) * (1.0 / HIDDEN)
        scale = lax.rsqrt(row_sum(centred * centred) * (1.0 / HIDDEN) + EPSILON)
        standard[...] = centred * scale
        normed[...] = (centred * scale * norm_gain[...] + norm_shift[...]).astype(BF16)

        logits = contract_cols(normed[...], gate_rows[...])
        in_first = info[:, 1:2] == 0.0
        level = sigmoid(logits[:, 6:7])
        shared_a = sigmoid(logits[:, 0:1] - logits[:, 1:2])
        shared_b = sigmoid(logits[:, 1:2] - logits[:, 0:1])
        lead = jnp.where(in_first, logits[:, 2:3] - logits[:, 3:4], logits[:, 4:5] - logits[:, 5:6])
        chosen_a, chosen_b = sigmoid(lead), sigmoid(-lead)
        zero = jnp.zeros_like(level)
        columns = [
            level * shared_a,
            level * shared_b,
            jnp.where(in_first, (1.0 - level) * chosen_a, zero),
            jnp.where(in_first, (1.0 - level) * chosen_b, zero),
            jnp.where(in_first, zero, (1.0 - level) * chosen_a),
            jnp.where(in_first, zero, (1.0 - level) * chosen_b),
        ]
        place = lanes((ROWS, 8))
        mixing[...] = sum(jnp.where(place == i, column, 0.0) for i, column in enumerate(columns))
        held = (scale, level, shared_a, shared_b, chosen_a, chosen_b)
        gates[...] = sum(jnp.where(place == i, column, 0.0) for i, column in enumerate(held))
        d_residual[...] = jnp.zeros_like(d_residual)

    def expert_forward(e, _):
        load_in(e).wait()
        load_out(e).wait()
        pre = product(normed[...], w_in[e]) + b_in[pl.ds(e, 1)]
        out, grade = gelu_both(pre)
        active[e] = out.astype(BF16)
        slope[e] = grade.astype(BF16)
        rows = product(active[e], w_out[e]) + b_out[pl.ds(e, 1)]
        expert[e] = rows.astype(BF16)
        weight = row_sum(jnp.where(lanes((ROWS, 8)) == e, mixing[...], 0.0))
        d_residual[...] += weight * rows
        return 0

    def tower_both():
        branch = d_residual[...]
        residual = activation[...] + branch
        in_first = info[:, 1:2] == 0.0
        valid = info[:, 2:3]
        residual_low[...] = residual.astype(BF16)
        tower_act, tower_slope = gelu_both(product(residual_low[...], tower_in[...]) + tower_bias[...])
        chosen = jnp.where(in_first, 0, 1) == lanes((ROWS, HIDDEN)) // 256
        ends = tower_end[...]
        end = jnp.where(in_first, ends[:, 0:1], ends[:, 1:2])
        predict = sigmoid(row_sum(jnp.where(chosen, tower_act * tower_out[...], 0.0)) + end)
        d_logit = info[:, 3:4] * valid * predict * (1.0 - predict)
        spread_logit = jnp.where(chosen, d_logit, 0.0)
        d_tower[...] = (spread_logit * tower_out[...] * tower_slope).astype(BF16)
        small[3:4] = column_sum(d_tower[...].astype(F32))
        small[4:5] = column_sum(tower_act * spread_logit)
        spots = lanes((1, HIDDEN))
        parts = (
            column_sum(jnp.where(in_first, d_logit, 0.0)),
            column_sum(jnp.where(in_first, 0.0, d_logit)),
            column_sum(valid * row_sum(residual * residual)),
            column_sum(valid * row_sum(branch * branch)),
            column_sum(valid),
        )
        small[5:6] = sum(jnp.where(spots == i, part, 0.0) for i, part in enumerate(parts))
        wide = jnp.transpose(jnp.broadcast_to(predict, (ROWS, LANES)))
        pred_all[0] = wide[:8, :LANES]
        pred_all[1] = wide[:8, LANES:]
        d_residual[...] = contract_cols(d_tower[...], tower_in[...])

    def spread_residual(e, _):
        weight = row_sum(jnp.where(lanes((ROWS, 8)) == e, mixing[...], 0.0))
        low = (weight * d_residual[...]).astype(BF16)
        d_expert[e] = low
        small[pl.ds(32 + e, 1)] = column_sum(low.astype(F32))
        inner = row_sum(expert[e].astype(F32) * d_residual[...])
        d_mixing[...] = jnp.where(lanes((ROWS, 8)) == e, inner, d_mixing[...])
        return 0

    def expert_backward(e, _):
        grade = contract_cols(d_expert[e], w_out[e]) * slope[e].astype(F32)
        low = grade.astype(BF16)
        slope[e] = low
        sums = column_sum(low.astype(F32))
        small[pl.ds(16 + e, 1)] = sums[:, :512]
        small[pl.ds(24 + e, 1)] = sums[:, 512:]
        d_normed[...] += contract_cols(low, w_in[e])
        return 0

    def front_backward():
        scale, level, shared_a, shared_b, chosen_a, chosen_b = gate_columns()
        in_first = info[:, 1:2] == 0.0
        grads = [d_mixing[:, e : e + 1] for e in range(EXPERTS)]
        grad_a = jnp.where(in_first, grads[2], grads[4])
        grad_b = jnp.where(in_first, grads[3], grads[5])
        d_level = grads[0] * shared_a + grads[1] * shared_b - grad_a * chosen_a - grad_b * chosen_b
        d_shared = level * shared_a * shared_b * (grads[0] - grads[1])
        d_lead = (1.0 - level) * chosen_a * chosen_b * (grad_a - grad_b)
        zero = jnp.zeros_like(d_lead)
        d_first = jnp.where(in_first, d_lead, zero)
        d_second = jnp.where(in_first, zero, d_lead)
        columns = (d_shared, -d_shared, d_first, -d_first, d_second, -d_second, d_level * level * (1.0 - level))
        place = lanes((ROWS, LANES))
        d_logits = sum(jnp.where(place == i, column, 0.0) for i, column in enumerate(columns)).astype(BF16)
        small[8:16] = jnp.transpose(contract_rows(normed[...], d_logits))[:8]
        total = d_normed[...] + product(d_logits[:, :16], gate_rows[...])
        std = standard[...]
        small[1:2] = column_sum(total * std)
        small[2:3] = column_sum(total)
        scaled = total * norm_gain[...]
        inner = scaled - row_sum(scaled) * (1.0 / HIDDEN) - std * (row_sum(scaled * std) * (1.0 / HIDDEN))
        d_act = (inner * scale + d_residual[...]).astype(BF16).astype(F32)
        low = (d_act * proj_slope[...]).astype(BF16)
        sums = column_sum(low.astype(F32))
        for i in range(HIDDEN // LANES):
            tiny[0, 16 + i : 17 + i] = sums[:, i * LANES : (i + 1) * LANES]
        d_proj_low[...] = low

    def store_seq(block):
        rows = pl.ds(block * BLOCK, BLOCK)
        return pltpu.make_async_copy(d_seq, d_seq_hbm.at[rows], seq_sem.at[block])

    def attention_back(block):
        rows = pl.ds(block * BLOCK, BLOCK)
        probe, attn = attention(rows)
        pooled_rows[rows] = exact(pool(rows, attn), pooled_w[...])
        d_joined = contract_cols(d_proj_low[rows], proj_turned[...])
        head = d_joined[:, :LANES]
        d_value_rows[rows] = head
        d_pooled = exact(head[:, :EMBED], back_w[...])
        d_attn = [group_sum(stretch(rows, at, width) * d_pooled[:, :width], 2) for at, width in PIECES]
        inner = row_sum(narrow_sum([a * d for a, d in zip(attn, d_attn)])) * (1.0 / EMBED)
        if block:
            store_seq(block - 1).wait()
        pieces = []
        for (at, width), a, d in zip(PIECES, attn, d_attn):
            grade = 0.5 * a * (d - inner)
            pieces.append(grade * stretch(rows, at, width))
            d_seq[:, at : at + width] = (a * d_pooled[:, :width] + grade * probe[:, :width]).astype(BF16)
        store_seq(block).start()
        wide = narrow_sum(pieces)
        d_probe_rows[rows] = exact(wide, pooled_w[...])
        d_target = exact(wide, target_w[...])
        d_fields[rows] = d_joined
        d_fields[rows, :LANES] = jnp.where(lanes(head.shape) < EMBED, d_target, head)

    def attention_weights():
        target = fields[:, 0:LANES].astype(F32)[:, :EMBED]
        d_probe = d_probe_rows[...][:, :EMBED]
        query_grad = exact_rows(target, exact(d_probe, w_key[...]))
        key_grad = exact_rows(d_probe, exact(target, w_query[...]))
        value_grad = exact_rows(pooled_rows[...][:, :EMBED], d_value_rows[...][:, :EMBED])
        grads = (query_grad, key_grad, value_grad)
        tiny[0, :EMBED] = sum(exact(g, lane_match(EMBED, LANES, 0, EMBED * i)) for i, g in enumerate(grads))

    def half_of(m, half):
        if m < 6:
            grad = contract_rows(active[m], d_expert[m, :, pl.ds(pl.multiple_of(half * 256, 256), 256)])
            return [grad[:, :LANES], grad[:, LANES:]]
        if m < 12:
            grad = contract_rows(normed[...], slope[m - 6, :, pl.ds(pl.multiple_of(half * 512, 512), 512)])
            columns = [grad[:, i * LANES : (i + 1) * LANES] for i in range(4)]
            return [jnp.concatenate(columns[:2], axis=0), jnp.concatenate(columns[2:], axis=0)]
        grad = contract_rows(residual_low[...], d_tower[:, pl.ds(pl.multiple_of(half * 256, 256), 256)])
        return [jnp.concatenate([grad[:, :LANES], grad[:, LANES:]], axis=0)]

    def proj_half(half):
        grad = contract_rows(joined[...], d_proj_low[:, pl.ds(pl.multiple_of(half * 256, 256), 256)])
        columns = []
        for j in range(2):
            column = grad[:, j * LANES : (j + 1) * LANES]
            columns += [column[EMBED:], column[:EMBED]]
        flat = jnp.concatenate(columns, axis=0)
        return [flat[unit * PROJ_ROWS : (unit + 1) * PROJ_ROWS] for unit in range(DIMS)]

    def small_half(half):
        columns = [small[:, pl.ds(pl.multiple_of(half * 256 + j * LANES, LANES), LANES)] for j in range(2)]
        return [jnp.concatenate(columns, axis=0)]

    def tiny_copy(step):
        return pltpu.make_async_remote_copy(
            src_ref=tiny.at[step],
            dst_ref=tiny_arrived.at[step],
            send_sem=tiny_send.at[step],
            recv_sem=tiny_recv.at[step],
            device_id=sibling() if step == DIMS else neighbour(step),
            device_id_type=MESH,
        )

    def tiny_step(step):
        if step:
            tiny_copy(step - 1).wait_recv()
            tiny[step] = tiny[step - 1] + tiny_arrived[step - 1]
        if step <= DIMS:
            tiny_copy(step).start()

    def expert_back(e):
        expert_backward(e, 0)

    def forward_all():
        prepare()
        lax.fori_loop(0, ROWS // BLOCK, attention_forward, 0)
        front_forward()
        lax.fori_loop(0, EXPERTS, expert_forward, 0)
        tower_both()
        d_normed[...] = jnp.zeros_like(d_normed)
        d_mixing[...] = jnp.zeros_like(d_mixing)
        lax.fori_loop(0, EXPERTS, spread_residual, 0)
        pl.semaphore_wait(barrier, 7)

    def family(i, first=0, to_other=False):
        out = (big_out, proj_out, small_out)[i]
        return Family(FAMILIES[i][3], out, family_refs[9 * i : 9 * i + 9], first, to_other)

    def perform(plan, big, extra):
        work = {
            "send": lambda m: big.send(m, 2 * m, half_of(m, 1 - core)),
            "take": lambda m: big.take(m, 2 * m, half_of(m, core)),
            "back": expert_back,
            "sum": lambda c, step: big.reduce(DIMS * c, DIMS, step),
            "all": lambda c, step: big.gather(DIMS * c, DIMS, step),
            **extra,
        }
        for name, *where in plan:
            work[name](*where)

    @pl.when(section == 0)
    def _():
        big = family(0, 2 * SPLIT, True)
        proj = family(1)
        forward_all()
        perform(
            PLAN_FIRST,
            big,
            {
                "front": front_backward,
                "seq": attention_back,
                "weights": attention_weights,
                "send_p": lambda: proj.send(0, 0, proj_half(1 - core)),
                "take_p": lambda: proj.take(0, 0, proj_half(core)),
                "sum_p": lambda step: proj.reduce(0, DIMS, step),
                "all_p": lambda step: proj.gather(0, DIMS, step),
                "tiny": tiny_step,
            },
        )
        big.drain(FAMILIES[0][0] - 2 * SPLIT, 0)
        proj.drain(DIMS, DIMS)
        for step in range(DIMS + 1):
            tiny_copy(step).wait_send()
        result = pltpu.make_async_copy(tiny.at[DIMS + 1], tiny_out, load_sem.at[12])
        result.start()
        store_seq(3).wait()
        result.wait()

    @pl.when(section == 1)
    def _():
        big = family(0)
        vectors = family(2)
        forward_all()
        perform(
            PLAN_SECOND,
            big,
            {
                "front": front_backward,
                "send_v": lambda: vectors.send(0, 0, small_half(1 - core)),
                "take_v": lambda: vectors.take(0, 0, small_half(core)),
                "sum_v": lambda step: vectors.reduce(0, 1, step),
                "all_v": lambda step: vectors.gather(0, 1, step),
            },
        )
        big.drain(2 * SPLIT, FAMILIES[0][0])
        vectors.drain(1, 1)


def run(*args):
    here = pl.BlockSpec(memory_space=pltpu.VMEM)
    far = pl.BlockSpec(memory_space=pl.ANY)

    def keep(*shape, dtype=F32):
        return pltpu.VMEM(shape, dtype)

    scratch = [
        keep(ROWS, SEQ, dtype=BF16),
        keep(EXPERTS, HIDDEN, WIDE, dtype=BF16),
        keep(EXPERTS, WIDE, HIDDEN, dtype=BF16),
        keep(SPAN, SPAN, dtype=BF16),
        keep(EMBED, SPAN),
        keep(SPAN, LANES),
        keep(SPAN, LANES),
        keep(EMBED, SPAN),
        keep(SPAN, LANES),
        keep(FIELDS, HIDDEN, dtype=BF16),
        keep(16, HIDDEN, dtype=BF16),
        keep(ROWS, 8),
        keep(ROWS, FIELDS, dtype=BF16),
        keep(ROWS, HIDDEN),
        keep(ROWS, HIDDEN),
        keep(ROWS, HIDDEN, dtype=BF16),
        keep(ROWS, HIDDEN),
        keep(EXPERTS, ROWS, WIDE, dtype=BF16),
        keep(EXPERTS, ROWS, WIDE, dtype=BF16),
        keep(EXPERTS, ROWS, HIDDEN, dtype=BF16),
        keep(EXPERTS, ROWS, HIDDEN, dtype=BF16),
        keep(ROWS, HIDDEN),
        keep(ROWS, HIDDEN),
        keep(ROWS, 8),
        keep(ROWS, 8),
        keep(ROWS, 8),
        keep(ROWS, HIDDEN, dtype=BF16),
        keep(ROWS, HIDDEN, dtype=BF16),
        keep(ROWS, HIDDEN, dtype=BF16),
        keep(ROWS, LANES),
        keep(ROWS, LANES),
        keep(ROWS, LANES),
        keep(64, HIDDEN),
        keep(DIMS + 2, TINY_ROWS, LANES),
        keep(DIMS + 1, TINY_ROWS, LANES),
        keep(BLOCK, SEQ, dtype=BF16),
        pltpu.SemaphoreType.DMA((13,)),
        pltpu.SemaphoreType.DMA((4,)),
        pltpu.SemaphoreType.DMA((DIMS + 1,)),
        pltpu.SemaphoreType.DMA((DIMS + 1,)),
    ]
    for family in FAMILIES:
        scratch += family_scratch(*family)
    outs = [jax.ShapeDtypeStruct((units, 2, rows, LANES), dtype) for units, _, _, rows, dtype in FAMILIES]
    outs += [
        jax.ShapeDtypeStruct((TINY_ROWS, LANES), F32),
        jax.ShapeDtypeStruct((2, 8, LANES), F32),
        jax.ShapeDtypeStruct((ROWS, FIELDS), F32),
        jax.ShapeDtypeStruct((ROWS, SEQ), BF16),
    ]
    return pl.pallas_call(
        kernel,
        out_shape=outs,
        in_specs=[here] * 19 + [far] * 3,
        out_specs=[far] * 4 + [here] * 2 + [far],
        scratch_shapes=scratch,
        compiler_params=pltpu.CompilerParams(
            collective_id=0, has_side_effects=True, vmem_limit_bytes=64 << 20
        ),
        name="rank_and_sum",
    )(*args)


def place_kernel(
    out_units,
    in_units,
    tower_unit,
    proj_units,
    small,
    tiny,
    pred_all,
    field_rows,
    seq_rows,
    out_grad,
    in_grad,
    predictions,
    field_grad,
    seq_grad,
    proj,
    tower,
    b_proj,
    gain,
    shift,
    tower_b,
    tower_o,
    tower_e,
    roots,
    gate,
    in_b,
    out_b,
    query,
    key,
    value,
):
    step = pl.program_id(0)
    section = lax.axis_index("section")
    second = (section == 1).astype(F32)
    first = 1.0 - second

    @pl.when(section == 1)
    def _():
        for core in range(2):
            for j in range(2):
                at = (2 * core + j) * LANES
                out_grad[0, 0, :, at : at + LANES] = out_units[j, core].astype(F32)
                for i in range(2):
                    at = (4 * core + 2 * j + i) * LANES
                    in_grad[0, 0, :, at : at + LANES] = in_units[j, core, i * 512 : (i + 1) * 512].astype(F32)

    @pl.when(section == 0)
    def _():
        out_grad[...] = jnp.zeros_like(out_grad)
        in_grad[...] = jnp.zeros_like(in_grad)

    @pl.when(step < 4)
    def _():
        field_grad[0] = jnp.where(section == 0, field_rows[...], 0.0)
        seq_grad[0] = jnp.where(section == 0, seq_rows[...].astype(F32), 0.0)

    @pl.when(step == 0)
    def _():
        for j in range(2):
            at = slice(j * LANES, (j + 1) * LANES)
            predictions[:, at] = jnp.where(section == 1, pred_all[j, 0:1], 0.0)
        for core in range(2):
            flat = jnp.concatenate([proj_units[i, core].astype(F32) for i in range(DIMS)], axis=0)
            for j in range(2):
                at = slice((2 * core + j) * LANES, (2 * core + j + 1) * LANES)
                block = tower_unit[0, core, j * 512 : (j + 1) * 512].astype(F32)
                tower[0, :, at] = jnp.where(section == 1, block, 0.0)
                proj[0, :, at] = jnp.where(section == 0, flat[j * FIELDS : (j + 1) * FIELDS], 0.0)

        def rows(start, count):
            found = jnp.concatenate(
                [small[core, j * 64 + start : j * 64 + start + count] for core in range(2) for j in range(2)],
                axis=1,
            )
            return jnp.where(section == 1, found, 0.0)

        head = rows(0, 8)
        gain[...] = head[1:2] * second
        shift[...] = head[2:3] * second
        tower_b[...] = head[3:4] * second
        tower_o[...] = head[4:5] * second
        tower_e[...] = head[5:6, 0:2] * second
        count = head[5:6, 4:5]
        squares = head[5:6, 2:4] / (float(HIDDEN) * jnp.maximum(count, 1.0)) + EPSILON
        roots[...] = jnp.where(count > 0.0, jnp.sqrt(squares), 0.0) * second
        gate_lines, out_lines = rows(8, 8) * second, rows(32, 8) * second
        in_lines = jnp.concatenate([rows(16, 8), rows(24, 8)], axis=1) * second
        for i in range(7):
            gate[i] = gate_lines[i : i + 1]
        for e in range(EXPERTS):
            in_b[e] = in_lines[e : e + 1]
            out_b[e] = out_lines[e : e + 1]
        three = jnp.where(section == 0, tiny[...], 0.0)
        b_proj[...] = jnp.concatenate([three[16 + i : 17 + i] for i in range(4)], axis=1)
        query[0] = three[:EMBED, 0:16]
        key[0] = three[:EMBED, 16:32]
        value[0] = three[:EMBED, 32:48]


def place(big, proj, small, tiny, pred_all, field_rows, seq_rows):
    def whole(*shape):
        return jax.ShapeDtypeStruct(shape, F32), pl.BlockSpec(shape, lambda i: (0,) * len(shape))

    def strip(width):
        return (
            jax.ShapeDtypeStruct((1, ROWS, width), F32),
            pl.BlockSpec((1, BLOCK, width), lambda i: (0, jnp.minimum(i, 3), 0)),
        )

    shapes, specs = zip(
        (jax.ShapeDtypeStruct((1, 6, 1024, 512), F32), pl.BlockSpec((1, 1, 1024, 512), lambda i: (0, i, 0, 0))),
        (jax.ShapeDtypeStruct((1, 6, 512, 1024), F32), pl.BlockSpec((1, 1, 512, 1024), lambda i: (0, i, 0, 0))),
        whole(1, ROWS),
        strip(FIELDS),
        strip(SEQ),
        whole(1, 640, 512),
        whole(1, 512, 512),
        whole(1, 512),
        whole(1, 512),
        whole(1, 512),
        whole(1, 512),
        whole(1, 512),
        whole(1, 2),
        whole(1, 2),
        whole(7, 1, 512),
        whole(6, 1, 1024),
        whole(6, 1, 512),
        whole(1, 16, 16),
        whole(1, 16, 16),
        whole(1, 16, 16),
    )
    return pl.pallas_call(
        place_kernel,
        grid=(6,),
        out_shape=shapes,
        in_specs=[
            pl.BlockSpec((2, 2, 1024, LANES), lambda i: (i, 0, 0, 0)),
            pl.BlockSpec((2, 2, 1024, LANES), lambda i: (i + 6, 0, 0, 0)),
            pl.BlockSpec((1, 2, 1024, LANES), lambda i: (24, 0, 0, 0)),
            pl.BlockSpec((DIMS, 2, PROJ_ROWS, LANES), lambda i: (0, 0, 0, 0)),
            pl.BlockSpec((2, SMALL_ROWS, LANES), lambda i: (0, 0, 0)),
            pl.BlockSpec((TINY_ROWS, LANES), lambda i: (0, 0)),
            pl.BlockSpec((2, 8, LANES), lambda i: (0, 0, 0)),
            pl.BlockSpec((BLOCK, FIELDS), lambda i: (jnp.minimum(i, 3), 0)),
            pl.BlockSpec((BLOCK, SEQ), lambda i: (jnp.minimum(i, 3), 0)),
        ],
        out_specs=specs,
        compiler_params=pltpu.CompilerParams(vmem_limit_bytes=56 << 20),
        name="place",
    )(big, big, big, proj, small, tiny, pred_all, field_rows, seq_rows)


def body(
    fields,
    behaviour,
    lengths,
    domains,
    validity,
    cotangent,
    w_query,
    w_key,
    w_value,
    w_proj,
    b_proj,
    norm_gain,
    norm_shift,
    gate_weight,
    w_in,
    b_in,
    w_out,
    b_out,
    tower_in,
    tower_bias,
    tower_out,
    tower_end,
):
    def line(array):
        return array.reshape(1, -1)

    big, proj, small, tiny, pred_all, field_rows, seq_rows = run(
        fields,
        line(lengths),
        line(domains),
        line(validity),
        line(cotangent),
        w_query,
        w_key,
        w_value,
        w_proj,
        line(b_proj),
        line(norm_gain),
        line(norm_shift),
        gate_weight.T,
        b_in,
        b_out,
        tower_in,
        line(tower_bias),
        line(tower_out),
        line(tower_end),
        behaviour,
        w_in,
        w_out,
    )
    (
        out_grad,
        in_grad,
        predictions,
        field_grad,
        seq_grad,
        proj,
        tower,
        b_proj_grad,
        gain,
        shift,
        tower_b,
        tower_o,
        tower_e,
        roots,
        gate,
        in_b,
        out_b,
        query,
        key,
        value,
    ) = place(big, proj, small.reshape(2, SMALL_ROWS, LANES), tiny, pred_all, field_rows, seq_rows)
    return (
        predictions,
        field_grad,
        seq_grad,
        query,
        key,
        value,
        proj,
        b_proj_grad,
        gain,
        shift,
        gate.transpose(1, 2, 0),
        in_grad,
        in_b.transpose(1, 0, 2),
        out_grad,
        out_b.transpose(1, 0, 2),
        tower,
        tower_b,
        tower_o,
        tower_e,
        roots,
    )


def solution(mesh):
    each = (P("dp", None), P("dp", None), P("dp"), P("dp"), P("dp"), P("dp"))
    ranks = (2, 3, 3, 3, 3, 3, 3, 2, 2, 2, 3, 4, 3, 4, 3, 3, 2, 2, 2, 2)
    outs = tuple(
        P("section", "dp", *(None,) * (rank - 2)) if i < 3 else P("section", *(None,) * (rank - 1))
        for i, rank in enumerate(ranks)
    )
    return jax.shard_map(
        body, mesh=mesh, in_specs=each + (P(),) * 16, out_specs=outs, check_vma=False
    )
```

```python
import jax
import jax.numpy as jnp
from jax import lax
from jax.experimental import pallas as pl
from jax.experimental.pallas import tpu as pltpu
from jax.sharding import PartitionSpec as P

EPSILON = 1e-05
MESH = pl.DeviceIdType.MESH
F32 = jnp.float32
BF16 = jnp.bfloat16

LANES = 128
DIMS = 5
HALVINGS = 3
SLOTS = 7 + HALVINGS
ROWS = 256
EXPERTS = 6
HIDDEN = 512
WIDE = 1024
FIELDS = 640
EMBED = 16
SEQ = 3200
SPAN = 256
PIECES = tuple((at, SPAN) for at in range(0, 3072, SPAN)) + ((3072, LANES),)
PROJ_ROWS = 256
SMALL_ROWS = 128
BLOCK = 64


def coords():
    section, place = lax.axis_index("section"), lax.axis_index("dp")
    return 2 * section + place // 32, (place // 8) % 4, (place // 2) % 4, place % 2


def device_at(z, x, y, core):
    return {"section": z // 2, "dp": (((z % 2) * 4 + x) * 4 + y) * 2 + core}


def hop(r, kind):
    near, far = 1 - 2 * (r % 2), 3 - 2 * r
    return near + kind * (far - near)


def side(r, kind):
    near = (r + r // 2) % 2
    return near + kind * (r // 2 - near)


def picks(dim):
    a = dim % 3
    return (1 - a) * (2 - a) // 2, a * (2 - a), a * (a - 1) // 2, dim // 3


def neighbour(dim):
    z, x, y, core = coords()
    ex, ey, ez, kind = picks(dim)
    return device_at(z + ez * hop(z, kind), x + ex * hop(x, kind), y + ey * hop(y, kind), core)


def which_half(dim):
    z, x, y, core = coords()
    ex, ey, ez, kind = picks(dim)
    return ex * side(x, kind) + ey * side(y, kind) + ez * side(z, kind)


def sibling():
    z, x, y, core = coords()
    return device_at(z, x, y, 1 - core)


def cross():
    z, x, y, core = coords()
    return device_at(3 - z, x, y, core)


class Family:
    def __init__(self, rows, out, refs, first, to_other=False):
        self.rows = rows
        self.share = rows >> HALVINGS
        self.out = out
        self.first = first
        self.to_other = to_other
        (
            self.kept,
            self.arrived,
            self.doubled,
            self.pair_send,
            self.pair_recv,
            self.send_sem,
            self.recv_sem,
        ) = refs

    def total(self, units, rows=slice(None)):
        return self.out.at[units, coords()[3], rows]

    def remote(self, unit, slot, src, dst, to):
        return pltpu.make_async_remote_copy(
            src_ref=src,
            dst_ref=dst,
            send_sem=self.send_sem.at[slot],
            recv_sem=self.recv_sem.at[unit // DIMS, slot],
            device_id=to,
            device_id_type=MESH,
        )

    def start_of(self, part, step):
        start = 0
        for k in range(step):
            start = start + which_half((part + k) % DIMS) * (self.rows >> (k + 1))
        return start

    def span(self, start, size):
        return pl.ds(pl.multiple_of(start, size), size)

    def own_share(self, unit):
        return self.span(self.start_of(unit % DIMS, HALVINGS), self.share)

    def across(self, group, unit, count):
        return pltpu.make_async_remote_copy(
            src_ref=self.total(pl.ds(unit, count)),
            dst_ref=self.kept.at[pl.ds(unit - self.first, count)],
            send_sem=self.pair_send.at[group],
            recv_sem=self.pair_recv.at[group],
            device_id=sibling(),
            device_id_type=MESH,
        )

    def halve(self, unit, k):
        size = self.rows >> (k + 1)
        dim = (unit + k) % DIMS
        start = self.start_of(unit % DIMS, k) + (1 - which_half(dim)) * size
        local = unit - self.first
        return self.remote(
            unit,
            k,
            self.kept.at[local, self.span(start, size)],
            self.arrived.at[local, pl.ds(self.rows - 2 * size, size)],
            neighbour(dim),
        )

    def double(self, unit, j):
        local = unit - self.first
        src = self.kept.at[local, self.own_share(unit)] if j == 0 else self.doubled.at[local, j - 1]
        return self.remote(
            unit,
            HALVINGS + j,
            src,
            self.arrived.at[local, pl.ds(self.rows - self.share + j * self.share, self.share)],
            neighbour((unit + HALVINGS + j) % DIMS),
        )

    def over(self, unit):
        region = self.total(unit, self.own_share(unit))
        return self.remote(unit, DIMS, region, region, cross())

    def spread(self, unit, k):
        size = self.rows >> (k + 1)
        region = self.total(unit, self.span(self.start_of(unit % DIMS, k + 1), size))
        return self.remote(unit, DIMS + 1 + k, region, region, neighbour((unit + k) % DIMS))

    def back(self, unit):
        return self.remote(unit, DIMS + 1 + HALVINGS, self.total(unit), self.total(unit), sibling())

    def send(self, group, unit, halves):
        for i, rows in enumerate(halves):
            self.out[unit + i, coords()[3]] = rows.astype(self.out.dtype)
        self.across(group, unit, len(halves)).start()

    def take(self, group, unit, halves):
        pair = self.across(group, unit, len(halves))
        pair.wait_send()
        pair.wait_recv()
        for i, rows in enumerate(halves):
            local = unit + i - self.first
            self.kept[local] = (rows + self.kept[local].astype(F32)).astype(self.kept.dtype)
            self.halve(unit + i, 0).start()

    def await_chunk(self, slot, base, ref):
        pltpu.make_async_copy(ref, ref, self.recv_sem.at[base // DIMS, slot]).wait()

    def each(self, base, count, work):
        def one(i, _):
            work(base + i)
            return 0

        lax.fori_loop(0, count, one, 0)

    def reduce(self, base, count, step):
        dtype = self.kept.dtype
        local = pl.ds(base - self.first, count)
        if step < HALVINGS:
            size = self.rows >> (step + 1)
            arrivals = pl.ds(self.rows - 2 * size, size)
        else:
            size = self.share
            arrivals = pl.ds(self.rows - size + (step - HALVINGS) * size, size)
        self.await_chunk(step, base, self.arrived.at[local, arrivals])

        def one(unit):
            here = unit - self.first
            came = self.arrived[here, arrivals].astype(F32)
            if step < HALVINGS:
                region = self.span(self.start_of(unit % DIMS, step + 1), size)
                self.kept[here, region] = (self.kept[here, region].astype(F32) + came).astype(dtype)
                if step + 1 < HALVINGS:
                    self.halve(unit, step + 1).start()
                else:
                    self.double(unit, 0).start()
                return
            j = step - HALVINGS
            region = self.own_share(unit)
            old = self.kept[here, region] if j == 0 else self.doubled[here, j - 1]
            new = (old.astype(F32) + came).astype(dtype)
            if step + 1 < DIMS:
                self.doubled[here, j] = new
                self.double(unit, j + 1).start()
            else:
                self.out[unit, coords()[3], region] = new
                if self.to_other:
                    self.over(unit).start()
                else:
                    self.spread(unit, HALVINGS - 1).start()

        self.each(base, count, one)

    def gather(self, base, count, step):
        units = pl.ds(base, count)
        if step == 0:
            self.await_chunk(DIMS, base, self.total(units, pl.ds(0, self.share)))
            self.each(base, count, lambda unit: self.spread(unit, HALVINGS - 1).start())
        elif step <= HALVINGS:
            k = HALVINGS - step
            self.await_chunk(DIMS + 1 + k, base, self.total(units, pl.ds(0, self.rows >> (k + 1))))

            def one(unit):
                if k > 0:
                    self.spread(unit, k - 1).start()
                else:
                    self.back(unit).start()

            self.each(base, count, one)
        else:
            self.await_chunk(DIMS + 1 + HALVINGS, base, self.out.at[units, 1 - coords()[3]])

    def drain(self, reduced, gathered):
        def sent(slot, ref):
            pltpu.make_async_copy(ref, ref, self.send_sem.at[slot]).wait()

        for step in range(DIMS):
            size = self.rows >> (step + 1) if step < HALVINGS else self.share
            sent(step, self.kept.at[pl.ds(0, reduced), pl.ds(0, size)])
        if self.to_other:
            sent(DIMS, self.kept.at[pl.ds(0, reduced), pl.ds(0, self.share)])
        if gathered:
            for k in range(HALVINGS):
                sent(DIMS + 1 + k, self.total(pl.ds(0, gathered), pl.ds(0, self.rows >> (k + 1))))
            sent(DIMS + 1 + HALVINGS, self.total(pl.ds(0, gathered)))


def family_scratch(units, reduced, groups, rows, dtype):
    share = rows >> HALVINGS
    chunks = pl.cdiv(units, DIMS)
    return [
        pltpu.VMEM((reduced, rows, LANES), dtype),
        pltpu.VMEM((reduced, rows - share + (DIMS - HALVINGS) * share, LANES), dtype),
        pltpu.VMEM((reduced, max(1, DIMS - HALVINGS - 1), share, LANES), dtype),
        pltpu.SemaphoreType.DMA((groups,)),
        pltpu.SemaphoreType.DMA((groups,)),
        pltpu.SemaphoreType.DMA((SLOTS,)),
        pltpu.SemaphoreType.DMA((chunks, SLOTS)),
    ]


FAMILIES = ((25, 15, 13, 1024, BF16), (DIMS, DIMS, 1, PROJ_ROWS, BF16), (1, 1, 1, SMALL_ROWS, F32))
TOWER_UNIT = 12
IN_UNIT = 13
SPLIT = 15
TINY_ROWS = 24


PLAN_FIRST = (
    ("ins", 1, 6), ("back", 0, 1), ("sum", 3, 0), ("front",), ("sum", 3, 1), ("sum", 4, 0), ("send_p",), ("sum", 3, 2),
    ("sum", 4, 1), ("take_p",), ("sum", 3, 3), ("sum", 4, 2), ("sum", 3, 4), ("sum", 4, 3), ("sum_p", 0), ("sum", 4, 4),
    ("sum_p", 1), ("seq", 0, 2), ("sum_p", 2), ("seq", 2, 4), ("sum_p", 3), ("weights",), ("tiny", 0), ("sum_p", 4),
    ("tiny", 1), ("all_p", 1), ("tiny", 2), ("all_p", 2), ("tiny", 3), ("all_p", 3), ("tiny", 4), ("all_p", 4),
    ("tiny", 5), ("tiny", 6),
)
PLAN_SECOND = (
    ("outs", 0, 6), ("tower",), ("ins", 0, 1), ("sum", 0, 0), ("back", 1, 3), ("sum", 1, 0), ("sum", 0, 1),
    ("back", 3, 6), ("sum", 0, 2), ("sum", 1, 1), ("sum", 2, 0), ("front",), ("sum", 0, 3), ("sum", 1, 2), ("sum", 2, 1),
    ("send_v",), ("sum", 0, 4), ("sum", 1, 3), ("sum", 2, 2), ("take_v",), ("all", 0, 1), ("sum", 1, 4), ("sum", 2, 3),
    ("sum_v", 0), ("all", 0, 2), ("all", 1, 1), ("sum", 2, 4), ("sum_v", 1), ("all", 3, 0), ("all", 0, 3), ("all", 1, 2),
    ("all", 2, 1), ("sum_v", 2), ("all", 3, 1), ("all", 4, 0), ("all", 1, 3), ("all", 2, 2), ("sum_v", 3), ("all", 0, 4),
    ("all", 3, 2), ("all", 4, 1), ("sum_v", 4), ("all", 2, 3), ("all", 1, 4), ("all_v", 1), ("all", 3, 3), ("all", 4, 2),
    ("all_v", 2), ("all", 2, 4), ("all", 4, 3), ("all_v", 3), ("all", 3, 4), ("all_v", 4), ("all", 4, 4),
)


def exact(left, right):
    return jnp.dot(left, right, precision=lax.Precision.HIGHEST, preferred_element_type=F32)


def exact_cols(left, right):
    return lax.dot_general(
        left, right, (((1,), (1,)), ((), ())), precision=lax.Precision.HIGHEST, preferred_element_type=F32
    )


def exact_rows(left, right):
    return lax.dot_general(
        left, right, (((0,), (0,)), ((), ())), precision=lax.Precision.HIGHEST, preferred_element_type=F32
    )


def product(left, right):
    return jnp.dot(left, right, preferred_element_type=F32)


def contract_rows(left, right):
    return lax.dot_general(left, right, (((0,), (0,)), ((), ())), preferred_element_type=F32)


def contract_cols(left, right):
    return lax.dot_general(left, right, (((1,), (1,)), ((), ())), preferred_element_type=F32)


def split(value, terms):
    out = []
    for _ in range(terms):
        out.append(value.astype(BF16))
        value = value - out[-1].astype(F32)
    return out


def sigmoid(v):
    return 1.0 / (1.0 + jnp.exp(-v))


ROOT = 0.7978845608028654
CUBE = 0.044715


def gelu_both(v):
    square = v * v
    bent = jnp.tanh(v * (ROOT + ROOT * CUBE * square))
    half = 0.5 + 0.5 * bent
    slope = half + 0.5 * v * (1.0 - bent * bent) * (ROOT + 3.0 * ROOT * CUBE * square)
    return v * half, slope


def column_sum(array):
    return jnp.sum(array, axis=0, keepdims=True)


def row_sum(array):
    return jnp.sum(array, axis=1, keepdims=True)


def lanes(shape):
    return lax.broadcasted_iota(jnp.int32, shape, 1)


def lane_match(rows, columns, period, shift=0):
    place = lax.broadcasted_iota(jnp.int32, (rows, columns), 1) - shift
    if period:
        place = place % period
    return (place == lax.broadcasted_iota(jnp.int32, (rows, columns), 0)).astype(F32)


def kernel(
    fields,
    lengths,
    domains,
    validity,
    cotangent,
    w_query,
    w_key,
    w_value,
    w_proj,
    b_proj,
    norm_gain,
    norm_shift,
    gate_turned,
    b_in,
    b_out,
    tower_in,
    tower_bias,
    tower_out,
    tower_end,
    behaviour_hbm,
    w_in_hbm,
    w_out_hbm,
    big_out,
    proj_out,
    small_out,
    tiny_out,
    pred_all,
    d_fields,
    d_seq,
    behaviour,
    w_in,
    w_out,
    groups,
    probe_w,
    value_w,
    pooled_w,
    back_w,
    target_w,
    proj_turned,
    gate_rows,
    info,
    joined,
    activation,
    proj_slope,
    normed,
    standard,
    active,
    slope,
    expert,
    d_expert,
    d_normed,
    d_residual,
    mixing,
    d_mixing,
    gates,
    residual_low,
    d_tower,
    d_proj_low,
    pooled_rows,
    d_value_rows,
    d_probe_rows,
    small,
    tiny,
    tiny_arrived,
    load_sem,
    tiny_send,
    tiny_recv,
    *family_refs,
):
    section = lax.axis_index("section")
    core = coords()[3]

    barrier = pltpu.get_barrier_semaphore()
    for dim in range(DIMS):
        pl.semaphore_signal(barrier, inc=1, device_id=neighbour(dim), device_id_type=MESH)
    for other in (sibling(), cross()):
        pl.semaphore_signal(barrier, inc=1, device_id=other, device_id_type=MESH)

    seq_copy = pltpu.make_async_copy(behaviour_hbm, behaviour, load_sem.at[12])

    def load_in(e):
        return pltpu.make_async_copy(w_in_hbm.at[e], w_in.at[e], load_sem.at[e])

    def load_out(e):
        return pltpu.make_async_copy(w_out_hbm.at[e], w_out.at[e], load_sem.at[6 + e])

    tile = lane_match(EMBED, SPAN, EMBED)

    def prepare():
        seq_copy.start()
        for e in range(EXPERTS):
            load_in(e).start()
            load_out(e).start()
        group = lax.broadcasted_iota(jnp.int32, (SPAN, SPAN), 0) // EMBED
        groups[...] = (group == lanes((SPAN, SPAN)) // EMBED).astype(F32).astype(BF16)
        eye = lane_match(EMBED, LANES, 0)
        probe_w[...] = exact(w_query[...], exact_rows(w_key[...], tile))
        value_w[...] = exact_rows(tile, exact(w_value[...], eye))
        pooled_w[...] = exact_rows(tile, eye)
        back_w[...] = exact_rows(w_value[...], tile)
        target_w[...] = exact_rows(tile, exact(exact_cols(w_key[...], w_query[...]), eye))
        proj_turned[:EMBED] = w_proj[FIELDS - EMBED :]
        proj_turned[EMBED:] = w_proj[: FIELDS - EMBED]
        rows = [lengths[...].astype(F32), domains[...].astype(F32), validity[...].astype(F32), cotangent[...]]
        info[...] = jnp.transpose(jnp.concatenate(rows + [jnp.zeros((4, ROWS), F32)], axis=0))
        gate_rows[...] = jnp.zeros_like(gate_rows)
        gate_rows[:7] = gate_turned[...]
        small[...] = jnp.zeros_like(small)
        tiny[0] = jnp.zeros((TINY_ROWS, LANES), F32)
        seq_copy.wait()

    def group_sum(value, terms):
        count, width = value.shape
        stacked = jnp.concatenate(split(value, terms), axis=0)
        sums = product(stacked, groups[:width, :width])
        return sum(sums[i * count : (i + 1) * count] for i in range(terms))

    def narrow_sum(pieces):
        wide = sum(pieces[:-1])
        return jnp.concatenate([wide[:, :LANES] + pieces[-1], wide[:, LANES:]], axis=1)

    def stretch(rows, at, width):
        return behaviour[rows, at : at + width].astype(F32)

    def attention(rows):
        target = fields[rows, 0:LANES].astype(F32)[:, :EMBED]
        probe = exact(target, probe_w[...])
        length = info[rows, 0:1]
        scores = []
        for at, width in PIECES:
            sums = group_sum(stretch(rows, at, width) * probe[:, :width], 3)
            place = ((lanes((1, width)) + at) // EMBED).astype(F32)
            scores.append(jnp.where(place < length, 0.5 * sums, -1e30))
        peak = scores[0]
        for piece in scores[1:-1]:
            peak = jnp.maximum(peak, piece)
        peak = jnp.maximum(jnp.max(peak, axis=1, keepdims=True), jnp.max(scores[-1], axis=1, keepdims=True))
        raised = [jnp.exp(piece - peak) for piece in scores]
        scale = float(EMBED) / row_sum(narrow_sum(raised))
        return probe, [piece * scale for piece in raised]

    def pool(rows, attn):
        return narrow_sum([w * stretch(rows, at, width) for w, (at, width) in zip(attn, PIECES)])

    def attention_forward(block, _):
        rows = pl.ds(pl.multiple_of(block * BLOCK, BLOCK), BLOCK)
        _, attn = attention(rows)
        value = exact(pool(rows, attn), value_w[...])
        joined[rows, LANES:] = fields[rows, LANES:]
        head = fields[rows, :LANES]
        joined[rows, :LANES] = jnp.where(lanes(head.shape) < EMBED, value.astype(BF16), head)
        return 0

    def gate_columns():
        return [gates[:, i : i + 1] for i in range(6)]

    def front_forward():
        projected = product(joined[...], proj_turned[...]) + b_proj[...]
        act, slope_proj = gelu_both(projected)
        act = act.astype(BF16).astype(F32)
        activation[...] = act
        proj_slope[...] = slope_proj
        centred = act - row_sum(act) * (1.0 / HIDDEN)
        scale = lax.rsqrt(row_sum(centred * centred) * (1.0 / HIDDEN) + EPSILON)
        standard[...] = centred * scale
        normed[...] = (centred * scale * norm_gain[...] + norm_shift[...]).astype(BF16)

        logits = contract_cols(normed[...], gate_rows[...])
        in_first = info[:, 1:2] == 0.0
        level = sigmoid(logits[:, 6:7])
        shared_a = sigmoid(logits[:, 0:1] - logits[:, 1:2])
        shared_b = sigmoid(logits[:, 1:2] - logits[:, 0:1])
        lead = jnp.where(in_first, logits[:, 2:3] - logits[:, 3:4], logits[:, 4:5] - logits[:, 5:6])
        chosen_a, chosen_b = sigmoid(lead), sigmoid(-lead)
        zero = jnp.zeros_like(level)
        columns = [
            level * shared_a,
            level * shared_b,
            jnp.where(in_first, (1.0 - level) * chosen_a, zero),
            jnp.where(in_first, (1.0 - level) * chosen_b, zero),
            jnp.where(in_first, zero, (1.0 - level) * chosen_a),
            jnp.where(in_first, zero, (1.0 - level) * chosen_b),
        ]
        place = lanes((ROWS, 8))
        mixing[...] = sum(jnp.where(place == i, column, 0.0) for i, column in enumerate(columns))
        held = (scale, level, shared_a, shared_b, chosen_a, chosen_b)
        gates[...] = sum(jnp.where(place == i, column, 0.0) for i, column in enumerate(held))
        d_residual[...] = jnp.zeros_like(d_residual)

    def expert_forward(e, _):
        load_in(e).wait()
        load_out(e).wait()
        pre = product(normed[...], w_in[e]) + b_in[pl.ds(e, 1)]
        out, grade = gelu_both(pre)
        active[e] = out.astype(BF16)
        slope[e] = grade.astype(BF16)
        rows = product(active[e], w_out[e]) + b_out[pl.ds(e, 1)]
        expert[e] = rows.astype(BF16)
        weight = row_sum(jnp.where(lanes((ROWS, 8)) == e, mixing[...], 0.0))
        d_residual[...] += weight * rows
        return 0

    def tower_both():
        branch = d_residual[...]
        residual = activation[...] + branch
        in_first = info[:, 1:2] == 0.0
        valid = info[:, 2:3]
        residual_low[...] = residual.astype(BF16)
        tower_act, tower_slope = gelu_both(product(residual_low[...], tower_in[...]) + tower_bias[...])
        chosen = jnp.where(in_first, 0, 1) == lanes((ROWS, HIDDEN)) // 256
        ends = tower_end[...]
        end = jnp.where(in_first, ends[:, 0:1], ends[:, 1:2])
        predict = sigmoid(row_sum(jnp.where(chosen, tower_act * tower_out[...], 0.0)) + end)
        d_logit = info[:, 3:4] * valid * predict * (1.0 - predict)
        spread_logit = jnp.where(chosen, d_logit, 0.0)
        d_tower[...] = (spread_logit * tower_out[...] * tower_slope).astype(BF16)
        small[3:4] = column_sum(d_tower[...].astype(F32))
        small[4:5] = column_sum(tower_act * spread_logit)
        spots = lanes((1, HIDDEN))
        parts = (
            column_sum(jnp.where(in_first, d_logit, 0.0)),
            column_sum(jnp.where(in_first, 0.0, d_logit)),
            column_sum(valid * row_sum(residual * residual)),
            column_sum(valid * row_sum(branch * branch)),
            column_sum(valid),
        )
        small[5:6] = sum(jnp.where(spots == i, part, 0.0) for i, part in enumerate(parts))
        wide = jnp.transpose(jnp.broadcast_to(predict, (ROWS, LANES)))
        pred_all[0] = wide[:8, :LANES]
        pred_all[1] = wide[:8, LANES:]
        d_residual[...] = contract_cols(d_tower[...], tower_in[...])

    def spread_residual(e, _):
        weight = row_sum(jnp.where(lanes((ROWS, 8)) == e, mixing[...], 0.0))
        low = (weight * d_residual[...]).astype(BF16)
        d_expert[e] = low
        small[pl.ds(32 + e, 1)] = column_sum(low.astype(F32))
        inner = row_sum(expert[e].astype(F32) * d_residual[...])
        d_mixing[...] = jnp.where(lanes((ROWS, 8)) == e, inner, d_mixing[...])
        return 0

    def expert_backward(e, _):
        grade = contract_cols(d_expert[e], w_out[e]) * slope[e].astype(F32)
        low = grade.astype(BF16)
        slope[e] = low
        sums = column_sum(low.astype(F32))
        small[pl.ds(16 + e, 1)] = sums[:, :512]
        small[pl.ds(24 + e, 1)] = sums[:, 512:]
        d_normed[...] += contract_cols(low, w_in[e])
        return 0

    def front_backward():
        scale, level, shared_a, shared_b, chosen_a, chosen_b = gate_columns()
        in_first = info[:, 1:2] == 0.0
        grads = [d_mixing[:, e : e + 1] for e in range(EXPERTS)]
        grad_a = jnp.where(in_first, grads[2], grads[4])
        grad_b = jnp.where(in_first, grads[3], grads[5])
        d_level = grads[0] * shared_a + grads[1] * shared_b - grad_a * chosen_a - grad_b * chosen_b
        d_shared = level * shared_a * shared_b * (grads[0] - grads[1])
        d_lead = (1.0 - level) * chosen_a * chosen_b * (grad_a - grad_b)
        zero = jnp.zeros_like(d_lead)
        d_first = jnp.where(in_first, d_lead, zero)
        d_second = jnp.where(in_first, zero, d_lead)
        columns = (d_shared, -d_shared, d_first, -d_first, d_second, -d_second, d_level * level * (1.0 - level))
        place = lanes((ROWS, LANES))
        d_logits = sum(jnp.where(place == i, column, 0.0) for i, column in enumerate(columns)).astype(BF16)
        small[8:16] = jnp.transpose(contract_rows(normed[...], d_logits))[:8]
        total = d_normed[...] + product(d_logits[:, :16], gate_rows[...])
        std = standard[...]
        small[1:2] = column_sum(total * std)
        small[2:3] = column_sum(total)
        scaled = total * norm_gain[...]
        inner = scaled - row_sum(scaled) * (1.0 / HIDDEN) - std * (row_sum(scaled * std) * (1.0 / HIDDEN))
        d_act = (inner * scale + d_residual[...]).astype(BF16).astype(F32)
        low = (d_act * proj_slope[...]).astype(BF16)
        sums = column_sum(low.astype(F32))
        for i in range(HIDDEN // LANES):
            tiny[0, 16 + i : 17 + i] = sums[:, i * LANES : (i + 1) * LANES]
        d_proj_low[...] = low

    def attention_back(block):
        rows = pl.ds(pl.multiple_of(block * BLOCK, BLOCK), BLOCK)
        probe, attn = attention(rows)
        pooled_rows[rows] = exact(pool(rows, attn), pooled_w[...])
        d_joined = contract_cols(d_proj_low[rows], proj_turned[...])
        head = d_joined[:, :LANES]
        d_value_rows[rows] = head
        d_pooled = exact(head[:, :EMBED], back_w[...])
        d_attn = [group_sum(stretch(rows, at, width) * d_pooled[:, :width], 2) for at, width in PIECES]
        inner = row_sum(narrow_sum([a * d for a, d in zip(attn, d_attn)])) * (1.0 / EMBED)
        pieces = []
        for (at, width), a, d in zip(PIECES, attn, d_attn):
            grade = 0.5 * a * (d - inner)
            pieces.append(grade * stretch(rows, at, width))
            d_seq[rows, at : at + width] = (a * d_pooled[:, :width] + grade * probe[:, :width]).astype(BF16)
        wide = narrow_sum(pieces)
        d_probe_rows[rows] = exact(wide, pooled_w[...])
        d_target = exact(wide, target_w[...])
        d_fields[rows] = d_joined
        d_fields[rows, :LANES] = jnp.where(lanes(head.shape) < EMBED, d_target, head)

    def attention_weights():
        target = fields[:, 0:LANES].astype(F32)[:, :EMBED]
        d_probe = d_probe_rows[...][:, :EMBED]
        query_grad = exact_rows(target, exact(d_probe, w_key[...]))
        key_grad = exact_rows(d_probe, exact(target, w_query[...]))
        value_grad = exact_rows(pooled_rows[...][:, :EMBED], d_value_rows[...][:, :EMBED])
        grads = (query_grad, key_grad, value_grad)
        tiny[0, :EMBED] = sum(exact(g, lane_match(EMBED, LANES, 0, EMBED * i)) for i, g in enumerate(grads))

    def out_halves(e, half):
        grad = contract_rows(active[e], d_expert[e, :, pl.ds(pl.multiple_of(half * 256, 256), 256)])
        return [grad[:, :LANES], grad[:, LANES:]]

    def in_halves(e, half):
        grad = contract_rows(normed[...], slope[e, :, pl.ds(pl.multiple_of(half * 512, 512), 512)])
        columns = [grad[:, i * LANES : (i + 1) * LANES] for i in range(4)]
        return [jnp.concatenate(columns[:2], axis=0), jnp.concatenate(columns[2:], axis=0)]

    def tower_halves(half):
        grad = contract_rows(residual_low[...], d_tower[:, pl.ds(pl.multiple_of(half * 256, 256), 256)])
        return [jnp.concatenate([grad[:, :LANES], grad[:, LANES:]], axis=0)]

    def proj_half(half):
        grad = contract_rows(joined[...], d_proj_low[:, pl.ds(pl.multiple_of(half * 256, 256), 256)])
        columns = []
        for j in range(2):
            column = grad[:, j * LANES : (j + 1) * LANES]
            columns += [column[EMBED:], column[:EMBED]]
        flat = jnp.concatenate(columns, axis=0)
        return [flat[unit * PROJ_ROWS : (unit + 1) * PROJ_ROWS] for unit in range(DIMS)]

    def small_half(half):
        columns = [small[:, pl.ds(pl.multiple_of(half * 256 + j * LANES, LANES), LANES)] for j in range(2)]
        return [jnp.concatenate(columns, axis=0)]

    def tiny_copy(step):
        return pltpu.make_async_remote_copy(
            src_ref=tiny.at[step],
            dst_ref=tiny_arrived.at[step],
            send_sem=tiny_send.at[step],
            recv_sem=tiny_recv.at[step],
            device_id=sibling() if step == DIMS else neighbour(step),
            device_id_type=MESH,
        )

    def tiny_step(step):
        if step:
            tiny_copy(step - 1).wait_recv()
            tiny[step] = tiny[step - 1] + tiny_arrived[step - 1]
        if step <= DIMS:
            tiny_copy(step).start()

    def forward_all():
        prepare()
        lax.fori_loop(0, ROWS // BLOCK, attention_forward, 0)
        front_forward()
        lax.fori_loop(0, EXPERTS, expert_forward, 0)
        tower_both()
        d_normed[...] = jnp.zeros_like(d_normed)
        d_mixing[...] = jnp.zeros_like(d_mixing)
        lax.fori_loop(0, EXPERTS, spread_residual, 0)
        pl.semaphore_wait(barrier, 7)

    def family(i, first=0, to_other=False):
        out = (big_out, proj_out, small_out)[i]
        return Family(FAMILIES[i][3], out, family_refs[7 * i : 7 * i + 7], first, to_other)

    def perform(plan, big, extra):
        def backs(start, end):
            lax.fori_loop(start, end, expert_backward, 0)

        def outs(start, end):
            @pl.loop(start, end + 1)
            def _(e):
                @pl.when(e < end)
                def _():
                    big.send(e, 2 * e, out_halves(e, 1 - core))

                @pl.when(e > start)
                def _():
                    big.take(e - 1, 2 * e - 2, out_halves(e - 1, core))

        def ins(start, end):
            @pl.loop(start, end + 1)
            def _(e):
                @pl.when(e < end)
                def _():
                    expert_backward(e, 0)
                    big.send(6 + e, IN_UNIT + 2 * e, in_halves(e, 1 - core))

                @pl.when(e > start)
                def _():
                    big.take(5 + e, IN_UNIT + 2 * e - 2, in_halves(e - 1, core))

        def tower():
            big.send(12, TOWER_UNIT, tower_halves(1 - core))
            big.take(12, TOWER_UNIT, tower_halves(core))

        work = {
            "outs": outs,
            "ins": ins,
            "tower": tower,
            "back": backs,
            "front": front_backward,
            "sum": lambda c, step: big.reduce(DIMS * c, DIMS, step),
            "all": lambda c, step: big.gather(DIMS * c, DIMS, step),
            **extra,
        }
        for name, *where in plan:
            work[name](*where)

    forward_all()

    @pl.when(section == 0)
    def _():
        big = family(0, SPLIT, True)
        proj = family(1)
        perform(
            PLAN_FIRST,
            big,
            {
                "seq": lambda start, end: pl.loop(start, end)(attention_back),
                "weights": attention_weights,
                "send_p": lambda: proj.send(0, 0, proj_half(1 - core)),
                "take_p": lambda: proj.take(0, 0, proj_half(core)),
                "sum_p": lambda step: proj.reduce(0, DIMS, step),
                "all_p": lambda step: proj.gather(0, DIMS, step),
                "tiny": tiny_step,
            },
        )
        big.drain(FAMILIES[0][0] - SPLIT, 0)
        proj.drain(DIMS, DIMS)
        for step in range(DIMS + 1):
            tiny_copy(step).wait_send()
        tiny_out[...] = tiny[DIMS + 1]

    @pl.when(section == 1)
    def _():
        big = family(0)
        vectors = family(2)
        perform(
            PLAN_SECOND,
            big,
            {
                "send_v": lambda: vectors.send(0, 0, small_half(1 - core)),
                "take_v": lambda: vectors.take(0, 0, small_half(core)),
                "sum_v": lambda step: vectors.reduce(0, 1, step),
                "all_v": lambda step: vectors.gather(0, 1, step),
            },
        )
        big.drain(SPLIT, FAMILIES[0][0])
        vectors.drain(1, 1)


def run(*args):
    here = pl.BlockSpec(memory_space=pltpu.VMEM)
    far = pl.BlockSpec(memory_space=pl.ANY)

    def keep(*shape, dtype=F32):
        return pltpu.VMEM(shape, dtype)

    scratch = [
        keep(ROWS, SEQ, dtype=BF16),
        keep(EXPERTS, HIDDEN, WIDE, dtype=BF16),
        keep(EXPERTS, WIDE, HIDDEN, dtype=BF16),
        keep(SPAN, SPAN, dtype=BF16),
        keep(EMBED, SPAN),
        keep(SPAN, LANES),
        keep(SPAN, LANES),
        keep(EMBED, SPAN),
        keep(SPAN, LANES),
        keep(FIELDS, HIDDEN, dtype=BF16),
        keep(16, HIDDEN, dtype=BF16),
        keep(ROWS, 8),
        keep(ROWS, FIELDS, dtype=BF16),
        keep(ROWS, HIDDEN),
        keep(ROWS, HIDDEN),
        keep(ROWS, HIDDEN, dtype=BF16),
        keep(ROWS, HIDDEN),
        keep(EXPERTS, ROWS, WIDE, dtype=BF16),
        keep(EXPERTS, ROWS, WIDE, dtype=BF16),
        keep(EXPERTS, ROWS, HIDDEN, dtype=BF16),
        keep(EXPERTS, ROWS, HIDDEN, dtype=BF16),
        keep(ROWS, HIDDEN),
        keep(ROWS, HIDDEN),
        keep(ROWS, 8),
        keep(ROWS, 8),
        keep(ROWS, 8),
        keep(ROWS, HIDDEN, dtype=BF16),
        keep(ROWS, HIDDEN, dtype=BF16),
        keep(ROWS, HIDDEN, dtype=BF16),
        keep(ROWS, LANES),
        keep(ROWS, LANES),
        keep(ROWS, LANES),
        keep(64, HIDDEN),
        keep(DIMS + 2, TINY_ROWS, LANES),
        keep(DIMS + 1, TINY_ROWS, LANES),
        pltpu.SemaphoreType.DMA((13,)),
        pltpu.SemaphoreType.DMA((DIMS + 1,)),
        pltpu.SemaphoreType.DMA((DIMS + 1,)),
    ]
    for family in FAMILIES:
        scratch += family_scratch(*family)
    outs = [pltpu.VMEM((units, 2, rows, LANES), dtype) for units, _, _, rows, dtype in FAMILIES]
    outs += [
        pltpu.VMEM((TINY_ROWS, LANES), F32),
        pltpu.VMEM((2, 8, LANES), F32),
        pltpu.VMEM((ROWS, FIELDS), F32),
        pltpu.VMEM((ROWS, SEQ), BF16),
    ]
    return pl.pallas_call(
        kernel,
        out_shape=outs,
        in_specs=[here] * 19 + [far] * 3,
        out_specs=[here] * 7,
        scratch_shapes=scratch,
        compiler_params=pltpu.CompilerParams(
            collective_id=0, has_side_effects=True, vmem_limit_bytes=46 << 20
        ),
        name="rank_and_sum",
    )(*args)


def place_kernel(
    big,
    proj_units,
    small,
    tiny,
    pred_all,
    field_rows,
    seq_rows,
    out_grad,
    in_grad,
    field_grad,
    seq_grad,
    proj,
    tower,
    predictions,
    b_proj,
    gain,
    shift,
    tower_b,
    tower_o,
    tower_e,
    roots,
    gate,
    in_b,
    out_b,
    query,
    key,
    value,
    out_stage,
    in_stage,
    seq_stage,
    field_stage,
    proj_stage,
    tower_stage,
    out_sem,
    in_sem,
    other_sem,
):
    section = lax.axis_index("section")
    second = (section == 1).astype(F32)

    def out_copy(e, slot):
        return pltpu.make_async_copy(out_stage.at[slot], out_grad.at[0, e], out_sem.at[e])

    def in_copy(e, slot):
        return pltpu.make_async_copy(in_stage.at[slot], in_grad.at[0, e], in_sem.at[e])

    stages = ((seq_stage, seq_grad), (field_stage, field_grad), (proj_stage, proj), (tower_stage, tower))
    others = [pltpu.make_async_copy(stage, grad.at[0], other_sem.at[i]) for i, (stage, grad) in enumerate(stages)]

    @pl.when(section == 0)
    def _():
        out_stage[0] = jnp.zeros((WIDE, HIDDEN), F32)
        in_stage[0] = jnp.zeros((HIDDEN, WIDE), F32)
        for e in range(EXPERTS):
            out_copy(e, 0).start()
            in_copy(e, 0).start()
        seq_stage[...] = seq_rows[...].astype(F32)
        others[0].start()
        field_stage[...] = field_rows[...]
        others[1].start()
        for core in range(2):
            flat = jnp.concatenate([proj_units[i, core].astype(F32) for i in range(DIMS)], axis=0)
            for j in range(2):
                at = slice((2 * core + j) * LANES, (2 * core + j + 1) * LANES)
                proj_stage[:, at] = flat[j * FIELDS : (j + 1) * FIELDS]
        others[2].start()
        tower_stage[...] = jnp.zeros_like(tower_stage)
        others[3].start()
        for e in range(EXPERTS):
            out_copy(e, 0).wait()
            in_copy(e, 0).wait()

    @pl.when(section == 1)
    def _():
        @pl.loop(0, EXPERTS)
        def _(e):
            slot = e % 2

            @pl.when(e > 1)
            def _():
                out_copy(e - 2, slot).wait()

            for core in range(2):
                for j in range(2):
                    at = (2 * core + j) * LANES
                    out_stage[slot, :, at : at + LANES] = big[2 * e + j, core].astype(F32)
            out_copy(e, slot).start()

            @pl.when(e > 1)
            def _():
                in_copy(e - 2, slot).wait()

            for core in range(2):
                for j in range(2):
                    for i in range(2):
                        at = (4 * core + 2 * j + i) * LANES
                        rows = slice(i * HIDDEN, (i + 1) * HIDDEN)
                        in_stage[slot, :, at : at + LANES] = big[IN_UNIT + 2 * e + j, core, rows].astype(F32)
            in_copy(e, slot).start()

        for core in range(2):
            for j in range(2):
                at = slice((2 * core + j) * LANES, (2 * core + j + 1) * LANES)
                tower_stage[:, at] = big[TOWER_UNIT, core, j * HIDDEN : (j + 1) * HIDDEN].astype(F32)
        seq_stage[...] = jnp.zeros_like(seq_stage)
        field_stage[...] = jnp.zeros_like(field_stage)
        proj_stage[...] = jnp.zeros_like(proj_stage)
        for other in others:
            other.start()
        for e in (EXPERTS - 2, EXPERTS - 1):
            out_copy(e, e % 2).wait()
            in_copy(e, e % 2).wait()

    for j in range(2):
        predictions[:, j * LANES : (j + 1) * LANES] = jnp.where(section == 1, pred_all[j, 0:1], 0.0)

    def rows(start, count):
        found = jnp.concatenate(
            [small[0, core, j * 64 + start : j * 64 + start + count] for core in range(2) for j in range(2)],
            axis=1,
        )
        return jnp.where(section == 1, found, 0.0)

    head = rows(0, 8)
    gain[...] = head[1:2]
    shift[...] = head[2:3]
    tower_b[...] = head[3:4]
    tower_o[...] = head[4:5]
    tower_e[...] = head[5:6, 0:2]
    count = head[5:6, 4:5]
    squares = head[5:6, 2:4] / (float(HIDDEN) * jnp.maximum(count, 1.0)) + EPSILON
    roots[...] = jnp.where(count > 0.0, jnp.sqrt(squares), 0.0) * second
    gate_lines, out_lines = rows(8, 8), rows(32, 8)
    in_lines = jnp.concatenate([rows(16, 8), rows(24, 8)], axis=1)
    for i in range(7):
        gate[i] = gate_lines[i : i + 1]
    for e in range(EXPERTS):
        in_b[e] = in_lines[e : e + 1]
        out_b[e] = out_lines[e : e + 1]
    three = jnp.where(section == 0, tiny[...], 0.0)
    b_proj[...] = jnp.concatenate([three[16 + i : 17 + i] for i in range(4)], axis=1)
    query[0] = three[:EMBED, 0:16]
    key[0] = three[:EMBED, 16:32]
    value[0] = three[:EMBED, 32:48]
    for other in others:
        other.wait()


def place(*results):
    here = pl.BlockSpec(memory_space=pltpu.VMEM)
    far = pl.BlockSpec(memory_space=pl.ANY)
    shapes = [(1, 6, 1024, 512), (1, 6, 512, 1024), (1, ROWS, FIELDS), (1, ROWS, SEQ), (1, 640, 512), (1, 512, 512)]
    shapes += [(1, ROWS)] + [(1, 512)] * 5 + [(1, 2)] * 2
    shapes += [(7, 1, 512), (6, 1, 1024), (6, 1, 512)] + [(1, 16, 16)] * 3
    return pl.pallas_call(
        place_kernel,
        out_shape=[jax.ShapeDtypeStruct(shape, F32) for shape in shapes],
        in_specs=[here] * 7,
        out_specs=[far] * 6 + [here] * 14,
        scratch_shapes=[
            pltpu.VMEM((2, WIDE, HIDDEN), F32),
            pltpu.VMEM((2, HIDDEN, WIDE), F32),
            pltpu.VMEM((ROWS, SEQ), F32),
            pltpu.VMEM((ROWS, FIELDS), F32),
            pltpu.VMEM((FIELDS, HIDDEN), F32),
            pltpu.VMEM((HIDDEN, HIDDEN), F32),
            pltpu.SemaphoreType.DMA((EXPERTS,)),
            pltpu.SemaphoreType.DMA((EXPERTS,)),
            pltpu.SemaphoreType.DMA((4,)),
        ],
        compiler_params=pltpu.CompilerParams(vmem_limit_bytes=24 << 20),
        name="place",
    )(*(pltpu.with_memory_space_constraint(result, pltpu.VMEM) for result in results))


def body(
    fields,
    behaviour,
    lengths,
    domains,
    validity,
    cotangent,
    w_query,
    w_key,
    w_value,
    w_proj,
    b_proj,
    norm_gain,
    norm_shift,
    gate_weight,
    w_in,
    b_in,
    w_out,
    b_out,
    tower_in,
    tower_bias,
    tower_out,
    tower_end,
):
    def line(array):
        return array.reshape(1, -1)

    results = run(
        fields,
        line(lengths),
        line(domains),
        line(validity),
        line(cotangent),
        w_query,
        w_key,
        w_value,
        w_proj,
        line(b_proj),
        line(norm_gain),
        line(norm_shift),
        gate_weight.T,
        b_in,
        b_out,
        tower_in,
        line(tower_bias),
        line(tower_out),
        line(tower_end),
        behaviour,
        w_in,
        w_out,
    )
    (
        out_grad,
        in_grad,
        field_grad,
        seq_grad,
        proj,
        tower,
        predictions,
        b_proj_grad,
        gain,
        shift,
        tower_b,
        tower_o,
        tower_e,
        roots,
        gate,
        in_b,
        out_b,
        query,
        key,
        value,
    ) = place(*results)
    return (
        predictions,
        field_grad,
        seq_grad,
        query,
        key,
        value,
        proj,
        b_proj_grad,
        gain,
        shift,
        gate.transpose(1, 2, 0),
        in_grad,
        in_b.transpose(1, 0, 2),
        out_grad,
        out_b.transpose(1, 0, 2),
        tower,
        tower_b,
        tower_o,
        tower_e,
        roots,
    )


def solution(mesh):
    each = (P("dp", None), P("dp", None), P("dp"), P("dp"), P("dp"), P("dp"))
    ranks = (2, 3, 3, 3, 3, 3, 3, 2, 2, 2, 3, 4, 3, 4, 3, 3, 2, 2, 2, 2)
    outs = tuple(
        P("section", "dp", *(None,) * (rank - 2)) if i < 3 else P("section", *(None,) * (rank - 1))
        for i, rank in enumerate(ranks)
    )
    return jax.shard_map(
        body, mesh=mesh, in_specs=each + (P(),) * 16, out_specs=outs, check_vma=False
    )
```

```python
import jax
import jax.numpy as jnp
from jax import lax
from jax.experimental import pallas as pl
from jax.experimental.pallas import tpu as pltpu
from jax.sharding import PartitionSpec as P

EPSILON = 1e-05
MESH = pl.DeviceIdType.MESH
F32 = jnp.float32
BF16 = jnp.bfloat16

LANES = 128
DIMS = 5
HALVINGS = 3
SLOTS = 7 + HALVINGS
ROWS = 256
EXPERTS = 6
HIDDEN = 512
WIDE = 1024
FIELDS = 640
EMBED = 16
SEQ = 3200
SPAN = 256
PIECES = tuple((at, SPAN) for at in range(0, 3072, SPAN)) + ((3072, LANES),)
PROJ_ROWS = 256
SMALL_ROWS = 128
BLOCK = 128
BACK_BLOCK = 64


def coords():
    section, place = lax.axis_index("section"), lax.axis_index("dp")
    return 2 * section + place // 32, (place // 8) % 4, (place // 2) % 4, place % 2


def device_at(z, x, y, core):
    return {"section": z // 2, "dp": (((z % 2) * 4 + x) * 4 + y) * 2 + core}


def hop(r, kind):
    near, far = 1 - 2 * (r % 2), 3 - 2 * r
    return near + kind * (far - near)


def side(r, kind):
    near = (r + r // 2) % 2
    return near + kind * (r // 2 - near)


def picks(dim):
    a = dim % 3
    return (1 - a) * (2 - a) // 2, a * (2 - a), a * (a - 1) // 2, dim // 3


def neighbour(dim):
    z, x, y, core = coords()
    ex, ey, ez, kind = picks(dim)
    return device_at(z + ez * hop(z, kind), x + ex * hop(x, kind), y + ey * hop(y, kind), core)


def which_half(dim):
    z, x, y, core = coords()
    ex, ey, ez, kind = picks(dim)
    return ex * side(x, kind) + ey * side(y, kind) + ez * side(z, kind)


def sibling():
    z, x, y, core = coords()
    return device_at(z, x, y, 1 - core)


def cross():
    z, x, y, core = coords()
    return device_at(3 - z, x, y, core)


class Family:
    def __init__(self, rows, out, refs, first, to_other=False):
        self.rows = rows
        self.share = rows >> HALVINGS
        self.out = out
        self.first = first
        self.to_other = to_other
        (
            self.kept,
            self.arrived,
            self.doubled,
            self.pair_send,
            self.pair_recv,
            self.send_sem,
            self.recv_sem,
        ) = refs

    def total(self, units, rows=slice(None)):
        return self.out.at[units, coords()[3], rows]

    def remote(self, unit, slot, src, dst, to):
        return pltpu.make_async_remote_copy(
            src_ref=src,
            dst_ref=dst,
            send_sem=self.send_sem.at[slot],
            recv_sem=self.recv_sem.at[unit // DIMS, slot],
            device_id=to,
            device_id_type=MESH,
        )

    def start_of(self, part, step):
        start = 0
        for k in range(step):
            start = start + which_half((part + k) % DIMS) * (self.rows >> (k + 1))
        return start

    def span(self, start, size):
        return pl.ds(pl.multiple_of(start, size), size)

    def own_share(self, unit):
        return self.span(self.start_of(unit % DIMS, HALVINGS), self.share)

    def across(self, group, unit, count):
        return pltpu.make_async_remote_copy(
            src_ref=self.total(pl.ds(unit, count)),
            dst_ref=self.kept.at[pl.ds(unit - self.first, count)],
            send_sem=self.pair_send.at[group],
            recv_sem=self.pair_recv.at[group],
            device_id=sibling(),
            device_id_type=MESH,
        )

    def halve(self, unit, k):
        size = self.rows >> (k + 1)
        dim = (unit + k) % DIMS
        start = self.start_of(unit % DIMS, k) + (1 - which_half(dim)) * size
        local = unit - self.first
        return self.remote(
            unit,
            k,
            self.kept.at[local, self.span(start, size)],
            self.arrived.at[local, pl.ds(self.rows - 2 * size, size)],
            neighbour(dim),
        )

    def double(self, unit, j):
        local = unit - self.first
        src = self.kept.at[local, self.own_share(unit)] if j == 0 else self.doubled.at[local, j - 1]
        return self.remote(
            unit,
            HALVINGS + j,
            src,
            self.arrived.at[local, pl.ds(self.rows - self.share + j * self.share, self.share)],
            neighbour((unit + HALVINGS + j) % DIMS),
        )

    def over(self, unit):
        region = self.total(unit, self.own_share(unit))
        return self.remote(unit, DIMS, region, region, cross())

    def spread(self, unit, k):
        size = self.rows >> (k + 1)
        region = self.total(unit, self.span(self.start_of(unit % DIMS, k + 1), size))
        return self.remote(unit, DIMS + 1 + k, region, region, neighbour((unit + k) % DIMS))

    def back(self, unit, late):
        size = self.rows // 2
        own = which_half(unit % DIMS)
        region = self.total(unit, self.span((own + late * (1 - 2 * own)) * size, size))
        return self.remote(unit, DIMS + 1 + HALVINGS, region, region, sibling())

    def send(self, group, unit, halves):
        for i, rows in enumerate(halves):
            self.out[unit + i, coords()[3]] = rows.astype(self.out.dtype)
        self.across(group, unit, len(halves)).start()

    def take(self, group, unit, halves):
        pair = self.across(group, unit, len(halves))
        pair.wait_send()
        pair.wait_recv()
        for i, rows in enumerate(halves):
            local = unit + i - self.first
            self.kept[local] = (rows + self.kept[local].astype(F32)).astype(self.kept.dtype)
            self.halve(unit + i, 0).start()

    def await_chunk(self, slot, base, ref):
        pltpu.make_async_copy(ref, ref, self.recv_sem.at[base // DIMS, slot]).wait()

    def each(self, base, count, work):
        def one(i, _):
            work(base + i)
            return 0

        lax.fori_loop(0, count, one, 0)

    def reduce(self, base, count, step):
        dtype = self.kept.dtype
        local = pl.ds(base - self.first, count)
        if step < HALVINGS:
            size = self.rows >> (step + 1)
            arrivals = pl.ds(self.rows - 2 * size, size)
        else:
            size = self.share
            arrivals = pl.ds(self.rows - size + (step - HALVINGS) * size, size)
        self.await_chunk(step, base, self.arrived.at[local, arrivals])

        def one(unit):
            here = unit - self.first
            came = self.arrived[here, arrivals].astype(F32)
            if step < HALVINGS:
                region = self.span(self.start_of(unit % DIMS, step + 1), size)
                self.kept[here, region] = (self.kept[here, region].astype(F32) + came).astype(dtype)
                if step + 1 < HALVINGS:
                    self.halve(unit, step + 1).start()
                else:
                    self.double(unit, 0).start()
                return
            j = step - HALVINGS
            region = self.own_share(unit)
            old = self.kept[here, region] if j == 0 else self.doubled[here, j - 1]
            new = (old.astype(F32) + came).astype(dtype)
            if step + 1 < DIMS:
                self.doubled[here, j] = new
                self.double(unit, j + 1).start()
            else:
                self.out[unit, coords()[3], region] = new
                if self.to_other:
                    self.over(unit).start()
                else:
                    self.spread(unit, HALVINGS - 1).start()

        self.each(base, count, one)

    def gather(self, base, count, step):
        units = pl.ds(base, count)
        if step == 0:
            self.await_chunk(DIMS, base, self.total(units, pl.ds(0, self.share)))
            self.each(base, count, lambda unit: self.spread(unit, HALVINGS - 1).start())
        elif step <= HALVINGS:
            k = HALVINGS - step
            self.await_chunk(DIMS + 1 + k, base, self.total(units, pl.ds(0, self.rows >> (k + 1))))

            def one(unit):
                if k > 0:
                    self.spread(unit, k - 1).start()
                if k < 2:
                    self.back(unit, 1 - k).start()

            self.each(base, count, one)
        else:
            self.await_chunk(DIMS + 1 + HALVINGS, base, self.out.at[units, 1 - coords()[3]])

    def drain(self, reduced, gathered):
        def sent(slot, ref):
            pltpu.make_async_copy(ref, ref, self.send_sem.at[slot]).wait()

        for step in range(DIMS):
            size = self.rows >> (step + 1) if step < HALVINGS else self.share
            sent(step, self.kept.at[pl.ds(0, reduced), pl.ds(0, size)])
        if self.to_other:
            sent(DIMS, self.kept.at[pl.ds(0, reduced), pl.ds(0, self.share)])
        if gathered:
            for k in range(HALVINGS):
                sent(DIMS + 1 + k, self.total(pl.ds(0, gathered), pl.ds(0, self.rows >> (k + 1))))
            sent(DIMS + 1 + HALVINGS, self.total(pl.ds(0, gathered)))


def family_scratch(units, reduced, groups, rows, dtype):
    share = rows >> HALVINGS
    chunks = pl.cdiv(units, DIMS)
    return [
        pltpu.VMEM((reduced, rows, LANES), dtype),
        pltpu.VMEM((reduced, rows - share + (DIMS - HALVINGS) * share, LANES), dtype),
        pltpu.VMEM((reduced, max(1, DIMS - HALVINGS - 1), share, LANES), dtype),
        pltpu.SemaphoreType.DMA((groups,)),
        pltpu.SemaphoreType.DMA((groups,)),
        pltpu.SemaphoreType.DMA((SLOTS,)),
        pltpu.SemaphoreType.DMA((chunks, SLOTS)),
    ]


FAMILIES = ((25, 15, 13, 1024, BF16), (DIMS, DIMS, 1, PROJ_ROWS, BF16), (1, 1, 1, SMALL_ROWS, F32))
TOWER_UNIT = 12
IN_UNIT = 13
SPLIT = 15
TINY_ROWS = 24


PLAN_FIRST = (
    ("ins", 1, 6), ("back", 0, 1), ("front",), ("sum", 3, 0), ("sum", 4, 0), ("send_p",), ("sum", 3, 1), ("take_p",),
    ("sum", 4, 1), ("sum", 3, 2), ("sum", 4, 2), ("sum", 3, 3), ("sum_p", 0), ("sum", 3, 4), ("sum", 4, 3),
    ("sum_p", 1), ("seq", 0, 1), ("sum", 4, 4), ("sum_p", 2), ("seq", 1, 2), ("weights",), ("tiny", 0), ("sum_p", 3),
    ("sum_p", 4), ("tiny", 1), ("tiny", 2), ("all_p", 1), ("tiny", 3), ("all_p", 2), ("tiny", 4), ("all_p", 3),
    ("tiny", 5), ("all_p", 4), ("tiny", 6),
)
PLAN_SECOND = (
    ("outs", 0, 6), ("send_t", 0), ("back", 0, 1), ("send_i", 0), ("sum", 0, 0), ("take_t", 0), ("take_i", 0),
    ("sum", 1, 0), ("back", 3, 6), ("sum", 0, 1), ("back", 1, 3), ("sum", 1, 1), ("sum", 2, 0), ("sum", 0, 2),
    ("front",), ("sum", 1, 2), ("send_v",), ("sum", 2, 1), ("sum", 0, 3), ("take_v",), ("sum", 1, 3), ("sum", 2, 2),
    ("sum", 0, 4), ("sum_v", 0), ("sum", 1, 4), ("sum", 2, 3), ("sum_v", 1), ("all", 0, 1), ("all", 1, 1),
    ("sum", 2, 4), ("sum_v", 2), ("all", 3, 0), ("all", 0, 2), ("all", 3, 1), ("sum_v", 3), ("all", 4, 0),
    ("all", 2, 1), ("all", 1, 2), ("sum_v", 4), ("all", 4, 1), ("all", 2, 2), ("all_v", 1), ("all", 4, 2),
    ("all_v", 2), ("all", 1, 3), ("all", 3, 2), ("all", 0, 3), ("all_v", 3), ("all", 4, 3), ("all_v", 4),
    ("all", 2, 3), ("all", 1, 4), ("all", 3, 3), ("all", 0, 4), ("all", 2, 4), ("all", 4, 4), ("all", 3, 4),
)


def exact(left, right):
    return jnp.dot(left, right, precision=lax.Precision.HIGHEST, preferred_element_type=F32)


def exact_cols(left, right):
    return lax.dot_general(
        left, right, (((1,), (1,)), ((), ())), precision=lax.Precision.HIGHEST, preferred_element_type=F32
    )


def exact_rows(left, right):
    return lax.dot_general(
        left, right, (((0,), (0,)), ((), ())), precision=lax.Precision.HIGHEST, preferred_element_type=F32
    )


def product(left, right):
    return jnp.dot(left, right, preferred_element_type=F32)


def contract_rows(left, right):
    return lax.dot_general(left, right, (((0,), (0,)), ((), ())), preferred_element_type=F32)


def contract_cols(left, right):
    return lax.dot_general(left, right, (((1,), (1,)), ((), ())), preferred_element_type=F32)


def split(value, terms):
    out = []
    for _ in range(terms):
        out.append(value.astype(BF16))
        value = value - out[-1].astype(F32)
    return out


def sigmoid(v):
    return 1.0 / (1.0 + jnp.exp(-v))


ROOT = 0.7978845608028654
CUBE = 0.044715


def gelu_both(v):
    square = v * v
    bent = jnp.tanh(v * (ROOT + ROOT * CUBE * square))
    half = 0.5 + 0.5 * bent
    value = v * half
    slope = half + value * (1.0 - half) * (2.0 * ROOT + 6.0 * ROOT * CUBE * square)
    return value, slope


def column_sum(array):
    return jnp.sum(array, axis=0, keepdims=True)


def row_sum(array):
    return jnp.sum(array, axis=1, keepdims=True)


def lanes(shape):
    return lax.broadcasted_iota(jnp.int32, shape, 1)


def lane_match(rows, columns, period, shift=0):
    place = lax.broadcasted_iota(jnp.int32, (rows, columns), 1) - shift
    if period:
        place = place % period
    return (place == lax.broadcasted_iota(jnp.int32, (rows, columns), 0)).astype(F32)


def kernel(
    fields,
    lengths,
    domains,
    validity,
    cotangent,
    w_query,
    w_key,
    w_value,
    w_proj,
    b_proj,
    norm_gain,
    norm_shift,
    gate_turned,
    b_in,
    b_out,
    tower_in,
    tower_bias,
    tower_out,
    tower_end,
    behaviour_hbm,
    w_in_hbm,
    w_out_hbm,
    big_out,
    proj_out,
    small_out,
    tiny_out,
    pred_all,
    d_fields,
    d_seq,
    behaviour,
    w_in,
    w_out,
    groups,
    probe_w,
    value_w,
    pooled_w,
    back_w,
    target_w,
    proj_turned,
    gate_rows,
    info,
    joined,
    activation,
    proj_slope,
    normed,
    standard,
    active,
    slope,
    expert,
    d_expert,
    d_normed,
    d_residual,
    mixing,
    d_mixing,
    gates,
    residual_low,
    d_tower,
    d_proj_low,
    pooled_rows,
    d_value_rows,
    d_probe_rows,
    small,
    tiny,
    tiny_arrived,
    load_sem,
    tiny_send,
    tiny_recv,
    *family_refs,
):
    section = lax.axis_index("section")
    core = coords()[3]

    barrier = pltpu.get_barrier_semaphore()
    for dim in range(DIMS):
        pl.semaphore_signal(barrier, inc=1, device_id=neighbour(dim), device_id_type=MESH)
    for other in (sibling(), cross()):
        pl.semaphore_signal(barrier, inc=1, device_id=other, device_id_type=MESH)

    seq_copy = pltpu.make_async_copy(behaviour_hbm, behaviour, load_sem.at[12])

    def load_in(e):
        return pltpu.make_async_copy(w_in_hbm.at[e], w_in.at[e], load_sem.at[e])

    def load_out(e):
        return pltpu.make_async_copy(w_out_hbm.at[e], w_out.at[e], load_sem.at[6 + e])

    tile = lane_match(EMBED, SPAN, EMBED)

    def prepare():
        seq_copy.start()
        for e in range(EXPERTS):
            load_in(e).start()
            load_out(e).start()
        group = lax.broadcasted_iota(jnp.int32, (SPAN, SPAN), 0) // EMBED
        groups[...] = (group == lanes((SPAN, SPAN)) // EMBED).astype(F32).astype(BF16)
        eye = lane_match(EMBED, LANES, 0)
        probe_w[...] = exact(w_query[...], exact_rows(w_key[...], tile))
        value_w[...] = exact_rows(tile, exact(w_value[...], eye))
        pooled_w[...] = exact_rows(tile, eye)
        back_w[...] = exact_rows(w_value[...], tile)
        target_w[...] = exact_rows(tile, exact(exact_cols(w_key[...], w_query[...]), eye))
        proj_turned[:EMBED] = w_proj[FIELDS - EMBED :]
        proj_turned[EMBED:] = w_proj[: FIELDS - EMBED]
        rows = [lengths[...].astype(F32), domains[...].astype(F32), validity[...].astype(F32), cotangent[...]]
        info[...] = jnp.transpose(jnp.concatenate(rows + [jnp.zeros((4, ROWS), F32)], axis=0))
        gate_rows[...] = jnp.zeros_like(gate_rows)
        gate_rows[:7] = gate_turned[...]
        small[...] = jnp.zeros_like(small)
        tiny[0] = jnp.zeros((TINY_ROWS, LANES), F32)
        seq_copy.wait()

    def group_sum(value, terms):
        count, width = value.shape
        stacked = jnp.concatenate(split(value, terms), axis=0)
        sums = product(stacked, groups[:width, :width])
        return sum(sums[i * count : (i + 1) * count] for i in range(terms))

    def narrow_sum(pieces):
        wide = sum(pieces[:-1])
        return jnp.concatenate([wide[:, :LANES] + pieces[-1], wide[:, LANES:]], axis=1)

    def stretch(rows, at, width):
        return behaviour[rows, at : at + width].astype(F32)

    def attention(rows):
        target = fields[rows, 0:LANES].astype(F32)[:, :EMBED]
        probe = exact(target, probe_w[...])
        length = info[rows, 0:1]
        scores = []
        for at, width in PIECES:
            sums = group_sum(stretch(rows, at, width) * probe[:, :width], 3)
            place = ((lanes((1, width)) + at) // EMBED).astype(F32)
            scores.append(jnp.where(place < length, 0.5 * sums, -1e30))
        peak = scores[0]
        for piece in scores[1:-1]:
            peak = jnp.maximum(peak, piece)
        peak = jnp.maximum(jnp.max(peak, axis=1, keepdims=True), jnp.max(scores[-1], axis=1, keepdims=True))
        raised = [jnp.exp(piece - peak) for piece in scores]
        scale = float(EMBED) / row_sum(narrow_sum(raised))
        return probe, [piece * scale for piece in raised]

    def pool(rows, attn):
        return narrow_sum([w * stretch(rows, at, width) for w, (at, width) in zip(attn, PIECES)])

    def attention_forward(block, _):
        rows = pl.ds(pl.multiple_of(block * BLOCK, BLOCK), BLOCK)
        _, attn = attention(rows)
        value = exact(pool(rows, attn), value_w[...])
        joined[rows, LANES:] = fields[rows, LANES:]
        head = fields[rows, :LANES]
        joined[rows, :LANES] = jnp.where(lanes(head.shape) < EMBED, value.astype(BF16), head)
        return 0

    def gate_columns():
        return [gates[:, i : i + 1] for i in range(6)]

    def front_forward():
        projected = product(joined[...], proj_turned[...]) + b_proj[...]
        act, slope_proj = gelu_both(projected)
        activation[...] = act.astype(BF16)
        act = act.astype(BF16).astype(F32)
        proj_slope[...] = slope_proj
        centred = act - row_sum(act) * (1.0 / HIDDEN)
        scale = lax.rsqrt(row_sum(centred * centred) * (1.0 / HIDDEN) + EPSILON)
        standard[...] = centred * scale
        normed[...] = (centred * scale * norm_gain[...] + norm_shift[...]).astype(BF16)

        logits = contract_cols(normed[...], gate_rows[...])
        in_first = info[:, 1:2] == 0.0
        level = sigmoid(logits[:, 6:7])
        shared_a = sigmoid(logits[:, 0:1] - logits[:, 1:2])
        shared_b = sigmoid(logits[:, 1:2] - logits[:, 0:1])
        lead = jnp.where(in_first, logits[:, 2:3] - logits[:, 3:4], logits[:, 4:5] - logits[:, 5:6])
        chosen_a, chosen_b = sigmoid(lead), sigmoid(-lead)
        zero = jnp.zeros_like(level)
        columns = [
            level * shared_a,
            level * shared_b,
            jnp.where(in_first, (1.0 - level) * chosen_a, zero),
            jnp.where(in_first, (1.0 - level) * chosen_b, zero),
            jnp.where(in_first, zero, (1.0 - level) * chosen_a),
            jnp.where(in_first, zero, (1.0 - level) * chosen_b),
        ]
        place = lanes((ROWS, 8))
        mixing[...] = sum(jnp.where(place == i, column, 0.0) for i, column in enumerate(columns))
        held = (scale, level, shared_a, shared_b, chosen_a, chosen_b)
        gates[...] = sum(jnp.where(place == i, column, 0.0) for i, column in enumerate(held))
        d_residual[...] = jnp.zeros_like(d_residual)

    def expert_forward(e, _):
        pre = product(normed[...], w_in[e]) + b_in[pl.ds(e, 1)]
        out, grade = gelu_both(pre)
        active[e] = out.astype(BF16)
        slope[e] = grade.astype(BF16)
        rows = product(active[e], w_out[e]) + b_out[pl.ds(e, 1)]
        expert[e] = rows.astype(BF16)
        weight = row_sum(jnp.where(lanes((ROWS, 8)) == e, mixing[...], 0.0))
        d_residual[...] += weight * rows
        return 0

    def tower_both():
        branch = d_residual[...]
        residual = activation[...].astype(F32) + branch
        in_first = info[:, 1:2] == 0.0
        valid = info[:, 2:3]
        residual_low[...] = residual.astype(BF16)
        tower_act, tower_slope = gelu_both(product(residual_low[...], tower_in[...]) + tower_bias[...])
        chosen = jnp.where(in_first, 0, 1) == lanes((ROWS, HIDDEN)) // 256
        ends = tower_end[...]
        end = jnp.where(in_first, ends[:, 0:1], ends[:, 1:2])
        predict = sigmoid(row_sum(jnp.where(chosen, tower_act * tower_out[...], 0.0)) + end)
        d_logit = info[:, 3:4] * valid * predict * (1.0 - predict)
        spread_logit = jnp.where(chosen, d_logit, 0.0)
        d_tower[...] = (spread_logit * tower_out[...] * tower_slope).astype(BF16)
        small[3:4] = column_sum(d_tower[...].astype(F32))
        small[4:5] = column_sum(tower_act * spread_logit)
        spots = lanes((1, HIDDEN))
        parts = (
            column_sum(jnp.where(in_first, d_logit, 0.0)),
            column_sum(jnp.where(in_first, 0.0, d_logit)),
            column_sum(valid * row_sum(residual * residual)),
            column_sum(valid * row_sum(branch * branch)),
            column_sum(valid),
        )
        small[5:6] = sum(jnp.where(spots == i, part, 0.0) for i, part in enumerate(parts))
        wide = jnp.transpose(jnp.broadcast_to(predict, (ROWS, LANES)))
        pred_all[0] = wide[:8, :LANES]
        pred_all[1] = wide[:8, LANES:]
        d_residual[...] = contract_cols(d_tower[...], tower_in[...])

    def spread_residual(e, _):
        weight = row_sum(jnp.where(lanes((ROWS, 8)) == e, mixing[...], 0.0))
        low = (weight * d_residual[...]).astype(BF16)
        d_expert[e] = low
        small[pl.ds(32 + e, 1)] = column_sum(low.astype(F32))
        inner = row_sum(expert[e].astype(F32) * d_residual[...])
        d_mixing[...] = jnp.where(lanes((ROWS, 8)) == e, inner, d_mixing[...])
        return 0

    def expert_backward(e, _):
        grade = contract_cols(d_expert[e], w_out[e]) * slope[e].astype(F32)
        low = grade.astype(BF16)
        slope[e] = low
        sums = column_sum(low.astype(F32))
        small[pl.ds(16 + e, 1)] = sums[:, :512]
        small[pl.ds(24 + e, 1)] = sums[:, 512:]
        d_normed[...] += contract_cols(low, w_in[e])
        return 0

    def front_backward():
        scale, level, shared_a, shared_b, chosen_a, chosen_b = gate_columns()
        in_first = info[:, 1:2] == 0.0
        grads = [d_mixing[:, e : e + 1] for e in range(EXPERTS)]
        grad_a = jnp.where(in_first, grads[2], grads[4])
        grad_b = jnp.where(in_first, grads[3], grads[5])
        d_level = grads[0] * shared_a + grads[1] * shared_b - grad_a * chosen_a - grad_b * chosen_b
        d_shared = level * shared_a * shared_b * (grads[0] - grads[1])
        d_lead = (1.0 - level) * chosen_a * chosen_b * (grad_a - grad_b)
        zero = jnp.zeros_like(d_lead)
        d_first = jnp.where(in_first, d_lead, zero)
        d_second = jnp.where(in_first, zero, d_lead)
        columns = (d_shared, -d_shared, d_first, -d_first, d_second, -d_second, d_level * level * (1.0 - level))
        place = lanes((ROWS, LANES))
        d_logits = sum(jnp.where(place == i, column, 0.0) for i, column in enumerate(columns)).astype(BF16)
        small[8:16] = jnp.transpose(contract_rows(normed[...], d_logits))[:8]
        total = d_normed[...] + product(d_logits[:, :16], gate_rows[...])
        std = standard[...]
        small[1:2] = column_sum(total * std)
        small[2:3] = column_sum(total)
        scaled = total * norm_gain[...]
        inner = scaled - row_sum(scaled) * (1.0 / HIDDEN) - std * (row_sum(scaled * std) * (1.0 / HIDDEN))
        d_act = (inner * scale + d_residual[...]).astype(BF16).astype(F32)
        low = (d_act * proj_slope[...]).astype(BF16)
        sums = column_sum(low.astype(F32))
        for i in range(HIDDEN // LANES):
            tiny[0, 16 + i : 17 + i] = sums[:, i * LANES : (i + 1) * LANES]
        d_proj_low[...] = low

    def attention_back(block):
        rows = pl.ds(pl.multiple_of(block * BACK_BLOCK, BACK_BLOCK), BACK_BLOCK)
        probe, attn = attention(rows)
        pooled_rows[rows] = exact(pool(rows, attn), pooled_w[...])
        d_joined = contract_cols(d_proj_low[rows], proj_turned[...])
        head = d_joined[:, :LANES]
        d_value_rows[rows] = head
        d_pooled = exact(head[:, :EMBED], back_w[...])
        d_attn = [group_sum(stretch(rows, at, width) * d_pooled[:, :width], 2) for at, width in PIECES]
        inner = row_sum(narrow_sum([a * d for a, d in zip(attn, d_attn)])) * (1.0 / EMBED)
        pieces = []
        for (at, width), a, d in zip(PIECES, attn, d_attn):
            grade = 0.5 * a * (d - inner)
            pieces.append(grade * stretch(rows, at, width))
            d_seq[rows, at : at + width] = (a * d_pooled[:, :width] + grade * probe[:, :width]).astype(BF16)
        wide = narrow_sum(pieces)
        d_probe_rows[rows] = exact(wide, pooled_w[...])
        d_target = exact(wide, target_w[...])
        d_fields[rows] = d_joined
        d_fields[rows, :LANES] = jnp.where(lanes(head.shape) < EMBED, d_target, head)

    def attention_weights():
        target = fields[:, 0:LANES].astype(F32)[:, :EMBED]
        d_probe = d_probe_rows[...][:, :EMBED]
        query_grad = exact_rows(target, exact(d_probe, w_key[...]))
        key_grad = exact_rows(d_probe, exact(target, w_query[...]))
        value_grad = exact_rows(pooled_rows[...][:, :EMBED], d_value_rows[...][:, :EMBED])
        grads = (query_grad, key_grad, value_grad)
        tiny[0, :EMBED] = sum(exact(g, lane_match(EMBED, LANES, 0, EMBED * i)) for i, g in enumerate(grads))

    def out_halves(e, half):
        grad = contract_rows(active[e], d_expert[e, :, pl.ds(pl.multiple_of(half * 256, 256), 256)])
        return [grad[:, :LANES], grad[:, LANES:]]

    def in_halves(e, half):
        grad = contract_rows(normed[...], slope[e, :, pl.ds(pl.multiple_of(half * 512, 512), 512)])
        columns = [grad[:, i * LANES : (i + 1) * LANES] for i in range(4)]
        return [jnp.concatenate(columns[:2], axis=0), jnp.concatenate(columns[2:], axis=0)]

    def tower_halves(half):
        grad = contract_rows(residual_low[...], d_tower[:, pl.ds(pl.multiple_of(half * 256, 256), 256)])
        return [jnp.concatenate([grad[:, :LANES], grad[:, LANES:]], axis=0)]

    def proj_half(half):
        grad = contract_rows(joined[...], d_proj_low[:, pl.ds(pl.multiple_of(half * 256, 256), 256)])
        columns = []
        for j in range(2):
            column = grad[:, j * LANES : (j + 1) * LANES]
            columns += [column[EMBED:], column[:EMBED]]
        flat = jnp.concatenate(columns, axis=0)
        return [flat[unit * PROJ_ROWS : (unit + 1) * PROJ_ROWS] for unit in range(DIMS)]

    def small_half(half):
        columns = [small[:, pl.ds(pl.multiple_of(half * 256 + j * LANES, LANES), LANES)] for j in range(2)]
        return [jnp.concatenate(columns, axis=0)]

    def tiny_copy(step):
        return pltpu.make_async_remote_copy(
            src_ref=tiny.at[step],
            dst_ref=tiny_arrived.at[step],
            send_sem=tiny_send.at[step],
            recv_sem=tiny_recv.at[step],
            device_id=sibling() if step == DIMS else neighbour(step),
            device_id_type=MESH,
        )

    def tiny_step(step):
        if step:
            tiny_copy(step - 1).wait_recv()
            tiny[step] = tiny[step - 1] + tiny_arrived[step - 1]
        if step <= DIMS:
            tiny_copy(step).start()

    def forward_all():
        prepare()
        lax.fori_loop(0, ROWS // BLOCK, attention_forward, 0)
        front_forward()
        for e in range(EXPERTS):
            load_in(e).wait()
            load_out(e).wait()

        @pl.loop(0, EXPERTS, step=2)
        def _(e):
            expert_forward(e, 0)
            expert_forward(e + 1, 0)

        tower_both()
        d_normed[...] = jnp.zeros_like(d_normed)
        d_mixing[...] = jnp.zeros_like(d_mixing)
        lax.fori_loop(0, EXPERTS, spread_residual, 0)
        pl.semaphore_wait(barrier, 7)

    def family(i, first=0, to_other=False):
        out = (big_out, proj_out, small_out)[i]
        return Family(FAMILIES[i][3], out, family_refs[7 * i : 7 * i + 7], first, to_other)

    def perform(plan, big, extra):
        def backs(start, end):
            lax.fori_loop(start, end, expert_backward, 0)

        def outs(start, end):
            @pl.loop(start, end + 1)
            def _(e):
                @pl.when(e < end)
                def _():
                    big.send(e, 2 * e, out_halves(e, 1 - core))

                @pl.when(e > start)
                def _():
                    big.take(e - 1, 2 * e - 2, out_halves(e - 1, core))

        def ins(start, end):
            @pl.loop(start, end + 1)
            def _(e):
                @pl.when(e < end)
                def _():
                    expert_backward(e, 0)
                    big.send(6 + e, IN_UNIT + 2 * e, in_halves(e, 1 - core))

                @pl.when(e > start)
                def _():
                    big.take(5 + e, IN_UNIT + 2 * e - 2, in_halves(e - 1, core))

        work = {
            "outs": outs,
            "ins": ins,
            "send_t": lambda e: big.send(12, TOWER_UNIT, tower_halves(1 - core)),
            "take_t": lambda e: big.take(12, TOWER_UNIT, tower_halves(core)),
            "send_i": lambda e: big.send(6 + e, IN_UNIT + 2 * e, in_halves(e, 1 - core)),
            "take_i": lambda e: big.take(6 + e, IN_UNIT + 2 * e, in_halves(e, core)),
            "back": backs,
            "front": front_backward,
            "sum": lambda c, step: big.reduce(DIMS * c, DIMS, step),
            "all": lambda c, step: big.gather(DIMS * c, DIMS, step),
            **extra,
        }
        for name, *where in plan:
            work[name](*where)

    forward_all()

    @pl.when(section == 0)
    def _():
        big = family(0, SPLIT, True)
        proj = family(1)
        perform(
            PLAN_FIRST,
            big,
            {
                "seq": lambda start, end: pl.loop(2 * start, 2 * end)(attention_back),
                "weights": attention_weights,
                "send_p": lambda: proj.send(0, 0, proj_half(1 - core)),
                "take_p": lambda: proj.take(0, 0, proj_half(core)),
                "sum_p": lambda step: proj.reduce(0, DIMS, step),
                "all_p": lambda step: proj.gather(0, DIMS, step),
                "tiny": tiny_step,
            },
        )
        big.drain(FAMILIES[0][0] - SPLIT, 0)
        proj.drain(DIMS, DIMS)
        for step in range(DIMS + 1):
            tiny_copy(step).wait_send()
        tiny_out[...] = tiny[DIMS + 1]

    @pl.when(section == 1)
    def _():
        big = family(0)
        vectors = family(2)
        perform(
            PLAN_SECOND,
            big,
            {
                "send_v": lambda: vectors.send(0, 0, small_half(1 - core)),
                "take_v": lambda: vectors.take(0, 0, small_half(core)),
                "sum_v": lambda step: vectors.reduce(0, 1, step),
                "all_v": lambda step: vectors.gather(0, 1, step),
            },
        )
        big.drain(SPLIT, FAMILIES[0][0])
        vectors.drain(1, 1)


def run(*args):
    here = pl.BlockSpec(memory_space=pltpu.VMEM)
    far = pl.BlockSpec(memory_space=pl.ANY)

    def keep(*shape, dtype=F32):
        return pltpu.VMEM(shape, dtype)

    scratch = [
        keep(ROWS, SEQ, dtype=BF16),
        keep(EXPERTS, HIDDEN, WIDE, dtype=BF16),
        keep(EXPERTS, WIDE, HIDDEN, dtype=BF16),
        keep(SPAN, SPAN, dtype=BF16),
        keep(EMBED, SPAN),
        keep(SPAN, LANES),
        keep(SPAN, LANES),
        keep(EMBED, SPAN),
        keep(SPAN, LANES),
        keep(FIELDS, HIDDEN, dtype=BF16),
        keep(16, HIDDEN, dtype=BF16),
        keep(ROWS, 8),
        keep(ROWS, FIELDS, dtype=BF16),
        keep(ROWS, HIDDEN, dtype=BF16),
        keep(ROWS, HIDDEN),
        keep(ROWS, HIDDEN, dtype=BF16),
        keep(ROWS, HIDDEN),
        keep(EXPERTS, ROWS, WIDE, dtype=BF16),
        keep(EXPERTS, ROWS, WIDE, dtype=BF16),
        keep(EXPERTS, ROWS, HIDDEN, dtype=BF16),
        keep(EXPERTS, ROWS, HIDDEN, dtype=BF16),
        keep(ROWS, HIDDEN),
        keep(ROWS, HIDDEN),
        keep(ROWS, 8),
        keep(ROWS, 8),
        keep(ROWS, 8),
        keep(ROWS, HIDDEN, dtype=BF16),
        keep(ROWS, HIDDEN, dtype=BF16),
        keep(ROWS, HIDDEN, dtype=BF16),
        keep(ROWS, LANES),
        keep(ROWS, LANES),
        keep(ROWS, LANES),
        keep(64, HIDDEN),
        keep(DIMS + 2, TINY_ROWS, LANES),
        keep(DIMS + 1, TINY_ROWS, LANES),
        pltpu.SemaphoreType.DMA((13,)),
        pltpu.SemaphoreType.DMA((DIMS + 1,)),
        pltpu.SemaphoreType.DMA((DIMS + 1,)),
    ]
    for family in FAMILIES:
        scratch += family_scratch(*family)
    outs = [pltpu.VMEM((units, 2, rows, LANES), dtype) for units, _, _, rows, dtype in FAMILIES]
    outs += [
        pltpu.VMEM((TINY_ROWS, LANES), F32),
        pltpu.VMEM((2, 8, LANES), F32),
        pltpu.VMEM((ROWS, FIELDS), F32),
        pltpu.VMEM((ROWS, SEQ), BF16),
    ]
    return pl.pallas_call(
        kernel,
        out_shape=outs,
        in_specs=[here] * 19 + [far] * 3,
        out_specs=[here] * 7,
        scratch_shapes=scratch,
        compiler_params=pltpu.CompilerParams(
            collective_id=0, has_side_effects=True, vmem_limit_bytes=46 << 20
        ),
        name="rank_and_sum",
    )(*args)


def place_kernel(
    big,
    proj_units,
    small,
    tiny,
    pred_all,
    field_rows,
    seq_rows,
    out_grad,
    in_grad,
    field_grad,
    seq_grad,
    proj,
    tower,
    predictions,
    b_proj,
    gain,
    shift,
    tower_b,
    tower_o,
    tower_e,
    roots,
    gate,
    in_b,
    out_b,
    query,
    key,
    value,
    out_stage,
    in_stage,
    seq_stage,
    field_stage,
    proj_stage,
    tower_stage,
    out_sem,
    in_sem,
    other_sem,
):
    section = lax.axis_index("section")
    second = (section == 1).astype(F32)

    def out_copy(e, slot):
        return pltpu.make_async_copy(out_stage.at[slot], out_grad.at[0, e], out_sem.at[e])

    def in_copy(e, slot):
        return pltpu.make_async_copy(in_stage.at[slot], in_grad.at[0, e], in_sem.at[e])

    stages = ((seq_stage, seq_grad), (field_stage, field_grad), (proj_stage, proj), (tower_stage, tower))
    others = [pltpu.make_async_copy(stage, grad.at[0], other_sem.at[i]) for i, (stage, grad) in enumerate(stages)]

    @pl.when(section == 0)
    def _():
        out_stage[0] = jnp.zeros((WIDE, HIDDEN), F32)
        in_stage[0] = jnp.zeros((HIDDEN, WIDE), F32)
        for e in range(EXPERTS):
            out_copy(e, 0).start()
            in_copy(e, 0).start()
        seq_stage[...] = seq_rows[...].astype(F32)
        others[0].start()
        field_stage[...] = field_rows[...]
        others[1].start()
        for core in range(2):
            flat = jnp.concatenate([proj_units[i, core].astype(F32) for i in range(DIMS)], axis=0)
            for j in range(2):
                at = slice((2 * core + j) * LANES, (2 * core + j + 1) * LANES)
                proj_stage[:, at] = flat[j * FIELDS : (j + 1) * FIELDS]
        others[2].start()
        tower_stage[...] = jnp.zeros_like(tower_stage)
        others[3].start()
        for e in range(EXPERTS):
            out_copy(e, 0).wait()
            in_copy(e, 0).wait()

    @pl.when(section == 1)
    def _():
        @pl.loop(0, EXPERTS)
        def _(e):
            slot = e % 2

            @pl.when(e > 1)
            def _():
                out_copy(e - 2, slot).wait()

            for core in range(2):
                for j in range(2):
                    at = (2 * core + j) * LANES
                    out_stage[slot, :, at : at + LANES] = big[2 * e + j, core].astype(F32)
            out_copy(e, slot).start()

            @pl.when(e > 1)
            def _():
                in_copy(e - 2, slot).wait()

            for core in range(2):
                for j in range(2):
                    for i in range(2):
                        at = (4 * core + 2 * j + i) * LANES
                        rows = slice(i * HIDDEN, (i + 1) * HIDDEN)
                        in_stage[slot, :, at : at + LANES] = big[IN_UNIT + 2 * e + j, core, rows].astype(F32)
            in_copy(e, slot).start()

        for core in range(2):
            for j in range(2):
                at = slice((2 * core + j) * LANES, (2 * core + j + 1) * LANES)
                tower_stage[:, at] = big[TOWER_UNIT, core, j * HIDDEN : (j + 1) * HIDDEN].astype(F32)
        seq_stage[...] = jnp.zeros_like(seq_stage)
        field_stage[...] = jnp.zeros_like(field_stage)
        proj_stage[...] = jnp.zeros_like(proj_stage)
        for other in others:
            other.start()
        for e in (EXPERTS - 2, EXPERTS - 1):
            out_copy(e, e % 2).wait()
            in_copy(e, e % 2).wait()

    for j in range(2):
        predictions[:, j * LANES : (j + 1) * LANES] = jnp.where(section == 1, pred_all[j, 0:1], 0.0)

    def rows(start, count):
        found = jnp.concatenate(
            [small[0, core, j * 64 + start : j * 64 + start + count] for core in range(2) for j in range(2)],
            axis=1,
        )
        return jnp.where(section == 1, found, 0.0)

    head = rows(0, 8)
    gain[...] = head[1:2]
    shift[...] = head[2:3]
    tower_b[...] = head[3:4]
    tower_o[...] = head[4:5]
    tower_e[...] = head[5:6, 0:2]
    count = head[5:6, 4:5]
    squares = head[5:6, 2:4] / (float(HIDDEN) * jnp.maximum(count, 1.0)) + EPSILON
    roots[...] = jnp.where(count > 0.0, jnp.sqrt(squares), 0.0) * second
    gate_lines, out_lines = rows(8, 8), rows(32, 8)
    in_lines = jnp.concatenate([rows(16, 8), rows(24, 8)], axis=1)
    for i in range(7):
        gate[i] = gate_lines[i : i + 1]
    for e in range(EXPERTS):
        in_b[e] = in_lines[e : e + 1]
        out_b[e] = out_lines[e : e + 1]
    three = jnp.where(section == 0, tiny[...], 0.0)
    b_proj[...] = jnp.concatenate([three[16 + i : 17 + i] for i in range(4)], axis=1)
    query[0] = three[:EMBED, 0:16]
    key[0] = three[:EMBED, 16:32]
    value[0] = three[:EMBED, 32:48]
    for other in others:
        other.wait()


def place(*results):
    here = pl.BlockSpec(memory_space=pltpu.VMEM)
    far = pl.BlockSpec(memory_space=pl.ANY)
    shapes = [(1, 6, 1024, 512), (1, 6, 512, 1024), (1, ROWS, FIELDS), (1, ROWS, SEQ), (1, 640, 512), (1, 512, 512)]
    shapes += [(1, ROWS)] + [(1, 512)] * 5 + [(1, 2)] * 2
    shapes += [(7, 1, 512), (6, 1, 1024), (6, 1, 512)] + [(1, 16, 16)] * 3
    return pl.pallas_call(
        place_kernel,
        out_shape=[jax.ShapeDtypeStruct(shape, F32) for shape in shapes],
        in_specs=[here] * 7,
        out_specs=[far] * 6 + [here] * 14,
        scratch_shapes=[
            pltpu.VMEM((2, WIDE, HIDDEN), F32),
            pltpu.VMEM((2, HIDDEN, WIDE), F32),
            pltpu.VMEM((ROWS, SEQ), F32),
            pltpu.VMEM((ROWS, FIELDS), F32),
            pltpu.VMEM((FIELDS, HIDDEN), F32),
            pltpu.VMEM((HIDDEN, HIDDEN), F32),
            pltpu.SemaphoreType.DMA((EXPERTS,)),
            pltpu.SemaphoreType.DMA((EXPERTS,)),
            pltpu.SemaphoreType.DMA((4,)),
        ],
        compiler_params=pltpu.CompilerParams(vmem_limit_bytes=24 << 20),
        name="place",
    )(*(pltpu.with_memory_space_constraint(result, pltpu.VMEM) for result in results))


def body(
    fields,
    behaviour,
    lengths,
    domains,
    validity,
    cotangent,
    w_query,
    w_key,
    w_value,
    w_proj,
    b_proj,
    norm_gain,
    norm_shift,
    gate_weight,
    w_in,
    b_in,
    w_out,
    b_out,
    tower_in,
    tower_bias,
    tower_out,
    tower_end,
):
    def line(array):
        return array.reshape(1, -1)

    results = run(
        fields,
        line(lengths),
        line(domains),
        line(validity),
        line(cotangent),
        w_query,
        w_key,
        w_value,
        w_proj,
        line(b_proj),
        line(norm_gain),
        line(norm_shift),
        gate_weight.T,
        b_in,
        b_out,
        tower_in,
        line(tower_bias),
        line(tower_out),
        line(tower_end),
        behaviour,
        w_in,
        w_out,
    )
    (
        out_grad,
        in_grad,
        field_grad,
        seq_grad,
        proj,
        tower,
        predictions,
        b_proj_grad,
        gain,
        shift,
        tower_b,
        tower_o,
        tower_e,
        roots,
        gate,
        in_b,
        out_b,
        query,
        key,
        value,
    ) = place(*results)
    return (
        predictions,
        field_grad,
        seq_grad,
        query,
        key,
        value,
        proj,
        b_proj_grad,
        gain,
        shift,
        gate.transpose(1, 2, 0),
        in_grad,
        in_b.transpose(1, 0, 2),
        out_grad,
        out_b.transpose(1, 0, 2),
        tower,
        tower_b,
        tower_o,
        tower_e,
        roots,
    )


def solution(mesh):
    each = (P("dp", None), P("dp", None), P("dp"), P("dp"), P("dp"), P("dp"))
    ranks = (2, 3, 3, 3, 3, 3, 3, 2, 2, 2, 3, 4, 3, 4, 3, 3, 2, 2, 2, 2)
    outs = tuple(
        P("section", "dp", *(None,) * (rank - 2)) if i < 3 else P("section", *(None,) * (rank - 1))
        for i, rank in enumerate(ranks)
    )
    return jax.shard_map(
        body, mesh=mesh, in_specs=each + (P(),) * 16, out_specs=outs, check_vma=False
    )
```

```python
import jax
import jax.numpy as jnp
from jax import lax
from jax.experimental import pallas as pl
from jax.experimental.pallas import tpu as pltpu
from jax.sharding import PartitionSpec as P

EPSILON = 1e-05
MESH = pl.DeviceIdType.MESH
F32 = jnp.float32
BF16 = jnp.bfloat16

LANES = 128
DIMS = 5
HALVINGS = 3
SLOTS = 7 + HALVINGS
ROWS = 256
EXPERTS = 6
HIDDEN = 512
WIDE = 1024
FIELDS = 640
EMBED = 16
SEQ = 3200
SPAN = 256
PIECES = tuple((at, SPAN) for at in range(0, 3072, SPAN)) + ((3072, LANES),)
PROJ_ROWS = 256
SMALL_ROWS = 128
BLOCK = 128
BACK_BLOCK = 64


def coords():
    section, place = lax.axis_index("section"), lax.axis_index("dp")
    return 2 * section + place // 32, (place // 8) % 4, (place // 2) % 4, place % 2


def device_at(z, x, y, core):
    return {"section": z // 2, "dp": (((z % 2) * 4 + x) * 4 + y) * 2 + core}


def hop(r, kind):
    near, far = 1 - 2 * (r % 2), 3 - 2 * r
    return near + kind * (far - near)


def side(r, kind):
    near = (r + r // 2) % 2
    return near + kind * (r // 2 - near)


def picks(dim):
    a = dim % 3
    return (1 - a) * (2 - a) // 2, a * (2 - a), a * (a - 1) // 2, dim // 3


def neighbour(dim):
    z, x, y, core = coords()
    ex, ey, ez, kind = picks(dim)
    return device_at(z + ez * hop(z, kind), x + ex * hop(x, kind), y + ey * hop(y, kind), core)


def which_half(dim):
    z, x, y, core = coords()
    ex, ey, ez, kind = picks(dim)
    return ex * side(x, kind) + ey * side(y, kind) + ez * side(z, kind)


def sibling():
    z, x, y, core = coords()
    return device_at(z, x, y, 1 - core)


def cross():
    z, x, y, core = coords()
    return device_at(3 - z, x, y, core)


class Family:
    def __init__(self, rows, out, refs, first, to_other=False):
        self.rows = rows
        self.share = rows >> HALVINGS
        self.out = out
        self.first = first
        self.to_other = to_other
        (
            self.kept,
            self.arrived,
            self.pair_send,
            self.pair_recv,
            self.send_sem,
            self.recv_sem,
        ) = refs

    def total(self, units, rows=slice(None)):
        return self.out.at[units, coords()[3], rows]

    def remote(self, unit, slot, src, dst, to):
        return pltpu.make_async_remote_copy(
            src_ref=src,
            dst_ref=dst,
            send_sem=self.send_sem.at[slot],
            recv_sem=self.recv_sem.at[unit // DIMS, slot],
            device_id=to,
            device_id_type=MESH,
        )

    def start_of(self, part, step):
        start = 0
        for k in range(step):
            start = start + which_half((part + k) % DIMS) * (self.rows >> (k + 1))
        return start

    def span(self, start, size):
        return pl.ds(pl.multiple_of(start, size), size)

    def own_share(self, unit):
        return self.span(self.start_of(unit % DIMS, HALVINGS), self.share)

    def across(self, group, unit, count):
        return pltpu.make_async_remote_copy(
            src_ref=self.total(pl.ds(unit, count)),
            dst_ref=self.kept.at[pl.ds(unit - self.first, count)],
            send_sem=self.pair_send.at[group],
            recv_sem=self.pair_recv.at[group],
            device_id=sibling(),
            device_id_type=MESH,
        )

    def halve(self, unit, k):
        size = self.rows >> (k + 1)
        dim = (unit + k) % DIMS
        start = self.start_of(unit % DIMS, k) + (1 - which_half(dim)) * size
        local = unit - self.first
        return self.remote(
            unit,
            k,
            self.kept.at[local, self.span(start, size)],
            self.arrived.at[local, pl.ds(self.rows - 2 * size, size)],
            neighbour(dim),
        )

    def double(self, unit, j):
        local = unit - self.first
        start = self.rows - self.share + j * self.share
        src = self.kept.at[local, self.own_share(unit)]
        if j:
            src = self.arrived.at[local, pl.ds(start - self.share, self.share)]
        return self.remote(
            unit,
            HALVINGS + j,
            src,
            self.arrived.at[local, pl.ds(start, self.share)],
            neighbour((unit + HALVINGS + j) % DIMS),
        )

    def over(self, unit):
        region = self.total(unit, self.own_share(unit))
        return self.remote(unit, DIMS, region, region, cross())

    def spread(self, unit, k):
        size = self.rows >> (k + 1)
        region = self.total(unit, self.span(self.start_of(unit % DIMS, k + 1), size))
        return self.remote(unit, DIMS + 1 + k, region, region, neighbour((unit + k) % DIMS))

    def back(self, unit, late):
        size = self.rows // 2
        own = which_half(unit % DIMS)
        region = self.total(unit, self.span((own + late * (1 - 2 * own)) * size, size))
        return self.remote(unit, DIMS + 1 + HALVINGS, region, region, sibling())

    def send(self, group, unit, halves):
        for i, rows in enumerate(halves):
            self.out[unit + i, coords()[3]] = rows.astype(self.out.dtype)
        self.across(group, unit, len(halves)).start()

    def take(self, group, unit, halves):
        pair = self.across(group, unit, len(halves))
        pair.wait_send()
        pair.wait_recv()
        for i, rows in enumerate(halves):
            local = unit + i - self.first
            self.kept[local] = (rows + self.kept[local].astype(F32)).astype(self.kept.dtype)
            self.halve(unit + i, 0).start()

    def await_chunk(self, slot, base, ref):
        pltpu.make_async_copy(ref, ref, self.recv_sem.at[base // DIMS, slot]).wait()

    def each(self, base, count, work):
        def one(i, _):
            work(base + i)
            return 0

        lax.fori_loop(0, count, one, 0)

    def reduce(self, base, count, step):
        dtype = self.kept.dtype
        local = pl.ds(base - self.first, count)
        if step < HALVINGS:
            size = self.rows >> (step + 1)
            arrivals = pl.ds(self.rows - 2 * size, size)
        else:
            size = self.share
            arrivals = pl.ds(self.rows - size + (step - HALVINGS) * size, size)
        self.await_chunk(step, base, self.arrived.at[local, arrivals])

        def one(unit):
            here = unit - self.first
            came = self.arrived[here, arrivals].astype(F32)
            if step < HALVINGS:
                region = self.span(self.start_of(unit % DIMS, step + 1), size)
                self.kept[here, region] = (self.kept[here, region].astype(F32) + came).astype(dtype)
                if step + 1 < HALVINGS:
                    self.halve(unit, step + 1).start()
                else:
                    self.double(unit, 0).start()
                return
            j = step - HALVINGS
            region = self.own_share(unit)
            before = pl.ds(self.rows - size + (j - 1) * size, size)
            old = self.arrived[here, before] if j else self.kept[here, region]
            new = (old.astype(F32) + came).astype(dtype)
            if step + 1 < DIMS:
                self.arrived[here, arrivals] = new
                self.double(unit, j + 1).start()
            else:
                self.out[unit, coords()[3], region] = new
                if self.to_other:
                    self.over(unit).start()
                else:
                    self.spread(unit, HALVINGS - 1).start()

        self.each(base, count, one)

    def gather(self, base, count, step):
        units = pl.ds(base, count)
        if step == 0:
            self.await_chunk(DIMS, base, self.total(units, pl.ds(0, self.share)))
            self.each(base, count, lambda unit: self.spread(unit, HALVINGS - 1).start())
        elif step <= HALVINGS:
            k = HALVINGS - step
            self.await_chunk(DIMS + 1 + k, base, self.total(units, pl.ds(0, self.rows >> (k + 1))))

            def one(unit):
                if k > 0:
                    self.spread(unit, k - 1).start()
                if k < 2:
                    self.back(unit, 1 - k).start()

            self.each(base, count, one)
        else:
            self.await_chunk(DIMS + 1 + HALVINGS, base, self.out.at[units, 1 - coords()[3]])

    def drain(self, reduced, gathered):
        def sent(slot, ref):
            pltpu.make_async_copy(ref, ref, self.send_sem.at[slot]).wait()

        for step in range(DIMS):
            size = self.rows >> (step + 1) if step < HALVINGS else self.share
            sent(step, self.kept.at[pl.ds(0, reduced), pl.ds(0, size)])
        if self.to_other:
            sent(DIMS, self.kept.at[pl.ds(0, reduced), pl.ds(0, self.share)])
        if gathered:
            for k in range(HALVINGS):
                sent(DIMS + 1 + k, self.total(pl.ds(0, gathered), pl.ds(0, self.rows >> (k + 1))))
            sent(DIMS + 1 + HALVINGS, self.total(pl.ds(0, gathered)))


def family_scratch(units, reduced, groups, rows, dtype):
    share = rows >> HALVINGS
    chunks = pl.cdiv(units, DIMS)
    return [
        pltpu.VMEM((reduced, rows, LANES), dtype),
        pltpu.VMEM((reduced, rows - share + (DIMS - HALVINGS) * share, LANES), dtype),
        pltpu.SemaphoreType.DMA((groups,)),
        pltpu.SemaphoreType.DMA((groups,)),
        pltpu.SemaphoreType.DMA((SLOTS,)),
        pltpu.SemaphoreType.DMA((chunks, SLOTS)),
    ]


FAMILIES = ((25, 15, 13, 1024, BF16), (DIMS, DIMS, 1, PROJ_ROWS, BF16), (1, 1, 1, SMALL_ROWS, F32))
TOWER_UNIT = 12
IN_UNIT = 13
SPLIT = 15
TINY_ROWS = 24


PLAN_FIRST = (
    ("ins", 1, 6), ("back", 0, 1), ("front",), ("sum", 3, 0), ("sum", 4, 0), ("send_p",), ("sum", 3, 1), ("take_p",),
    ("sum", 4, 1), ("sum", 3, 2), ("sum", 4, 2), ("sum", 3, 3), ("sum_p", 0), ("sum", 3, 4), ("sum", 4, 3),
    ("sum_p", 1), ("seq", 0, 1), ("sum", 4, 4), ("sum_p", 2), ("seq", 1, 2), ("weights",), ("tiny", 0), ("sum_p", 3),
    ("sum_p", 4), ("tiny", 1), ("tiny", 2), ("all_p", 1), ("tiny", 3), ("all_p", 2), ("tiny", 4), ("all_p", 3),
    ("tiny", 5), ("all_p", 4), ("tiny", 6),
)
PLAN_SECOND = (
    ("outs", 0, 6), ("send_t", 0), ("back", 0, 1), ("send_i", 0), ("sum", 0, 0), ("take_t", 0), ("take_i", 0),
    ("sum", 1, 0), ("back", 3, 6), ("sum", 0, 1), ("back", 1, 3), ("sum", 1, 1), ("sum", 2, 0), ("sum", 0, 2),
    ("front",), ("sum", 1, 2), ("send_v",), ("sum", 2, 1), ("sum", 0, 3), ("take_v",), ("sum", 1, 3), ("sum", 2, 2),
    ("sum", 0, 4), ("sum_v", 0), ("sum", 1, 4), ("sum", 2, 3), ("sum_v", 1), ("all", 0, 1), ("all", 1, 1),
    ("sum", 2, 4), ("sum_v", 2), ("all", 3, 0), ("all", 0, 2), ("all", 3, 1), ("sum_v", 3), ("all", 4, 0),
    ("all", 2, 1), ("all", 1, 2), ("sum_v", 4), ("all", 4, 1), ("all", 2, 2), ("all_v", 1), ("all", 4, 2),
    ("all_v", 2), ("all", 1, 3), ("all", 3, 2), ("all", 0, 3), ("all_v", 3), ("all", 4, 3), ("all_v", 4),
    ("all", 2, 3), ("all", 1, 4), ("all", 3, 3), ("all", 0, 4), ("all", 2, 4), ("all", 4, 4), ("all", 3, 4),
)


def exact(left, right):
    return jnp.dot(left, right, precision=lax.Precision.HIGHEST, preferred_element_type=F32)


def exact_cols(left, right):
    return lax.dot_general(
        left, right, (((1,), (1,)), ((), ())), precision=lax.Precision.HIGHEST, preferred_element_type=F32
    )


def exact_rows(left, right):
    return lax.dot_general(
        left, right, (((0,), (0,)), ((), ())), precision=lax.Precision.HIGHEST, preferred_element_type=F32
    )


def product(left, right):
    return jnp.dot(left, right, preferred_element_type=F32)


def contract_rows(left, right):
    return lax.dot_general(left, right, (((0,), (0,)), ((), ())), preferred_element_type=F32)


def contract_cols(left, right):
    return lax.dot_general(left, right, (((1,), (1,)), ((), ())), preferred_element_type=F32)


def split(value, terms):
    out = []
    for _ in range(terms):
        out.append(value.astype(BF16))
        value = value - out[-1].astype(F32)
    return out


def sigmoid(v):
    return 1.0 / (1.0 + jnp.exp(-v))


ROOT = 0.7978845608028654
CUBE = 0.044715


def gelu_both(v):
    square = v * v
    bent = jnp.tanh(v * (ROOT + ROOT * CUBE * square))
    half = 0.5 + 0.5 * bent
    value = v * half
    slope = half + value * (1.0 - half) * (2.0 * ROOT + 6.0 * ROOT * CUBE * square)
    return value, slope


def column_sum(array):
    return jnp.sum(array, axis=0, keepdims=True)


def row_sum(array):
    return jnp.sum(array, axis=1, keepdims=True)


def lanes(shape):
    return lax.broadcasted_iota(jnp.int32, shape, 1)


def lane_match(rows, columns, period, shift=0):
    place = lax.broadcasted_iota(jnp.int32, (rows, columns), 1) - shift
    if period:
        place = place % period
    return (place == lax.broadcasted_iota(jnp.int32, (rows, columns), 0)).astype(F32)


def kernel(
    lengths,
    domains,
    validity,
    cotangent,
    w_query,
    w_key,
    w_value,
    b_proj,
    norm_gain,
    norm_shift,
    gate_turned,
    b_in,
    b_out,
    tower_bias,
    tower_out,
    tower_end,
    fields_hbm,
    w_proj_hbm,
    tower_in_hbm,
    behaviour_hbm,
    w_in_hbm,
    w_out_hbm,
    big_out,
    proj_out,
    small_out,
    tiny_out,
    pred_all,
    d_fields,
    d_seq,
    fields,
    tower_in,
    behaviour,
    w_in,
    w_out,
    groups,
    probe_w,
    value_w,
    pooled_w,
    back_w,
    target_w,
    proj_turned,
    gate_rows,
    info,
    joined,
    activation,
    proj_slope,
    normed,
    standard,
    active,
    slope,
    expert,
    d_expert,
    d_normed,
    d_residual,
    mixing,
    d_mixing,
    gates,
    residual_low,
    d_tower,
    d_proj_low,
    pooled_rows,
    d_value_rows,
    d_probe_rows,
    small,
    tiny,
    tiny_arrived,
    load_sem,
    tiny_send,
    tiny_recv,
    *family_refs,
):
    section = lax.axis_index("section")
    core = coords()[3]

    barrier = pltpu.get_barrier_semaphore()
    for dim in range(DIMS):
        pl.semaphore_signal(barrier, inc=1, device_id=neighbour(dim), device_id_type=MESH)
    for other in (sibling(), cross()):
        pl.semaphore_signal(barrier, inc=1, device_id=other, device_id_type=MESH)

    seq_copy = pltpu.make_async_copy(behaviour_hbm, behaviour, load_sem.at[2])

    load_in = pltpu.make_async_copy(w_in_hbm, w_in, load_sem.at[0])
    load_out = pltpu.make_async_copy(w_out_hbm, w_out, load_sem.at[1])
    load_fields = pltpu.make_async_copy(fields_hbm, fields, load_sem.at[3])
    load_tower = pltpu.make_async_copy(tower_in_hbm, tower_in, load_sem.at[4])
    cut = FIELDS - EMBED
    load_proj = [
        pltpu.make_async_copy(w_proj_hbm.at[pl.ds(cut, EMBED)], proj_turned.at[pl.ds(0, EMBED)], load_sem.at[5]),
        pltpu.make_async_copy(w_proj_hbm.at[pl.ds(0, cut)], proj_turned.at[pl.ds(EMBED, cut)], load_sem.at[6]),
    ]

    tile = lane_match(EMBED, SPAN, EMBED)

    def prepare():
        seq_copy.start()
        load_fields.start()
        for copy in load_proj:
            copy.start()
        load_in.start()
        load_out.start()
        load_tower.start()
        group = lax.broadcasted_iota(jnp.int32, (SPAN, SPAN), 0) // EMBED
        groups[...] = (group == lanes((SPAN, SPAN)) // EMBED).astype(F32).astype(BF16)
        eye = lane_match(EMBED, LANES, 0)
        probe_w[...] = exact(w_query[...], exact_rows(w_key[...], tile))
        value_w[...] = exact_rows(tile, exact(w_value[...], eye))
        pooled_w[...] = exact_rows(tile, eye)
        back_w[...] = exact_rows(w_value[...], tile)
        target_w[...] = exact_rows(tile, exact(exact_cols(w_key[...], w_query[...]), eye))
        rows = [lengths[...].astype(F32), domains[...].astype(F32), validity[...].astype(F32), cotangent[...]]
        info[...] = jnp.transpose(jnp.concatenate(rows + [jnp.zeros((4, ROWS), F32)], axis=0))
        gate_rows[...] = jnp.zeros_like(gate_rows)
        gate_rows[:7] = gate_turned[...]
        small[...] = jnp.zeros_like(small)
        tiny[0] = jnp.zeros((TINY_ROWS, LANES), F32)
        seq_copy.wait()
        load_fields.wait()

    def group_sum(value, terms):
        count, width = value.shape
        stacked = jnp.concatenate(split(value, terms), axis=0)
        sums = product(stacked, groups[:width, :width])
        return sum(sums[i * count : (i + 1) * count] for i in range(terms))

    def narrow_sum(pieces):
        wide = sum(pieces[:-1])
        return jnp.concatenate([wide[:, :LANES] + pieces[-1], wide[:, LANES:]], axis=1)

    def stretch(rows, at, width):
        return behaviour[rows, at : at + width].astype(F32)

    def attention(rows):
        target = fields[rows, 0:LANES].astype(F32)[:, :EMBED]
        probe = exact(target, probe_w[...])
        length = info[rows, 0:1]
        scores = []
        for at, width in PIECES:
            sums = group_sum(stretch(rows, at, width) * probe[:, :width], 3)
            place = ((lanes((1, width)) + at) // EMBED).astype(F32)
            scores.append(jnp.where(place < length, 0.5 * sums, -1e30))
        peak = scores[0]
        for piece in scores[1:-1]:
            peak = jnp.maximum(peak, piece)
        peak = jnp.maximum(jnp.max(peak, axis=1, keepdims=True), jnp.max(scores[-1], axis=1, keepdims=True))
        raised = [jnp.exp(piece - peak) for piece in scores]
        scale = float(EMBED) / row_sum(narrow_sum(raised))
        return probe, [piece * scale for piece in raised]

    def pool(rows, attn):
        return narrow_sum([w * stretch(rows, at, width) for w, (at, width) in zip(attn, PIECES)])

    def attention_forward(block, _):
        rows = pl.ds(pl.multiple_of(block * BLOCK, BLOCK), BLOCK)
        _, attn = attention(rows)
        value = exact(pool(rows, attn), value_w[...])
        joined[rows, LANES:] = fields[rows, LANES:]
        head = fields[rows, :LANES]
        joined[rows, :LANES] = jnp.where(lanes(head.shape) < EMBED, value.astype(BF16), head)
        return 0

    def gate_columns():
        return [gates[:, i : i + 1] for i in range(6)]

    def front_forward():
        for copy in load_proj:
            copy.wait()
        projected = product(joined[...], proj_turned[...]) + b_proj[...]
        act, slope_proj = gelu_both(projected)
        activation[...] = act.astype(BF16)
        act = act.astype(BF16).astype(F32)
        proj_slope[...] = slope_proj
        centred = act - row_sum(act) * (1.0 / HIDDEN)
        scale = lax.rsqrt(row_sum(centred * centred) * (1.0 / HIDDEN) + EPSILON)
        standard[...] = centred * scale
        normed[...] = (centred * scale * norm_gain[...] + norm_shift[...]).astype(BF16)

        logits = contract_cols(normed[...], gate_rows[...])
        in_first = info[:, 1:2] == 0.0
        level = sigmoid(logits[:, 6:7])
        shared_a = sigmoid(logits[:, 0:1] - logits[:, 1:2])
        shared_b = sigmoid(logits[:, 1:2] - logits[:, 0:1])
        lead = jnp.where(in_first, logits[:, 2:3] - logits[:, 3:4], logits[:, 4:5] - logits[:, 5:6])
        chosen_a, chosen_b = sigmoid(lead), sigmoid(-lead)
        zero = jnp.zeros_like(level)
        columns = [
            level * shared_a,
            level * shared_b,
            jnp.where(in_first, (1.0 - level) * chosen_a, zero),
            jnp.where(in_first, (1.0 - level) * chosen_b, zero),
            jnp.where(in_first, zero, (1.0 - level) * chosen_a),
            jnp.where(in_first, zero, (1.0 - level) * chosen_b),
        ]
        place = lanes((ROWS, 8))
        mixing[...] = sum(jnp.where(place == i, column, 0.0) for i, column in enumerate(columns))
        held = (scale, level, shared_a, shared_b, chosen_a, chosen_b)
        gates[...] = sum(jnp.where(place == i, column, 0.0) for i, column in enumerate(held))
        d_residual[...] = jnp.zeros_like(d_residual)

    def expert_forward(e, _):
        pre = product(normed[...], w_in[e]) + b_in[pl.ds(e, 1)]
        out, grade = gelu_both(pre)
        active[e] = out.astype(BF16)
        slope[e] = grade.astype(BF16)
        rows = product(active[e], w_out[e]) + b_out[pl.ds(e, 1)]
        expert[e] = rows.astype(BF16)
        weight = row_sum(jnp.where(lanes((ROWS, 8)) == e, mixing[...], 0.0))
        d_residual[...] += weight * rows
        return 0

    def tower_both():
        load_tower.wait()
        branch = d_residual[...]
        residual = activation[...].astype(F32) + branch
        in_first = info[:, 1:2] == 0.0
        valid = info[:, 2:3]
        residual_low[...] = residual.astype(BF16)
        tower_act, tower_slope = gelu_both(product(residual_low[...], tower_in[...]) + tower_bias[...])
        chosen = jnp.where(in_first, 0, 1) == lanes((ROWS, HIDDEN)) // 256
        ends = tower_end[...]
        end = jnp.where(in_first, ends[:, 0:1], ends[:, 1:2])
        predict = sigmoid(row_sum(jnp.where(chosen, tower_act * tower_out[...], 0.0)) + end)
        d_logit = info[:, 3:4] * valid * predict * (1.0 - predict)
        spread_logit = jnp.where(chosen, d_logit, 0.0)
        d_tower[...] = (spread_logit * tower_out[...] * tower_slope).astype(BF16)
        small[3:4] = column_sum(d_tower[...].astype(F32))
        small[4:5] = column_sum(tower_act * spread_logit)
        spots = lanes((1, HIDDEN))
        parts = (
            column_sum(jnp.where(in_first, d_logit, 0.0)),
            column_sum(jnp.where(in_first, 0.0, d_logit)),
            column_sum(valid * row_sum(residual * residual)),
            column_sum(valid * row_sum(branch * branch)),
            column_sum(valid),
        )
        small[5:6] = sum(jnp.where(spots == i, part, 0.0) for i, part in enumerate(parts))
        wide = jnp.transpose(jnp.broadcast_to(predict, (ROWS, LANES)))
        pred_all[0] = wide[:8, :LANES]
        pred_all[1] = wide[:8, LANES:]
        d_residual[...] = contract_cols(d_tower[...], tower_in[...])

    def spread_residual(e, _):
        weight = row_sum(jnp.where(lanes((ROWS, 8)) == e, mixing[...], 0.0))
        low = (weight * d_residual[...]).astype(BF16)
        d_expert[e] = low
        small[pl.ds(32 + e, 1)] = column_sum(low.astype(F32))
        inner = row_sum(expert[e].astype(F32) * d_residual[...])
        d_mixing[...] = jnp.where(lanes((ROWS, 8)) == e, inner, d_mixing[...])
        return 0

    def expert_backward(e, _):
        grade = contract_cols(d_expert[e], w_out[e]) * slope[e].astype(F32)
        low = grade.astype(BF16)
        slope[e] = low
        sums = column_sum(low.astype(F32))
        small[pl.ds(16 + e, 1)] = sums[:, :512]
        small[pl.ds(24 + e, 1)] = sums[:, 512:]
        d_normed[...] += contract_cols(low, w_in[e])
        return 0

    def front_backward():
        scale, level, shared_a, shared_b, chosen_a, chosen_b = gate_columns()
        in_first = info[:, 1:2] == 0.0
        grads = [d_mixing[:, e : e + 1] for e in range(EXPERTS)]
        grad_a = jnp.where(in_first, grads[2], grads[4])
        grad_b = jnp.where(in_first, grads[3], grads[5])
        d_level = grads[0] * shared_a + grads[1] * shared_b - grad_a * chosen_a - grad_b * chosen_b
        d_shared = level * shared_a * shared_b * (grads[0] - grads[1])
        d_lead = (1.0 - level) * chosen_a * chosen_b * (grad_a - grad_b)
        zero = jnp.zeros_like(d_lead)
        d_first = jnp.where(in_first, d_lead, zero)
        d_second = jnp.where(in_first, zero, d_lead)
        columns = (d_shared, -d_shared, d_first, -d_first, d_second, -d_second, d_level * level * (1.0 - level))
        place = lanes((ROWS, LANES))
        d_logits = sum(jnp.where(place == i, column, 0.0) for i, column in enumerate(columns)).astype(BF16)
        small[8:16] = jnp.transpose(contract_rows(normed[...], d_logits))[:8]
        total = d_normed[...] + product(d_logits[:, :16], gate_rows[...])
        std = standard[...]
        small[1:2] = column_sum(total * std)
        small[2:3] = column_sum(total)
        scaled = total * norm_gain[...]
        inner = scaled - row_sum(scaled) * (1.0 / HIDDEN) - std * (row_sum(scaled * std) * (1.0 / HIDDEN))
        d_act = (inner * scale + d_residual[...]).astype(BF16).astype(F32)
        low = (d_act * proj_slope[...]).astype(BF16)
        sums = column_sum(low.astype(F32))
        for i in range(HIDDEN // LANES):
            tiny[0, 16 + i : 17 + i] = sums[:, i * LANES : (i + 1) * LANES]
        d_proj_low[...] = low

    def attention_back(block):
        rows = pl.ds(pl.multiple_of(block * BACK_BLOCK, BACK_BLOCK), BACK_BLOCK)
        probe, attn = attention(rows)
        pooled_rows[rows] = exact(pool(rows, attn), pooled_w[...])
        d_joined = contract_cols(d_proj_low[rows], proj_turned[...])
        head = d_joined[:, :LANES]
        d_value_rows[rows] = head
        d_pooled = exact(head[:, :EMBED], back_w[...])
        d_attn = [group_sum(stretch(rows, at, width) * d_pooled[:, :width], 2) for at, width in PIECES]
        inner = row_sum(narrow_sum([a * d for a, d in zip(attn, d_attn)])) * (1.0 / EMBED)
        pieces = []
        for (at, width), a, d in zip(PIECES, attn, d_attn):
            grade = 0.5 * a * (d - inner)
            pieces.append(grade * stretch(rows, at, width))
            d_seq[rows, at : at + width] = (a * d_pooled[:, :width] + grade * probe[:, :width]).astype(BF16)
        wide = narrow_sum(pieces)
        d_probe_rows[rows] = exact(wide, pooled_w[...])
        d_target = exact(wide, target_w[...])
        d_fields[rows] = d_joined
        d_fields[rows, :LANES] = jnp.where(lanes(head.shape) < EMBED, d_target, head)

    def attention_weights():
        target = fields[:, 0:LANES].astype(F32)[:, :EMBED]
        d_probe = d_probe_rows[...][:, :EMBED]
        query_grad = exact_rows(target, exact(d_probe, w_key[...]))
        key_grad = exact_rows(d_probe, exact(target, w_query[...]))
        value_grad = exact_rows(pooled_rows[...][:, :EMBED], d_value_rows[...][:, :EMBED])
        grads = (query_grad, key_grad, value_grad)
        tiny[0, :EMBED] = sum(exact(g, lane_match(EMBED, LANES, 0, EMBED * i)) for i, g in enumerate(grads))

    def out_halves(e, half):
        grad = contract_rows(active[e], d_expert[e, :, pl.ds(pl.multiple_of(half * 256, 256), 256)])
        return [grad[:, :LANES], grad[:, LANES:]]

    def in_halves(e, half):
        grad = contract_rows(normed[...], slope[e, :, pl.ds(pl.multiple_of(half * 512, 512), 512)])
        columns = [grad[:, i * LANES : (i + 1) * LANES] for i in range(4)]
        return [jnp.concatenate(columns[:2], axis=0), jnp.concatenate(columns[2:], axis=0)]

    def tower_halves(half):
        grad = contract_rows(residual_low[...], d_tower[:, pl.ds(pl.multiple_of(half * 256, 256), 256)])
        return [jnp.concatenate([grad[:, :LANES], grad[:, LANES:]], axis=0)]

    def proj_half(half):
        grad = contract_rows(joined[...], d_proj_low[:, pl.ds(pl.multiple_of(half * 256, 256), 256)])
        columns = []
        for j in range(2):
            column = grad[:, j * LANES : (j + 1) * LANES]
            columns += [column[EMBED:], column[:EMBED]]
        flat = jnp.concatenate(columns, axis=0)
        return [flat[unit * PROJ_ROWS : (unit + 1) * PROJ_ROWS] for unit in range(DIMS)]

    def small_half(half):
        columns = [small[:, pl.ds(pl.multiple_of(half * 256 + j * LANES, LANES), LANES)] for j in range(2)]
        return [jnp.concatenate(columns, axis=0)]

    def tiny_copy(step):
        return pltpu.make_async_remote_copy(
            src_ref=tiny.at[step],
            dst_ref=tiny_arrived.at[step],
            send_sem=tiny_send.at[step],
            recv_sem=tiny_recv.at[step],
            device_id=sibling() if step == DIMS else neighbour(step),
            device_id_type=MESH,
        )

    def tiny_step(step):
        if step:
            tiny_copy(step - 1).wait_recv()
            tiny[step] = tiny[step - 1] + tiny_arrived[step - 1]
        if step <= DIMS:
            tiny_copy(step).start()

    def forward_all():
        prepare()
        lax.fori_loop(0, ROWS // BLOCK, attention_forward, 0)
        front_forward()
        load_in.wait()
        load_out.wait()

        @pl.loop(0, EXPERTS, step=2)
        def _(e):
            expert_forward(e, 0)
            expert_forward(e + 1, 0)

        tower_both()
        d_normed[...] = jnp.zeros_like(d_normed)
        d_mixing[...] = jnp.zeros_like(d_mixing)
        pl.semaphore_wait(barrier, 7)

    def family(i, first=0, to_other=False):
        out = (big_out, proj_out, small_out)[i]
        return Family(FAMILIES[i][3], out, family_refs[6 * i : 6 * i + 6], first, to_other)

    def perform(plan, big, extra):
        def backs(start, end):
            lax.fori_loop(start, end, expert_backward, 0)

        def outs(start, end):
            @pl.loop(start, end + 1)
            def _(e):
                @pl.when(e < end)
                def _():
                    spread_residual(e, 0)
                    big.send(e, 2 * e, out_halves(e, 1 - core))

                @pl.when(e > start)
                def _():
                    big.take(e - 1, 2 * e - 2, out_halves(e - 1, core))

        def ins(start, end):
            @pl.loop(start, end + 1)
            def _(e):
                @pl.when(e < end)
                def _():
                    spread_residual(e, 0)
                    expert_backward(e, 0)
                    big.send(6 + e, IN_UNIT + 2 * e, in_halves(e, 1 - core))

                @pl.when(e > start)
                def _():
                    big.take(5 + e, IN_UNIT + 2 * e - 2, in_halves(e - 1, core))

        work = {
            "outs": outs,
            "ins": ins,
            "send_t": lambda e: big.send(12, TOWER_UNIT, tower_halves(1 - core)),
            "take_t": lambda e: big.take(12, TOWER_UNIT, tower_halves(core)),
            "send_i": lambda e: big.send(6 + e, IN_UNIT + 2 * e, in_halves(e, 1 - core)),
            "take_i": lambda e: big.take(6 + e, IN_UNIT + 2 * e, in_halves(e, core)),
            "back": backs,
            "front": front_backward,
            "sum": lambda c, step: big.reduce(DIMS * c, DIMS, step),
            "all": lambda c, step: big.gather(DIMS * c, DIMS, step),
            **extra,
        }
        for name, *where in plan:
            work[name](*where)

    forward_all()

    @pl.when(section == 0)
    def _():
        spread_residual(0, 0)
        big = family(0, SPLIT, True)
        proj = family(1)
        perform(
            PLAN_FIRST,
            big,
            {
                "seq": lambda start, end: pl.loop(2 * start, 2 * end)(attention_back),
                "weights": attention_weights,
                "send_p": lambda: proj.send(0, 0, proj_half(1 - core)),
                "take_p": lambda: proj.take(0, 0, proj_half(core)),
                "sum_p": lambda step: proj.reduce(0, DIMS, step),
                "all_p": lambda step: proj.gather(0, DIMS, step),
                "tiny": tiny_step,
            },
        )
        big.drain(FAMILIES[0][0] - SPLIT, 0)
        proj.drain(DIMS, DIMS)
        for step in range(DIMS + 1):
            tiny_copy(step).wait_send()
        tiny_out[...] = tiny[DIMS + 1]

    @pl.when(section == 1)
    def _():
        big = family(0)
        vectors = family(2)
        perform(
            PLAN_SECOND,
            big,
            {
                "send_v": lambda: vectors.send(0, 0, small_half(1 - core)),
                "take_v": lambda: vectors.take(0, 0, small_half(core)),
                "sum_v": lambda step: vectors.reduce(0, 1, step),
                "all_v": lambda step: vectors.gather(0, 1, step),
            },
        )
        big.drain(SPLIT, FAMILIES[0][0])
        vectors.drain(1, 1)


def run(*args):
    here = pl.BlockSpec(memory_space=pltpu.VMEM)
    far = pl.BlockSpec(memory_space=pl.ANY)

    def keep(*shape, dtype=F32):
        return pltpu.VMEM(shape, dtype)

    scratch = [
        keep(ROWS, FIELDS, dtype=BF16),
        keep(HIDDEN, HIDDEN, dtype=BF16),
        keep(ROWS, SEQ, dtype=BF16),
        keep(EXPERTS, HIDDEN, WIDE, dtype=BF16),
        keep(EXPERTS, WIDE, HIDDEN, dtype=BF16),
        keep(SPAN, SPAN, dtype=BF16),
        keep(EMBED, SPAN),
        keep(SPAN, LANES),
        keep(SPAN, LANES),
        keep(EMBED, SPAN),
        keep(SPAN, LANES),
        keep(FIELDS, HIDDEN, dtype=BF16),
        keep(16, HIDDEN, dtype=BF16),
        keep(ROWS, 8),
        keep(ROWS, FIELDS, dtype=BF16),
        keep(ROWS, HIDDEN, dtype=BF16),
        keep(ROWS, HIDDEN),
        keep(ROWS, HIDDEN, dtype=BF16),
        keep(ROWS, HIDDEN),
        keep(EXPERTS, ROWS, WIDE, dtype=BF16),
        keep(EXPERTS, ROWS, WIDE, dtype=BF16),
        keep(EXPERTS, ROWS, HIDDEN, dtype=BF16),
        keep(EXPERTS, ROWS, HIDDEN, dtype=BF16),
        keep(ROWS, HIDDEN),
        keep(ROWS, HIDDEN),
        keep(ROWS, 8),
        keep(ROWS, 8),
        keep(ROWS, 8),
        keep(ROWS, HIDDEN, dtype=BF16),
        keep(ROWS, HIDDEN, dtype=BF16),
        keep(ROWS, HIDDEN, dtype=BF16),
        keep(ROWS, LANES),
        keep(ROWS, LANES),
        keep(ROWS, LANES),
        keep(64, HIDDEN),
        keep(DIMS + 2, TINY_ROWS, LANES),
        keep(DIMS + 1, TINY_ROWS, LANES),
        pltpu.SemaphoreType.DMA((7,)),
        pltpu.SemaphoreType.DMA((DIMS + 1,)),
        pltpu.SemaphoreType.DMA((DIMS + 1,)),
    ]
    for family in FAMILIES:
        scratch += family_scratch(*family)
    outs = [pltpu.VMEM((units, 2, rows, LANES), dtype) for units, _, _, rows, dtype in FAMILIES]
    outs += [
        pltpu.VMEM((TINY_ROWS, LANES), F32),
        pltpu.VMEM((2, 8, LANES), F32),
        pltpu.VMEM((ROWS, FIELDS), F32),
        pltpu.VMEM((ROWS, SEQ), BF16),
    ]
    return pl.pallas_call(
        kernel,
        out_shape=outs,
        in_specs=[here] * 16 + [far] * 6,
        out_specs=[here] * 7,
        scratch_shapes=scratch,
        compiler_params=pltpu.CompilerParams(
            collective_id=0, has_side_effects=True, vmem_limit_bytes=46 << 20
        ),
        name="rank_and_sum",
    )(*args)


SMALL_SHAPES = ((1, ROWS),) + ((1, 512),) * 5 + ((1, 2),) * 2
SMALL_SHAPES += ((7, 1, 512), (6, 1, 1024), (6, 1, 512)) + ((1, 16, 16),) * 3


def place_kernel(
    big,
    proj_units,
    small,
    tiny,
    pred_all,
    field_rows,
    seq_rows,
    out_grad,
    in_grad,
    field_grad,
    seq_grad,
    proj,
    tower,
    *rest,
):
    count = len(SMALL_SHAPES)
    small_outs, small_stages = rest[:count], rest[count : 2 * count]
    (
        out_stage,
        in_stage,
        seq_stage,
        field_stage,
        proj_stage,
        tower_stage,
        out_sem,
        in_sem,
        other_sem,
        small_sem,
    ) = rest[2 * count :]
    section = lax.axis_index("section")
    second = (section == 1).astype(F32)

    def out_copy(e, slot):
        return pltpu.make_async_copy(out_stage.at[slot], out_grad.at[0, e], out_sem.at[slot])

    def in_copy(e, slot):
        return pltpu.make_async_copy(in_stage.at[slot], in_grad.at[0, e], in_sem.at[slot])

    stages = ((seq_stage, seq_grad), (field_stage, field_grad), (proj_stage, proj), (tower_stage, tower))
    others = [pltpu.make_async_copy(stage, grad.at[0], other_sem.at[i]) for i, (stage, grad) in enumerate(stages)]

    @pl.when(section == 0)
    def _():
        out_stage[0] = jnp.zeros((WIDE, HIDDEN), F32)
        in_stage[0] = jnp.zeros((HIDDEN, WIDE), F32)
        for e in range(EXPERTS):
            pltpu.make_async_copy(out_stage.at[0], out_grad.at[0, e], out_sem.at[2 + e]).start()
            pltpu.make_async_copy(in_stage.at[0], in_grad.at[0, e], in_sem.at[2 + e]).start()
        seq_stage[...] = seq_rows[...].astype(F32)
        others[0].start()
        field_stage[...] = field_rows[...]
        others[1].start()
        for core in range(2):
            flat = jnp.concatenate([proj_units[i, core].astype(F32) for i in range(DIMS)], axis=0)
            for j in range(2):
                at = slice((2 * core + j) * LANES, (2 * core + j + 1) * LANES)
                proj_stage[:, at] = flat[j * FIELDS : (j + 1) * FIELDS]
        others[2].start()
        tower_stage[...] = jnp.zeros_like(tower_stage)
        others[3].start()

    @pl.when(section == 1)
    def _():
        field_stage[...] = jnp.zeros_like(field_stage)
        others[1].start()
        proj_stage[...] = jnp.zeros_like(proj_stage)
        others[2].start()

        @pl.loop(0, EXPERTS)
        def _(e):
            slot = e % 2

            @pl.when(e > 1)
            def _():
                out_copy(e - 2, slot).wait()

            for core in range(2):
                for j in range(2):
                    at = (2 * core + j) * LANES
                    out_stage[slot, :, at : at + LANES] = big[2 * e + j, core].astype(F32)
            out_copy(e, slot).start()

            @pl.when(e > 1)
            def _():
                in_copy(e - 2, slot).wait()

            for core in range(2):
                for j in range(2):
                    for i in range(2):
                        at = (4 * core + 2 * j + i) * LANES
                        rows = slice(i * HIDDEN, (i + 1) * HIDDEN)
                        in_stage[slot, :, at : at + LANES] = big[IN_UNIT + 2 * e + j, core, rows].astype(F32)
            in_copy(e, slot).start()

            @pl.when(e == 0)
            def _():
                seq_stage[...] = jnp.zeros_like(seq_stage)
                others[0].start()

        for core in range(2):
            for j in range(2):
                at = slice((2 * core + j) * LANES, (2 * core + j + 1) * LANES)
                tower_stage[:, at] = big[TOWER_UNIT, core, j * HIDDEN : (j + 1) * HIDDEN].astype(F32)
        others[3].start()

    (
        predictions,
        b_proj,
        gain,
        shift,
        tower_b,
        tower_o,
        tower_e,
        roots,
        gate,
        in_b,
        out_b,
        query,
        key,
        value,
    ) = small_stages
    for j in range(2):
        predictions[:, j * LANES : (j + 1) * LANES] = jnp.where(section == 1, pred_all[j, 0:1], 0.0)

    def rows(start, count):
        found = jnp.concatenate(
            [small[0, core, j * 64 + start : j * 64 + start + count] for core in range(2) for j in range(2)],
            axis=1,
        )
        return jnp.where(section == 1, found, 0.0)

    head = rows(0, 8)
    gain[...] = head[1:2]
    shift[...] = head[2:3]
    tower_b[...] = head[3:4]
    tower_o[...] = head[4:5]
    tower_e[...] = head[5:6, 0:2]
    valid = head[5:6, 4:5]
    squares = head[5:6, 2:4] / (float(HIDDEN) * jnp.maximum(valid, 1.0)) + EPSILON
    roots[...] = jnp.where(valid > 0.0, jnp.sqrt(squares), 0.0) * second
    gate_lines, out_lines = rows(8, 8), rows(32, 8)
    in_lines = jnp.concatenate([rows(16, 8), rows(24, 8)], axis=1)
    for i in range(7):
        gate[i] = gate_lines[i : i + 1]
    for e in range(EXPERTS):
        in_b[e] = in_lines[e : e + 1]
        out_b[e] = out_lines[e : e + 1]
    three = jnp.where(section == 0, tiny[...], 0.0)
    b_proj[...] = jnp.concatenate([three[16 + i : 17 + i] for i in range(4)], axis=1)
    query[0] = three[:EMBED, 0:16]
    key[0] = three[:EMBED, 16:32]
    value[0] = three[:EMBED, 32:48]
    smalls = [
        pltpu.make_async_copy(stage, out, small_sem.at[i])
        for i, (stage, out) in enumerate(zip(small_stages, small_outs))
    ]
    for copy in smalls:
        copy.start()

    @pl.when(section == 0)
    def _():
        for e in range(EXPERTS):
            pltpu.make_async_copy(out_stage.at[0], out_grad.at[0, e], out_sem.at[2 + e]).wait()
            pltpu.make_async_copy(in_stage.at[0], in_grad.at[0, e], in_sem.at[2 + e]).wait()

    @pl.when(section == 1)
    def _():
        for e in (EXPERTS - 2, EXPERTS - 1):
            out_copy(e, e % 2).wait()
            in_copy(e, e % 2).wait()

    for copy in others + smalls:
        copy.wait()


def place(*results):
    here = pl.BlockSpec(memory_space=pltpu.VMEM)
    far = pl.BlockSpec(memory_space=pl.ANY)
    shapes = [(1, 6, 1024, 512), (1, 6, 512, 1024), (1, ROWS, FIELDS), (1, ROWS, SEQ), (1, 640, 512), (1, 512, 512)]
    shapes += SMALL_SHAPES
    return pl.pallas_call(
        place_kernel,
        out_shape=[jax.ShapeDtypeStruct(shape, F32) for shape in shapes],
        in_specs=[here] * 7,
        out_specs=[far] * 20,
        scratch_shapes=[pltpu.VMEM(shape, F32) for shape in SMALL_SHAPES]
        + [
            pltpu.VMEM((2, WIDE, HIDDEN), F32),
            pltpu.VMEM((2, HIDDEN, WIDE), F32),
            pltpu.VMEM((ROWS, SEQ), F32),
            pltpu.VMEM((ROWS, FIELDS), F32),
            pltpu.VMEM((FIELDS, HIDDEN), F32),
            pltpu.VMEM((HIDDEN, HIDDEN), F32),
            pltpu.SemaphoreType.DMA((2 + EXPERTS,)),
            pltpu.SemaphoreType.DMA((2 + EXPERTS,)),
            pltpu.SemaphoreType.DMA((4,)),
            pltpu.SemaphoreType.DMA((len(SMALL_SHAPES),)),
        ],
        compiler_params=pltpu.CompilerParams(vmem_limit_bytes=24 << 20),
        name="place",
    )(*(pltpu.with_memory_space_constraint(result, pltpu.VMEM) for result in results))


def body(
    fields,
    behaviour,
    lengths,
    domains,
    validity,
    cotangent,
    w_query,
    w_key,
    w_value,
    w_proj,
    b_proj,
    norm_gain,
    norm_shift,
    gate_weight,
    w_in,
    b_in,
    w_out,
    b_out,
    tower_in,
    tower_bias,
    tower_out,
    tower_end,
):
    def line(array):
        return array.reshape(1, -1)

    results = run(
        line(lengths),
        line(domains),
        line(validity),
        line(cotangent),
        w_query,
        w_key,
        w_value,
        line(b_proj),
        line(norm_gain),
        line(norm_shift),
        gate_weight.T,
        b_in,
        b_out,
        line(tower_bias),
        line(tower_out),
        line(tower_end),
        fields,
        w_proj,
        tower_in,
        behaviour,
        w_in,
        w_out,
    )
    (
        out_grad,
        in_grad,
        field_grad,
        seq_grad,
        proj,
        tower,
        predictions,
        b_proj_grad,
        gain,
        shift,
        tower_b,
        tower_o,
        tower_e,
        roots,
        gate,
        in_b,
        out_b,
        query,
        key,
        value,
    ) = place(*results)
    return (
        predictions,
        field_grad,
        seq_grad,
        query,
        key,
        value,
        proj,
        b_proj_grad,
        gain,
        shift,
        gate.transpose(1, 2, 0),
        in_grad,
        in_b.transpose(1, 0, 2),
        out_grad,
        out_b.transpose(1, 0, 2),
        tower,
        tower_b,
        tower_o,
        tower_e,
        roots,
    )


def solution(mesh):
    each = (P("dp", None), P("dp", None), P("dp"), P("dp"), P("dp"), P("dp"))
    ranks = (2, 3, 3, 3, 3, 3, 3, 2, 2, 2, 3, 4, 3, 4, 3, 3, 2, 2, 2, 2)
    outs = tuple(
        P("section", "dp", *(None,) * (rank - 2)) if i < 3 else P("section", *(None,) * (rank - 1))
        for i, rank in enumerate(ranks)
    )
    return jax.shard_map(
        body, mesh=mesh, in_specs=each + (P(),) * 16, out_specs=outs, check_vma=False
    )
```

```python
import jax
import jax.numpy as jnp
from jax import lax
from jax.experimental import pallas as pl
from jax.experimental.pallas import tpu as pltpu
from jax.sharding import PartitionSpec as P

EPSILON = 1e-05
MESH = pl.DeviceIdType.MESH
F32 = jnp.float32
BF16 = jnp.bfloat16

LANES = 128
DIMS = 5
HALVINGS = 3
SLOTS = 7 + HALVINGS
ROWS = 256
EXPERTS = 6
HIDDEN = 512
WIDE = 1024
FIELDS = 640
EMBED = 16
SEQ = 3200
SPAN = 256
PIECES = tuple((at, SPAN) for at in range(0, 3072, SPAN)) + ((3072, LANES),)
PROJ_ROWS = 256
SMALL_ROWS = 128
BLOCK = 128
BACK_BLOCK = 64


def coords():
    section, place = lax.axis_index("section"), lax.axis_index("dp")
    return 2 * section + place // 32, (place // 8) % 4, (place // 2) % 4, place % 2


def device_at(z, x, y, core):
    return {"section": z // 2, "dp": (((z % 2) * 4 + x) * 4 + y) * 2 + core}


def hop(r, kind):
    near, far = 1 - 2 * (r % 2), 3 - 2 * r
    return near + kind * (far - near)


def side(r, kind):
    near = (r + r // 2) % 2
    return near + kind * (r // 2 - near)


def picks(dim):
    a = dim % 3
    return (1 - a) * (2 - a) // 2, a * (2 - a), a * (a - 1) // 2, dim // 3


def neighbour(dim):
    z, x, y, core = coords()
    ex, ey, ez, kind = picks(dim)
    return device_at(z + ez * hop(z, kind), x + ex * hop(x, kind), y + ey * hop(y, kind), core)


def which_half(dim):
    z, x, y, core = coords()
    ex, ey, ez, kind = picks(dim)
    return ex * side(x, kind) + ey * side(y, kind) + ez * side(z, kind)


def sibling():
    z, x, y, core = coords()
    return device_at(z, x, y, 1 - core)


def cross():
    z, x, y, core = coords()
    return device_at(3 - z, x, y, core)


class Family:
    def __init__(self, rows, out, refs, first, here, to_other=False, unrolled=False):
        self.rows = rows
        self.share = rows >> HALVINGS
        self.out = out
        self.first = first
        self.to_other = to_other
        self.unrolled = unrolled
        self.sides, self.neighbours, self.core, self.sibling, self.cross = here
        (
            self.kept,
            self.arrived,
            self.pair_send,
            self.pair_recv,
            self.send_sem,
            self.recv_sem,
        ) = refs

    def side(self, dim):
        return self.sides[dim] if isinstance(dim, int) else which_half(dim)

    def neighbour(self, dim):
        return self.neighbours[dim] if isinstance(dim, int) else neighbour(dim)

    def total(self, units, rows=slice(None)):
        return self.out.at[units, self.core, rows]

    def remote(self, unit, slot, src, dst, to):
        return pltpu.make_async_remote_copy(
            src_ref=src,
            dst_ref=dst,
            send_sem=self.send_sem.at[slot],
            recv_sem=self.recv_sem.at[unit // DIMS, slot],
            device_id=to,
            device_id_type=MESH,
        )

    def start_of(self, part, step):
        start = 0
        for k in range(step):
            start = start + self.side((part + k) % DIMS) * (self.rows >> (k + 1))
        return start

    def span(self, start, size):
        return pl.ds(pl.multiple_of(start, size), size)

    def own_share(self, unit):
        return self.span(self.start_of(unit % DIMS, HALVINGS), self.share)

    def across(self, group, unit, count):
        return pltpu.make_async_remote_copy(
            src_ref=self.total(pl.ds(unit, count)),
            dst_ref=self.kept.at[pl.ds(unit - self.first, count)],
            send_sem=self.pair_send.at[group],
            recv_sem=self.pair_recv.at[group],
            device_id=self.sibling,
            device_id_type=MESH,
        )

    def halve(self, unit, k):
        size = self.rows >> (k + 1)
        dim = (unit + k) % DIMS
        start = self.start_of(unit % DIMS, k) + (1 - self.side(dim)) * size
        local = unit - self.first
        return self.remote(
            unit,
            k,
            self.kept.at[local, self.span(start, size)],
            self.arrived.at[local, pl.ds(self.rows - 2 * size, size)],
            self.neighbour(dim),
        )

    def double(self, unit, j):
        local = unit - self.first
        start = self.rows - self.share + j * self.share
        src = self.kept.at[local, self.own_share(unit)]
        if j:
            src = self.arrived.at[local, pl.ds(start - self.share, self.share)]
        return self.remote(
            unit,
            HALVINGS + j,
            src,
            self.arrived.at[local, pl.ds(start, self.share)],
            self.neighbour((unit + HALVINGS + j) % DIMS),
        )

    def over(self, unit):
        region = self.total(unit, self.own_share(unit))
        return self.remote(unit, DIMS, region, region, self.cross)

    def spread(self, unit, k):
        size = self.rows >> (k + 1)
        region = self.total(unit, self.span(self.start_of(unit % DIMS, k + 1), size))
        return self.remote(unit, DIMS + 1 + k, region, region, self.neighbour((unit + k) % DIMS))

    def back(self, unit, late):
        size = self.rows // 2
        own = self.side(unit % DIMS)
        region = self.total(unit, self.span((own + late * (1 - 2 * own)) * size, size))
        return self.remote(unit, DIMS + 1 + HALVINGS, region, region, self.sibling)

    def send(self, group, unit, halves):
        for i, rows in enumerate(halves):
            self.out[unit + i, self.core] = rows.astype(self.out.dtype)
        self.across(group, unit, len(halves)).start()

    def take(self, group, unit, halves):
        pair = self.across(group, unit, len(halves))
        pair.wait_send()
        pair.wait_recv()
        for i, rows in enumerate(halves):
            local = unit + i - self.first
            self.kept[local] = (rows + self.kept[local].astype(F32)).astype(self.kept.dtype)
            self.halve(unit + i, 0).start()

    def await_chunk(self, slot, base, ref):
        pltpu.make_async_copy(ref, ref, self.recv_sem.at[base // DIMS, slot]).wait()

    def each(self, base, count, work):
        if self.unrolled:
            for i in range(count):
                work(base + i)
            return

        def one(i, _):
            work(base + i)
            return 0

        lax.fori_loop(0, count, one, 0)

    def accumulate(self, here, to, start, size):
        step = min(size, LANES)

        def one(i, _):
            rows = pl.ds(pl.multiple_of(to + i * step, step), step)
            came = self.arrived[here, pl.ds(pl.multiple_of(start + i * step, step), step)]
            self.kept[here, rows] = (self.kept[here, rows].astype(F32) + came.astype(F32)).astype(self.kept.dtype)
            return 0

        lax.fori_loop(0, size // step, one, 0)

    def reduce(self, base, count, step):
        dtype = self.kept.dtype
        local = pl.ds(base - self.first, count)
        if step < HALVINGS:
            size = self.rows >> (step + 1)
            arrivals = pl.ds(self.rows - 2 * size, size)
        else:
            size = self.share
            arrivals = pl.ds(self.rows - size + (step - HALVINGS) * size, size)
        self.await_chunk(step, base, self.arrived.at[local, arrivals])

        def one(unit):
            here = unit - self.first
            if step < HALVINGS:
                self.accumulate(here, self.start_of(unit % DIMS, step + 1), arrivals.start, size)
                if step + 1 < HALVINGS:
                    self.halve(unit, step + 1).start()
                else:
                    self.double(unit, 0).start()
                return
            came = self.arrived[here, arrivals].astype(F32)
            j = step - HALVINGS
            region = self.own_share(unit)
            before = pl.ds(self.rows - size + (j - 1) * size, size)
            old = self.arrived[here, before] if j else self.kept[here, region]
            new = (old.astype(F32) + came).astype(dtype)
            if step + 1 < DIMS:
                self.arrived[here, arrivals] = new
                self.double(unit, j + 1).start()
            else:
                self.out[unit, self.core, region] = new
                if self.to_other:
                    self.over(unit).start()
                else:
                    self.spread(unit, HALVINGS - 1).start()

        self.each(base, count, one)

    def gather(self, base, count, step):
        units = pl.ds(base, count)
        if step == 0:
            self.await_chunk(DIMS, base, self.total(units, pl.ds(0, self.share)))
            self.each(base, count, lambda unit: self.spread(unit, HALVINGS - 1).start())
        elif step <= HALVINGS:
            k = HALVINGS - step
            self.await_chunk(DIMS + 1 + k, base, self.total(units, pl.ds(0, self.rows >> (k + 1))))

            def one(unit):
                if k > 0:
                    self.spread(unit, k - 1).start()
                if k < 2:
                    self.back(unit, 1 - k).start()

            self.each(base, count, one)
        else:
            self.await_chunk(DIMS + 1 + HALVINGS, base, self.out.at[units, 1 - self.core])

    def drain(self, reduced, gathered):
        def sent(slot, ref):
            pltpu.make_async_copy(ref, ref, self.send_sem.at[slot]).wait()

        for step in range(DIMS):
            size = self.rows >> (step + 1) if step < HALVINGS else self.share
            sent(step, self.kept.at[pl.ds(0, reduced), pl.ds(0, size)])
        if self.to_other:
            sent(DIMS, self.kept.at[pl.ds(0, reduced), pl.ds(0, self.share)])
        if gathered:
            for k in range(HALVINGS):
                sent(DIMS + 1 + k, self.total(pl.ds(0, gathered), pl.ds(0, self.rows >> (k + 1))))
            sent(DIMS + 1 + HALVINGS, self.total(pl.ds(0, gathered)))


def family_scratch(units, reduced, groups, rows, dtype):
    share = rows >> HALVINGS
    chunks = pl.cdiv(units, DIMS)
    return [
        pltpu.VMEM((reduced, rows, LANES), dtype),
        pltpu.VMEM((reduced, rows - share + (DIMS - HALVINGS) * share, LANES), dtype),
        pltpu.SemaphoreType.DMA((groups,)),
        pltpu.SemaphoreType.DMA((groups,)),
        pltpu.SemaphoreType.DMA((SLOTS,)),
        pltpu.SemaphoreType.DMA((chunks, SLOTS)),
    ]


FAMILIES = ((25, 15, 13, 1024, BF16), (DIMS, DIMS, 1, PROJ_ROWS, BF16), (1, 1, 1, SMALL_ROWS, F32))
TOWER_UNIT = 12
IN_UNIT = 13
SPLIT = 15
TINY_ROWS = 24


PLAN_FIRST = (
    ("ins", 1, 6), ("back", 0, 1), ("front",), ("sum", 3, 0), ("sum", 4, 0), ("send_p",), ("sum", 3, 1), ("take_p",),
    ("sum", 4, 1), ("sum", 3, 2), ("sum", 4, 2), ("sum", 3, 3), ("sum_p", 0), ("sum", 3, 4), ("sum", 4, 3),
    ("sum_p", 1), ("seq", 0, 1), ("sum", 4, 4), ("sum_p", 2), ("seq", 1, 2), ("weights",), ("tiny", 0), ("sum_p", 3),
    ("sum_p", 4), ("tiny", 1), ("tiny", 2), ("all_p", 1), ("tiny", 3), ("all_p", 2), ("tiny", 4), ("all_p", 3),
    ("tiny", 5), ("all_p", 4), ("tiny", 6),
)
PLAN_SECOND = (
    ("outs", 0, 6), ("send_t", 0), ("back", 0, 1), ("send_i", 0), ("sum", 0, 0), ("take_t", 0), ("take_i", 0),
    ("sum", 1, 0), ("back", 3, 6), ("sum", 0, 1), ("back", 1, 3), ("sum", 1, 1), ("sum", 2, 0), ("sum", 0, 2),
    ("front",), ("sum", 1, 2), ("send_v",), ("sum", 2, 1), ("sum", 0, 3), ("take_v",), ("sum", 1, 3), ("sum", 2, 2),
    ("sum", 0, 4), ("sum_v", 0), ("sum", 1, 4), ("sum", 2, 3), ("sum_v", 1), ("all", 0, 1), ("all", 1, 1),
    ("sum", 2, 4), ("sum_v", 2), ("all", 3, 0), ("all", 0, 2), ("all", 3, 1), ("sum_v", 3), ("all", 4, 0),
    ("all", 2, 1), ("all", 1, 2), ("sum_v", 4), ("all", 4, 1), ("all", 2, 2), ("all_v", 1), ("all", 4, 2),
    ("all_v", 2), ("all", 1, 3), ("all", 3, 2), ("all", 0, 3), ("all_v", 3), ("all", 4, 3), ("all_v", 4),
    ("all", 2, 3), ("all", 1, 4), ("all", 3, 3), ("all", 0, 4), ("all", 2, 4), ("all", 4, 4), ("all", 3, 4),
)


def exact(left, right):
    return jnp.dot(left, right, precision=lax.Precision.HIGHEST, preferred_element_type=F32)


def exact_cols(left, right):
    return lax.dot_general(
        left, right, (((1,), (1,)), ((), ())), precision=lax.Precision.HIGHEST, preferred_element_type=F32
    )


def exact_rows(left, right):
    return lax.dot_general(
        left, right, (((0,), (0,)), ((), ())), precision=lax.Precision.HIGHEST, preferred_element_type=F32
    )


def product(left, right):
    return jnp.dot(left, right, preferred_element_type=F32)


def contract_rows(left, right):
    return lax.dot_general(left, right, (((0,), (0,)), ((), ())), preferred_element_type=F32)


def contract_cols(left, right):
    return lax.dot_general(left, right, (((1,), (1,)), ((), ())), preferred_element_type=F32)


def split(value, terms):
    out = []
    for _ in range(terms):
        out.append(value.astype(BF16))
        value = value - out[-1].astype(F32)
    return out


def sigmoid(v):
    return 1.0 / (1.0 + jnp.exp(-v))


ROOT = 0.7978845608028654
CUBE = 0.044715


def gelu_both(v):
    square = v * v
    bent = jnp.tanh(v * (ROOT + ROOT * CUBE * square))
    half = 0.5 + 0.5 * bent
    value = v * half
    slope = half + value * (1.0 - half) * (2.0 * ROOT + 6.0 * ROOT * CUBE * square)
    return value, slope


def column_sum(array):
    return jnp.sum(array, axis=0, keepdims=True)


def row_sum(array):
    return jnp.sum(array, axis=1, keepdims=True)


def lanes(shape):
    return lax.broadcasted_iota(jnp.int32, shape, 1)


def lane_match(rows, columns, period, shift=0):
    place = lax.broadcasted_iota(jnp.int32, (rows, columns), 1) - shift
    if period:
        place = place % period
    return (place == lax.broadcasted_iota(jnp.int32, (rows, columns), 0)).astype(F32)


def kernel(
    lengths,
    domains,
    validity,
    cotangent,
    w_query,
    w_key,
    w_value,
    b_proj,
    norm_gain,
    norm_shift,
    gate_turned,
    b_in,
    b_out,
    tower_bias,
    tower_out,
    tower_end,
    fields_hbm,
    w_proj_hbm,
    tower_in_hbm,
    behaviour_hbm,
    w_in_hbm,
    w_out_hbm,
    big_out,
    proj_out,
    small_out,
    tiny_out,
    pred_all,
    d_fields,
    d_seq,
    fields,
    tower_in,
    behaviour,
    w_in,
    w_out,
    groups,
    probe_w,
    value_w,
    pooled_w,
    back_w,
    target_w,
    proj_turned,
    gate_rows,
    info,
    joined,
    activation,
    proj_slope,
    normed,
    standard,
    active,
    slope,
    expert,
    d_expert,
    d_normed,
    d_residual,
    mixing,
    d_mixing,
    gates,
    residual_low,
    d_tower,
    d_proj_low,
    pooled_rows,
    d_value_rows,
    d_probe_rows,
    small,
    tiny,
    tiny_arrived,
    load_sem,
    tiny_send,
    tiny_recv,
    *family_refs,
):
    section = lax.axis_index("section")
    core = coords()[3]

    barrier = pltpu.get_barrier_semaphore()
    for dim in range(DIMS):
        pl.semaphore_signal(barrier, inc=1, device_id=neighbour(dim), device_id_type=MESH)
    for other in (sibling(), cross()):
        pl.semaphore_signal(barrier, inc=1, device_id=other, device_id_type=MESH)

    seq_copy = pltpu.make_async_copy(behaviour_hbm, behaviour, load_sem.at[2])

    load_in = pltpu.make_async_copy(w_in_hbm, w_in, load_sem.at[0])
    load_out = pltpu.make_async_copy(w_out_hbm, w_out, load_sem.at[1])
    load_fields = pltpu.make_async_copy(fields_hbm, fields, load_sem.at[3])
    load_tower = pltpu.make_async_copy(tower_in_hbm, tower_in, load_sem.at[4])
    cut = FIELDS - EMBED
    load_proj = [
        pltpu.make_async_copy(w_proj_hbm.at[pl.ds(cut, EMBED)], proj_turned.at[pl.ds(0, EMBED)], load_sem.at[5]),
        pltpu.make_async_copy(w_proj_hbm.at[pl.ds(0, cut)], proj_turned.at[pl.ds(EMBED, cut)], load_sem.at[6]),
    ]

    tile = lane_match(EMBED, SPAN, EMBED)

    def prepare():
        seq_copy.start()
        load_fields.start()
        for copy in load_proj:
            copy.start()
        load_in.start()
        load_out.start()
        load_tower.start()
        group = lax.broadcasted_iota(jnp.int32, (SPAN, SPAN), 0) // EMBED
        groups[...] = (group == lanes((SPAN, SPAN)) // EMBED).astype(F32).astype(BF16)
        eye = lane_match(EMBED, LANES, 0)
        probe_w[...] = exact(w_query[...], exact_rows(w_key[...], tile))
        value_w[...] = exact_rows(tile, exact(w_value[...], eye))
        pooled_w[...] = exact_rows(tile, eye)
        back_w[...] = exact_rows(w_value[...], tile)
        target_w[...] = exact_rows(tile, exact(exact_cols(w_key[...], w_query[...]), eye))
        rows = [lengths[...].astype(F32), domains[...].astype(F32), validity[...].astype(F32), cotangent[...]]
        info[...] = jnp.transpose(jnp.concatenate(rows + [jnp.zeros((4, ROWS), F32)], axis=0))
        gate_rows[...] = jnp.zeros_like(gate_rows)
        gate_rows[:7] = gate_turned[...]
        small[...] = jnp.zeros_like(small)
        tiny[0] = jnp.zeros((TINY_ROWS, LANES), F32)
        seq_copy.wait()
        load_fields.wait()

    def group_sum(value, terms):
        count, width = value.shape
        stacked = jnp.concatenate(split(value, terms), axis=0)
        sums = product(stacked, groups[:width, :width])
        return sum(sums[i * count : (i + 1) * count] for i in range(terms))

    def narrow_sum(pieces):
        wide = sum(pieces[:-1])
        return jnp.concatenate([wide[:, :LANES] + pieces[-1], wide[:, LANES:]], axis=1)

    def stretch(rows, at, width):
        return behaviour[rows, at : at + width].astype(F32)

    def attention(rows):
        target = fields[rows, 0:LANES].astype(F32)[:, :EMBED]
        probe = exact(target, probe_w[...])
        length = info[rows, 0:1]
        scores = []
        for at, width in PIECES:
            sums = group_sum(stretch(rows, at, width) * probe[:, :width], 3)
            place = ((lanes((1, width)) + at) // EMBED).astype(F32)
            scores.append(jnp.where(place < length, 0.5 * sums, -1e30))
        peak = scores[0]
        for piece in scores[1:-1]:
            peak = jnp.maximum(peak, piece)
        peak = jnp.maximum(jnp.max(peak, axis=1, keepdims=True), jnp.max(scores[-1], axis=1, keepdims=True))
        raised = [jnp.exp(piece - peak) for piece in scores]
        scale = float(EMBED) / row_sum(narrow_sum(raised))
        return probe, [piece * scale for piece in raised]

    def pool(rows, attn):
        return narrow_sum([w * stretch(rows, at, width) for w, (at, width) in zip(attn, PIECES)])

    def attention_forward(block, _):
        rows = pl.ds(pl.multiple_of(block * BLOCK, BLOCK), BLOCK)
        _, attn = attention(rows)
        value = exact(pool(rows, attn), value_w[...])
        joined[rows, LANES:] = fields[rows, LANES:]
        head = fields[rows, :LANES]
        joined[rows, :LANES] = jnp.where(lanes(head.shape) < EMBED, value.astype(BF16), head)
        return 0

    def gate_columns():
        return [gates[:, i : i + 1] for i in range(6)]

    def front_forward():
        for copy in load_proj:
            copy.wait()
        projected = product(joined[...], proj_turned[...]) + b_proj[...]
        act, slope_proj = gelu_both(projected)
        activation[...] = act.astype(BF16)
        act = act.astype(BF16).astype(F32)
        proj_slope[...] = slope_proj
        centred = act - row_sum(act) * (1.0 / HIDDEN)
        scale = lax.rsqrt(row_sum(centred * centred) * (1.0 / HIDDEN) + EPSILON)
        standard[...] = centred * scale
        normed[...] = (centred * scale * norm_gain[...] + norm_shift[...]).astype(BF16)

        logits = contract_cols(normed[...], gate_rows[...])
        in_first = info[:, 1:2] == 0.0
        level = sigmoid(logits[:, 6:7])
        shared_a = sigmoid(logits[:, 0:1] - logits[:, 1:2])
        shared_b = sigmoid(logits[:, 1:2] - logits[:, 0:1])
        lead = jnp.where(in_first, logits[:, 2:3] - logits[:, 3:4], logits[:, 4:5] - logits[:, 5:6])
        chosen_a, chosen_b = sigmoid(lead), sigmoid(-lead)
        zero = jnp.zeros_like(level)
        columns = [
            level * shared_a,
            level * shared_b,
            jnp.where(in_first, (1.0 - level) * chosen_a, zero),
            jnp.where(in_first, (1.0 - level) * chosen_b, zero),
            jnp.where(in_first, zero, (1.0 - level) * chosen_a),
            jnp.where(in_first, zero, (1.0 - level) * chosen_b),
        ]
        place = lanes((ROWS, 8))
        mixing[...] = sum(jnp.where(place == i, column, 0.0) for i, column in enumerate(columns))
        held = (scale, level, shared_a, shared_b, chosen_a, chosen_b)
        gates[...] = sum(jnp.where(place == i, column, 0.0) for i, column in enumerate(held))
        d_residual[...] = jnp.zeros_like(d_residual)

    def expert_forward(e, _):
        pre = product(normed[...], w_in[e]) + b_in[pl.ds(e, 1)]
        out, grade = gelu_both(pre)
        active[e] = out.astype(BF16)
        slope[e] = grade.astype(BF16)
        rows = product(active[e], w_out[e]) + b_out[pl.ds(e, 1)]
        expert[e] = rows.astype(BF16)
        weight = row_sum(jnp.where(lanes((ROWS, 8)) == e, mixing[...], 0.0))
        d_residual[...] += weight * rows
        return 0

    def tower_both():
        load_tower.wait()
        branch = d_residual[...]
        residual = activation[...].astype(F32) + branch
        in_first = info[:, 1:2] == 0.0
        valid = info[:, 2:3]
        residual_low[...] = residual.astype(BF16)
        tower_act, tower_slope = gelu_both(product(residual_low[...], tower_in[...]) + tower_bias[...])
        chosen = jnp.where(in_first, 0, 1) == lanes((ROWS, HIDDEN)) // 256
        ends = tower_end[...]
        end = jnp.where(in_first, ends[:, 0:1], ends[:, 1:2])
        predict = sigmoid(row_sum(jnp.where(chosen, tower_act * tower_out[...], 0.0)) + end)
        d_logit = info[:, 3:4] * valid * predict * (1.0 - predict)
        spread_logit = jnp.where(chosen, d_logit, 0.0)
        d_tower[...] = (spread_logit * tower_out[...] * tower_slope).astype(BF16)
        small[3:4] = column_sum(d_tower[...].astype(F32))
        small[4:5] = column_sum(tower_act * spread_logit)
        spots = lanes((1, HIDDEN))
        parts = (
            column_sum(jnp.where(in_first, d_logit, 0.0)),
            column_sum(jnp.where(in_first, 0.0, d_logit)),
            column_sum(valid * row_sum(residual * residual)),
            column_sum(valid * row_sum(branch * branch)),
            column_sum(valid),
        )
        small[5:6] = sum(jnp.where(spots == i, part, 0.0) for i, part in enumerate(parts))
        wide = jnp.transpose(jnp.broadcast_to(predict, (ROWS, LANES)))
        pred_all[0] = wide[:8, :LANES]
        pred_all[1] = wide[:8, LANES:]
        d_residual[...] = contract_cols(d_tower[...], tower_in[...])

    def spread_residual(e, _):
        weight = row_sum(jnp.where(lanes((ROWS, 8)) == e, mixing[...], 0.0))
        low = (weight * d_residual[...]).astype(BF16)
        d_expert[e] = low
        small[pl.ds(32 + e, 1)] = column_sum(low.astype(F32))
        inner = row_sum(expert[e].astype(F32) * d_residual[...])
        d_mixing[...] = jnp.where(lanes((ROWS, 8)) == e, inner, d_mixing[...])
        return 0

    def expert_backward(e, _):
        grade = contract_cols(d_expert[e], w_out[e]) * slope[e].astype(F32)
        low = grade.astype(BF16)
        slope[e] = low
        sums = column_sum(low.astype(F32))
        small[pl.ds(16 + e, 1)] = sums[:, :512]
        small[pl.ds(24 + e, 1)] = sums[:, 512:]
        d_normed[...] += contract_cols(low, w_in[e])
        return 0

    def front_backward():
        scale, level, shared_a, shared_b, chosen_a, chosen_b = gate_columns()
        in_first = info[:, 1:2] == 0.0
        grads = [d_mixing[:, e : e + 1] for e in range(EXPERTS)]
        grad_a = jnp.where(in_first, grads[2], grads[4])
        grad_b = jnp.where(in_first, grads[3], grads[5])
        d_level = grads[0] * shared_a + grads[1] * shared_b - grad_a * chosen_a - grad_b * chosen_b
        d_shared = level * shared_a * shared_b * (grads[0] - grads[1])
        d_lead = (1.0 - level) * chosen_a * chosen_b * (grad_a - grad_b)
        zero = jnp.zeros_like(d_lead)
        d_first = jnp.where(in_first, d_lead, zero)
        d_second = jnp.where(in_first, zero, d_lead)
        columns = (d_shared, -d_shared, d_first, -d_first, d_second, -d_second, d_level * level * (1.0 - level))
        place = lanes((ROWS, LANES))
        d_logits = sum(jnp.where(place == i, column, 0.0) for i, column in enumerate(columns)).astype(BF16)
        small[8:16] = jnp.transpose(contract_rows(normed[...], d_logits))[:8]
        total = d_normed[...] + product(d_logits[:, :16], gate_rows[...])
        std = standard[...]
        small[1:2] = column_sum(total * std)
        small[2:3] = column_sum(total)
        scaled = total * norm_gain[...]
        inner = scaled - row_sum(scaled) * (1.0 / HIDDEN) - std * (row_sum(scaled * std) * (1.0 / HIDDEN))
        d_act = (inner * scale + d_residual[...]).astype(BF16).astype(F32)
        low = (d_act * proj_slope[...]).astype(BF16)
        sums = column_sum(low.astype(F32))
        for i in range(HIDDEN // LANES):
            tiny[0, 16 + i : 17 + i] = sums[:, i * LANES : (i + 1) * LANES]
        d_proj_low[...] = low

    def attention_back(block):
        rows = pl.ds(pl.multiple_of(block * BACK_BLOCK, BACK_BLOCK), BACK_BLOCK)
        probe, attn = attention(rows)
        pooled_rows[rows] = exact(pool(rows, attn), pooled_w[...])
        d_joined = contract_cols(d_proj_low[rows], proj_turned[...])
        head = d_joined[:, :LANES]
        d_value_rows[rows] = head
        d_pooled = exact(head[:, :EMBED], back_w[...])
        d_attn = [group_sum(stretch(rows, at, width) * d_pooled[:, :width], 2) for at, width in PIECES]
        inner = row_sum(narrow_sum([a * d for a, d in zip(attn, d_attn)])) * (1.0 / EMBED)
        pieces = []
        for (at, width), a, d in zip(PIECES, attn, d_attn):
            grade = 0.5 * a * (d - inner)
            pieces.append(grade * stretch(rows, at, width))
            d_seq[rows, at : at + width] = (a * d_pooled[:, :width] + grade * probe[:, :width]).astype(BF16)
        wide = narrow_sum(pieces)
        d_probe_rows[rows] = exact(wide, pooled_w[...])
        d_target = exact(wide, target_w[...])
        d_fields[rows] = d_joined
        d_fields[rows, :LANES] = jnp.where(lanes(head.shape) < EMBED, d_target, head)

    def attention_weights():
        target = fields[:, 0:LANES].astype(F32)[:, :EMBED]
        d_probe = d_probe_rows[...][:, :EMBED]
        query_grad = exact_rows(target, exact(d_probe, w_key[...]))
        key_grad = exact_rows(d_probe, exact(target, w_query[...]))
        value_grad = exact_rows(pooled_rows[...][:, :EMBED], d_value_rows[...][:, :EMBED])
        grads = (query_grad, key_grad, value_grad)
        tiny[0, :EMBED] = sum(exact(g, lane_match(EMBED, LANES, 0, EMBED * i)) for i, g in enumerate(grads))

    def out_halves(e, half):
        grad = contract_rows(active[e], d_expert[e, :, pl.ds(pl.multiple_of(half * 256, 256), 256)])
        return [grad[:, :LANES], grad[:, LANES:]]

    def in_halves(e, half):
        grad = contract_rows(normed[...], slope[e, :, pl.ds(pl.multiple_of(half * 512, 512), 512)])
        columns = [grad[:, i * LANES : (i + 1) * LANES] for i in range(4)]
        return [jnp.concatenate(columns[:2], axis=0), jnp.concatenate(columns[2:], axis=0)]

    def tower_halves(half):
        grad = contract_rows(residual_low[...], d_tower[:, pl.ds(pl.multiple_of(half * 256, 256), 256)])
        return [jnp.concatenate([grad[:, :LANES], grad[:, LANES:]], axis=0)]

    def proj_half(half):
        grad = contract_rows(joined[...], d_proj_low[:, pl.ds(pl.multiple_of(half * 256, 256), 256)])
        columns = []
        for j in range(2):
            column = grad[:, j * LANES : (j + 1) * LANES]
            columns += [column[EMBED:], column[:EMBED]]
        flat = jnp.concatenate(columns, axis=0)
        return [flat[unit * PROJ_ROWS : (unit + 1) * PROJ_ROWS] for unit in range(DIMS)]

    def small_half(half):
        columns = [small[:, pl.ds(pl.multiple_of(half * 256 + j * LANES, LANES), LANES)] for j in range(2)]
        return [jnp.concatenate(columns, axis=0)]

    def tiny_copy(step):
        return pltpu.make_async_remote_copy(
            src_ref=tiny.at[step],
            dst_ref=tiny_arrived.at[step],
            send_sem=tiny_send.at[step],
            recv_sem=tiny_recv.at[step],
            device_id=sibling() if step == DIMS else neighbour(step),
            device_id_type=MESH,
        )

    def tiny_step(step):
        if step:
            tiny_copy(step - 1).wait_recv()
            tiny[step] = tiny[step - 1] + tiny_arrived[step - 1]
        if step <= DIMS:
            tiny_copy(step).start()

    def forward_all():
        prepare()
        lax.fori_loop(0, ROWS // BLOCK, attention_forward, 0)
        front_forward()
        load_in.wait()
        load_out.wait()

        @pl.loop(0, EXPERTS, step=2)
        def _(e):
            expert_forward(e, 0)
            expert_forward(e + 1, 0)

        tower_both()
        d_normed[...] = jnp.zeros_like(d_normed)
        d_mixing[...] = jnp.zeros_like(d_mixing)
        pl.semaphore_wait(barrier, 7)

    here = (
        [which_half(dim) for dim in range(DIMS)],
        [neighbour(dim) for dim in range(DIMS)],
        core,
        sibling(),
        cross(),
    )

    def family(i, first=0, to_other=False, unrolled=False):
        out = (big_out, proj_out, small_out)[i]
        return Family(FAMILIES[i][3], out, family_refs[6 * i : 6 * i + 6], first, here, to_other, unrolled)

    def perform(plan, big, extra):
        def backs(start, end):
            lax.fori_loop(start, end, expert_backward, 0)

        def outs(start, end):
            @pl.loop(start, end + 1)
            def _(e):
                @pl.when(e < end)
                def _():
                    spread_residual(e, 0)
                    big.send(e, 2 * e, out_halves(e, 1 - core))

                @pl.when(e > start)
                def _():
                    big.take(e - 1, 2 * e - 2, out_halves(e - 1, core))

        def ins(start, end):
            @pl.loop(start, end + 1)
            def _(e):
                @pl.when(e < end)
                def _():
                    spread_residual(e, 0)
                    expert_backward(e, 0)
                    big.send(6 + e, IN_UNIT + 2 * e, in_halves(e, 1 - core))

                @pl.when(e > start)
                def _():
                    big.take(5 + e, IN_UNIT + 2 * e - 2, in_halves(e - 1, core))

        work = {
            "outs": outs,
            "ins": ins,
            "send_t": lambda e: big.send(12, TOWER_UNIT, tower_halves(1 - core)),
            "take_t": lambda e: big.take(12, TOWER_UNIT, tower_halves(core)),
            "send_i": lambda e: big.send(6 + e, IN_UNIT + 2 * e, in_halves(e, 1 - core)),
            "take_i": lambda e: big.take(6 + e, IN_UNIT + 2 * e, in_halves(e, core)),
            "back": backs,
            "front": front_backward,
            "sum": lambda c, step: big.reduce(DIMS * c, DIMS, step),
            "all": lambda c, step: big.gather(DIMS * c, DIMS, step),
            **extra,
        }
        for name, *where in plan:
            work[name](*where)

    forward_all()

    @pl.when(section == 0)
    def _():
        spread_residual(0, 0)
        big = family(0, SPLIT, True, True)
        proj = family(1, unrolled=True)
        perform(
            PLAN_FIRST,
            big,
            {
                "seq": lambda start, end: pl.loop(2 * start, 2 * end)(attention_back),
                "weights": attention_weights,
                "send_p": lambda: proj.send(0, 0, proj_half(1 - core)),
                "take_p": lambda: proj.take(0, 0, proj_half(core)),
                "sum_p": lambda step: proj.reduce(0, DIMS, step),
                "all_p": lambda step: proj.gather(0, DIMS, step),
                "tiny": tiny_step,
            },
        )
        big.drain(FAMILIES[0][0] - SPLIT, 0)
        proj.drain(DIMS, DIMS)
        for step in range(DIMS + 1):
            tiny_copy(step).wait_send()
        tiny_out[...] = tiny[DIMS + 1]

    @pl.when(section == 1)
    def _():
        big = family(0, unrolled=True)
        vectors = family(2, unrolled=True)
        perform(
            PLAN_SECOND,
            big,
            {
                "send_v": lambda: vectors.send(0, 0, small_half(1 - core)),
                "take_v": lambda: vectors.take(0, 0, small_half(core)),
                "sum_v": lambda step: vectors.reduce(0, 1, step),
                "all_v": lambda step: vectors.gather(0, 1, step),
            },
        )
        big.drain(SPLIT, FAMILIES[0][0])
        vectors.drain(1, 1)


def run(*args):
    here = pl.BlockSpec(memory_space=pltpu.VMEM)
    far = pl.BlockSpec(memory_space=pl.ANY)

    def keep(*shape, dtype=F32):
        return pltpu.VMEM(shape, dtype)

    scratch = [
        keep(ROWS, FIELDS, dtype=BF16),
        keep(HIDDEN, HIDDEN, dtype=BF16),
        keep(ROWS, SEQ, dtype=BF16),
        keep(EXPERTS, HIDDEN, WIDE, dtype=BF16),
        keep(EXPERTS, WIDE, HIDDEN, dtype=BF16),
        keep(SPAN, SPAN, dtype=BF16),
        keep(EMBED, SPAN),
        keep(SPAN, LANES),
        keep(SPAN, LANES),
        keep(EMBED, SPAN),
        keep(SPAN, LANES),
        keep(FIELDS, HIDDEN, dtype=BF16),
        keep(16, HIDDEN, dtype=BF16),
        keep(ROWS, 8),
        keep(ROWS, FIELDS, dtype=BF16),
        keep(ROWS, HIDDEN, dtype=BF16),
        keep(ROWS, HIDDEN),
        keep(ROWS, HIDDEN, dtype=BF16),
        keep(ROWS, HIDDEN),
        keep(EXPERTS, ROWS, WIDE, dtype=BF16),
        keep(EXPERTS, ROWS, WIDE, dtype=BF16),
        keep(EXPERTS, ROWS, HIDDEN, dtype=BF16),
        keep(EXPERTS, ROWS, HIDDEN, dtype=BF16),
        keep(ROWS, HIDDEN),
        keep(ROWS, HIDDEN),
        keep(ROWS, 8),
        keep(ROWS, 8),
        keep(ROWS, 8),
        keep(ROWS, HIDDEN, dtype=BF16),
        keep(ROWS, HIDDEN, dtype=BF16),
        keep(ROWS, HIDDEN, dtype=BF16),
        keep(ROWS, LANES),
        keep(ROWS, LANES),
        keep(ROWS, LANES),
        keep(64, HIDDEN),
        keep(DIMS + 2, TINY_ROWS, LANES),
        keep(DIMS + 1, TINY_ROWS, LANES),
        pltpu.SemaphoreType.DMA((7,)),
        pltpu.SemaphoreType.DMA((DIMS + 1,)),
        pltpu.SemaphoreType.DMA((DIMS + 1,)),
    ]
    for family in FAMILIES:
        scratch += family_scratch(*family)
    outs = [pltpu.VMEM((units, 2, rows, LANES), dtype) for units, _, _, rows, dtype in FAMILIES]
    outs += [
        pltpu.VMEM((TINY_ROWS, LANES), F32),
        pltpu.VMEM((2, 8, LANES), F32),
        pltpu.VMEM((ROWS, FIELDS), F32),
        pltpu.VMEM((ROWS, SEQ), BF16),
    ]
    return pl.pallas_call(
        kernel,
        out_shape=outs,
        in_specs=[here] * 16 + [far] * 6,
        out_specs=[here] * 7,
        scratch_shapes=scratch,
        compiler_params=pltpu.CompilerParams(
            collective_id=0, has_side_effects=True, vmem_limit_bytes=46 << 20
        ),
        name="rank_and_sum",
    )(*args)


SMALL_SHAPES = ((1, ROWS),) + ((1, 512),) * 5 + ((1, 2),) * 2
SMALL_SHAPES += ((7, 1, 512), (6, 1, 1024), (6, 1, 512)) + ((1, 16, 16),) * 3


def place_kernel(
    big,
    proj_units,
    small,
    tiny,
    pred_all,
    field_rows,
    seq_rows,
    out_grad,
    in_grad,
    field_grad,
    seq_grad,
    proj,
    tower,
    *rest,
):
    count = len(SMALL_SHAPES)
    small_outs, small_stages = rest[:count], rest[count : 2 * count]
    (
        out_stage,
        in_stage,
        seq_stage,
        field_stage,
        proj_stage,
        tower_stage,
        out_sem,
        in_sem,
        other_sem,
        small_sem,
    ) = rest[2 * count :]
    section = lax.axis_index("section")
    second = (section == 1).astype(F32)

    def out_copy(e, slot):
        return pltpu.make_async_copy(out_stage.at[slot], out_grad.at[0, e], out_sem.at[slot])

    def in_copy(e, slot):
        return pltpu.make_async_copy(in_stage.at[slot], in_grad.at[0, e], in_sem.at[slot])

    stages = ((seq_stage, seq_grad), (field_stage, field_grad), (proj_stage, proj), (tower_stage, tower))
    others = [pltpu.make_async_copy(stage, grad.at[0], other_sem.at[i]) for i, (stage, grad) in enumerate(stages)]

    @pl.when(section == 0)
    def _():
        out_stage[0] = jnp.zeros((WIDE, HIDDEN), F32)
        in_stage[0] = jnp.zeros((HIDDEN, WIDE), F32)
        for e in range(EXPERTS):
            pltpu.make_async_copy(out_stage.at[0], out_grad.at[0, e], out_sem.at[2 + e]).start()
            pltpu.make_async_copy(in_stage.at[0], in_grad.at[0, e], in_sem.at[2 + e]).start()
        seq_stage[...] = seq_rows[...].astype(F32)
        others[0].start()
        field_stage[...] = field_rows[...]
        others[1].start()
        for core in range(2):
            flat = jnp.concatenate([proj_units[i, core].astype(F32) for i in range(DIMS)], axis=0)
            for j in range(2):
                at = slice((2 * core + j) * LANES, (2 * core + j + 1) * LANES)
                proj_stage[:, at] = flat[j * FIELDS : (j + 1) * FIELDS]
        others[2].start()
        tower_stage[...] = jnp.zeros_like(tower_stage)
        others[3].start()

    @pl.when(section == 1)
    def _():
        field_stage[...] = jnp.zeros_like(field_stage)
        others[1].start()
        proj_stage[...] = jnp.zeros_like(proj_stage)
        others[2].start()

        @pl.loop(0, EXPERTS)
        def _(e):
            slot = e % 2

            @pl.when(e > 1)
            def _():
                out_copy(e - 2, slot).wait()

            for core in range(2):
                for j in range(2):
                    at = (2 * core + j) * LANES
                    out_stage[slot, :, at : at + LANES] = big[2 * e + j, core].astype(F32)
            out_copy(e, slot).start()

            @pl.when(e > 1)
            def _():
                in_copy(e - 2, slot).wait()

            for core in range(2):
                for j in range(2):
                    for i in range(2):
                        at = (4 * core + 2 * j + i) * LANES
                        rows = slice(i * HIDDEN, (i + 1) * HIDDEN)
                        in_stage[slot, :, at : at + LANES] = big[IN_UNIT + 2 * e + j, core, rows].astype(F32)
            in_copy(e, slot).start()

            @pl.when(e == 0)
            def _():
                seq_stage[...] = jnp.zeros_like(seq_stage)
                others[0].start()

        for core in range(2):
            for j in range(2):
                at = slice((2 * core + j) * LANES, (2 * core + j + 1) * LANES)
                tower_stage[:, at] = big[TOWER_UNIT, core, j * HIDDEN : (j + 1) * HIDDEN].astype(F32)
        others[3].start()

    (
        predictions,
        b_proj,
        gain,
        shift,
        tower_b,
        tower_o,
        tower_e,
        roots,
        gate,
        in_b,
        out_b,
        query,
        key,
        value,
    ) = small_stages
    for j in range(2):
        predictions[:, j * LANES : (j + 1) * LANES] = jnp.where(section == 1, pred_all[j, 0:1], 0.0)

    def rows(start, count):
        found = jnp.concatenate(
            [small[0, core, j * 64 + start : j * 64 + start + count] for core in range(2) for j in range(2)],
            axis=1,
        )
        return jnp.where(section == 1, found, 0.0)

    head = rows(0, 8)
    gain[...] = head[1:2]
    shift[...] = head[2:3]
    tower_b[...] = head[3:4]
    tower_o[...] = head[4:5]
    tower_e[...] = head[5:6, 0:2]
    valid = head[5:6, 4:5]
    squares = head[5:6, 2:4] / (float(HIDDEN) * jnp.maximum(valid, 1.0)) + EPSILON
    roots[...] = jnp.where(valid > 0.0, jnp.sqrt(squares), 0.0) * second
    gate_lines, out_lines = rows(8, 8), rows(32, 8)
    in_lines = jnp.concatenate([rows(16, 8), rows(24, 8)], axis=1)
    for i in range(7):
        gate[i] = gate_lines[i : i + 1]
    for e in range(EXPERTS):
        in_b[e] = in_lines[e : e + 1]
        out_b[e] = out_lines[e : e + 1]
    three = jnp.where(section == 0, tiny[...], 0.0)
    b_proj[...] = jnp.concatenate([three[16 + i : 17 + i] for i in range(4)], axis=1)
    query[0] = three[:EMBED, 0:16]
    key[0] = three[:EMBED, 16:32]
    value[0] = three[:EMBED, 32:48]
    smalls = [
        pltpu.make_async_copy(stage, out, small_sem.at[i])
        for i, (stage, out) in enumerate(zip(small_stages, small_outs))
    ]
    for copy in smalls:
        copy.start()

    @pl.when(section == 0)
    def _():
        for e in range(EXPERTS):
            pltpu.make_async_copy(out_stage.at[0], out_grad.at[0, e], out_sem.at[2 + e]).wait()
            pltpu.make_async_copy(in_stage.at[0], in_grad.at[0, e], in_sem.at[2 + e]).wait()

    @pl.when(section == 1)
    def _():
        for e in (EXPERTS - 2, EXPERTS - 1):
            out_copy(e, e % 2).wait()
            in_copy(e, e % 2).wait()

    for copy in others + smalls:
        copy.wait()


def place(*results):
    here = pl.BlockSpec(memory_space=pltpu.VMEM)
    far = pl.BlockSpec(memory_space=pl.ANY)
    shapes = [(1, 6, 1024, 512), (1, 6, 512, 1024), (1, ROWS, FIELDS), (1, ROWS, SEQ), (1, 640, 512), (1, 512, 512)]
    shapes += SMALL_SHAPES
    return pl.pallas_call(
        place_kernel,
        out_shape=[jax.ShapeDtypeStruct(shape, F32) for shape in shapes],
        in_specs=[here] * 7,
        out_specs=[far] * 20,
        scratch_shapes=[pltpu.VMEM(shape, F32) for shape in SMALL_SHAPES]
        + [
            pltpu.VMEM((2, WIDE, HIDDEN), F32),
            pltpu.VMEM((2, HIDDEN, WIDE), F32),
            pltpu.VMEM((ROWS, SEQ), F32),
            pltpu.VMEM((ROWS, FIELDS), F32),
            pltpu.VMEM((FIELDS, HIDDEN), F32),
            pltpu.VMEM((HIDDEN, HIDDEN), F32),
            pltpu.SemaphoreType.DMA((2 + EXPERTS,)),
            pltpu.SemaphoreType.DMA((2 + EXPERTS,)),
            pltpu.SemaphoreType.DMA((4,)),
            pltpu.SemaphoreType.DMA((len(SMALL_SHAPES),)),
        ],
        compiler_params=pltpu.CompilerParams(vmem_limit_bytes=24 << 20),
        name="place",
    )(*(pltpu.with_memory_space_constraint(result, pltpu.VMEM) for result in results))


def body(
    fields,
    behaviour,
    lengths,
    domains,
    validity,
    cotangent,
    w_query,
    w_key,
    w_value,
    w_proj,
    b_proj,
    norm_gain,
    norm_shift,
    gate_weight,
    w_in,
    b_in,
    w_out,
    b_out,
    tower_in,
    tower_bias,
    tower_out,
    tower_end,
):
    def line(array):
        return array.reshape(1, -1)

    results = run(
        line(lengths),
        line(domains),
        line(validity),
        line(cotangent),
        w_query,
        w_key,
        w_value,
        line(b_proj),
        line(norm_gain),
        line(norm_shift),
        gate_weight.T,
        b_in,
        b_out,
        line(tower_bias),
        line(tower_out),
        line(tower_end),
        fields,
        w_proj,
        tower_in,
        behaviour,
        w_in,
        w_out,
    )
    (
        out_grad,
        in_grad,
        field_grad,
        seq_grad,
        proj,
        tower,
        predictions,
        b_proj_grad,
        gain,
        shift,
        tower_b,
        tower_o,
        tower_e,
        roots,
        gate,
        in_b,
        out_b,
        query,
        key,
        value,
    ) = place(*results)
    return (
        predictions,
        field_grad,
        seq_grad,
        query,
        key,
        value,
        proj,
        b_proj_grad,
        gain,
        shift,
        gate.transpose(1, 2, 0),
        in_grad,
        in_b.transpose(1, 0, 2),
        out_grad,
        out_b.transpose(1, 0, 2),
        tower,
        tower_b,
        tower_o,
        tower_e,
        roots,
    )


def solution(mesh):
    each = (P("dp", None), P("dp", None), P("dp"), P("dp"), P("dp"), P("dp"))
    ranks = (2, 3, 3, 3, 3, 3, 3, 2, 2, 2, 3, 4, 3, 4, 3, 3, 2, 2, 2, 2)
    outs = tuple(
        P("section", "dp", *(None,) * (rank - 2)) if i < 3 else P("section", *(None,) * (rank - 1))
        for i, rank in enumerate(ranks)
    )
    return jax.shard_map(
        body, mesh=mesh, in_specs=each + (P(),) * 16, out_specs=outs, check_vma=False
    )
```

```python
import jax
import jax.numpy as jnp
from jax import lax
from jax.experimental import pallas as pl
from jax.experimental.pallas import tpu as pltpu
from jax.sharding import PartitionSpec as P

EPSILON = 1e-05
MESH = pl.DeviceIdType.MESH
F32 = jnp.float32
BF16 = jnp.bfloat16

LANES = 128
DIMS = 5
HALVINGS = 3
SLOTS = 7 + HALVINGS
ROWS = 256
EXPERTS = 6
HIDDEN = 512
WIDE = 1024
FIELDS = 640
EMBED = 16
SEQ = 3200
SPAN = 256
PIECES = tuple((at, SPAN) for at in range(0, 3072, SPAN)) + ((3072, LANES),)
PROJ_ROWS = 256
SMALL_ROWS = 128
BLOCK = 128
BACK_BLOCK = 64


def coords():
    section, place = lax.axis_index("section"), lax.axis_index("dp")
    return 2 * section + place // 32, (place // 8) % 4, (place // 2) % 4, place % 2


def device_at(z, x, y, core):
    return {"section": z // 2, "dp": (((z % 2) * 4 + x) * 4 + y) * 2 + core}


def hop(r, kind):
    near, far = 1 - 2 * (r % 2), 3 - 2 * r
    return near + kind * (far - near)


def side(r, kind):
    near = (r + r // 2) % 2
    return near + kind * (r // 2 - near)


def picks(dim):
    a = dim % 3
    return (1 - a) * (2 - a) // 2, a * (2 - a), a * (a - 1) // 2, dim // 3


def neighbour(dim):
    z, x, y, core = coords()
    ex, ey, ez, kind = picks(dim)
    return device_at(z + ez * hop(z, kind), x + ex * hop(x, kind), y + ey * hop(y, kind), core)


def which_half(dim):
    z, x, y, core = coords()
    ex, ey, ez, kind = picks(dim)
    return ex * side(x, kind) + ey * side(y, kind) + ez * side(z, kind)


def sibling():
    z, x, y, core = coords()
    return device_at(z, x, y, 1 - core)


def cross():
    z, x, y, core = coords()
    return device_at(3 - z, x, y, core)


class Family:
    def __init__(self, rows, out, refs, first, here, to_other=False, unrolled=False):
        self.rows = rows
        self.share = rows >> HALVINGS
        self.out = out
        self.first = first
        self.to_other = to_other
        self.unrolled = unrolled
        self.sides, self.neighbours, self.core, self.sibling, self.cross = here
        (
            self.kept,
            self.arrived,
            self.pair_send,
            self.pair_recv,
            self.send_sem,
            self.recv_sem,
        ) = refs

    def side(self, dim):
        return self.sides[dim] if isinstance(dim, int) else which_half(dim)

    def neighbour(self, dim):
        return self.neighbours[dim] if isinstance(dim, int) else neighbour(dim)

    def total(self, units, rows=slice(None)):
        return self.out.at[units, self.core, rows]

    def remote(self, unit, slot, src, dst, to):
        return pltpu.make_async_remote_copy(
            src_ref=src,
            dst_ref=dst,
            send_sem=self.send_sem.at[slot],
            recv_sem=self.recv_sem.at[unit // DIMS, slot],
            device_id=to,
            device_id_type=MESH,
        )

    def start_of(self, part, step):
        start = 0
        for k in range(step):
            start = start + self.side((part + k) % DIMS) * (self.rows >> (k + 1))
        return start

    def span(self, start, size):
        return pl.ds(pl.multiple_of(start, size), size)

    def own_share(self, unit):
        return self.span(self.start_of(unit % DIMS, HALVINGS), self.share)

    def across(self, group, unit, count):
        return pltpu.make_async_remote_copy(
            src_ref=self.total(pl.ds(unit, count)),
            dst_ref=self.kept.at[pl.ds(unit - self.first, count)],
            send_sem=self.pair_send.at[group],
            recv_sem=self.pair_recv.at[group],
            device_id=self.sibling,
            device_id_type=MESH,
        )

    def halve(self, unit, k):
        size = self.rows >> (k + 1)
        dim = (unit + k) % DIMS
        start = self.start_of(unit % DIMS, k) + (1 - self.side(dim)) * size
        local = unit - self.first
        return self.remote(
            unit,
            k,
            self.kept.at[local, self.span(start, size)],
            self.arrived.at[local, pl.ds(self.rows - 2 * size, size)],
            self.neighbour(dim),
        )

    def double(self, unit, j):
        local = unit - self.first
        start = self.rows - self.share + j * self.share
        src = self.kept.at[local, self.own_share(unit)]
        if j:
            src = self.arrived.at[local, pl.ds(start - self.share, self.share)]
        return self.remote(
            unit,
            HALVINGS + j,
            src,
            self.arrived.at[local, pl.ds(start, self.share)],
            self.neighbour((unit + HALVINGS + j) % DIMS),
        )

    def over(self, unit):
        region = self.total(unit, self.own_share(unit))
        return self.remote(unit, DIMS, region, region, self.cross)

    def spread(self, unit, k):
        size = self.rows >> (k + 1)
        region = self.total(unit, self.span(self.start_of(unit % DIMS, k + 1), size))
        return self.remote(unit, DIMS + 1 + k, region, region, self.neighbour((unit + k) % DIMS))

    def back(self, unit, late):
        size = self.rows // 2
        own = self.side(unit % DIMS)
        region = self.total(unit, self.span((own + late * (1 - 2 * own)) * size, size))
        return self.remote(unit, DIMS + 1 + HALVINGS, region, region, self.sibling)

    def send(self, group, unit, halves):
        for i, rows in enumerate(halves):
            self.out[unit + i, self.core] = rows.astype(self.out.dtype)
        self.across(group, unit, len(halves)).start()

    def take(self, group, unit, halves):
        pair = self.across(group, unit, len(halves))
        pair.wait_send()
        pair.wait_recv()
        for i, rows in enumerate(halves):
            local = unit + i - self.first
            self.kept[local] = (rows + self.kept[local].astype(F32)).astype(self.kept.dtype)
            self.halve(unit + i, 0).start()

    def await_chunk(self, slot, base, ref):
        pltpu.make_async_copy(ref, ref, self.recv_sem.at[base // DIMS, slot]).wait()

    def each(self, base, count, work):
        if self.unrolled:
            for i in range(count):
                work(base + i)
            return

        def one(i, _):
            work(base + i)
            return 0

        lax.fori_loop(0, count, one, 0)

    def accumulate(self, here, to, start, size):
        step = min(size, LANES)

        def one(i, _):
            rows = pl.ds(pl.multiple_of(to + i * step, step), step)
            came = self.arrived[here, pl.ds(pl.multiple_of(start + i * step, step), step)]
            self.kept[here, rows] = (self.kept[here, rows].astype(F32) + came.astype(F32)).astype(self.kept.dtype)
            return 0

        lax.fori_loop(0, size // step, one, 0)

    def reduce(self, base, count, step):
        dtype = self.kept.dtype
        local = pl.ds(base - self.first, count)
        if step < HALVINGS:
            size = self.rows >> (step + 1)
            arrivals = pl.ds(self.rows - 2 * size, size)
        else:
            size = self.share
            arrivals = pl.ds(self.rows - size + (step - HALVINGS) * size, size)
        self.await_chunk(step, base, self.arrived.at[local, arrivals])

        def one(unit):
            here = unit - self.first
            if step < HALVINGS:
                self.accumulate(here, self.start_of(unit % DIMS, step + 1), arrivals.start, size)
                if step + 1 < HALVINGS:
                    self.halve(unit, step + 1).start()
                else:
                    self.double(unit, 0).start()
                return
            came = self.arrived[here, arrivals].astype(F32)
            j = step - HALVINGS
            region = self.own_share(unit)
            before = pl.ds(self.rows - size + (j - 1) * size, size)
            old = self.arrived[here, before] if j else self.kept[here, region]
            new = (old.astype(F32) + came).astype(dtype)
            if step + 1 < DIMS:
                self.arrived[here, arrivals] = new
                self.double(unit, j + 1).start()
            else:
                self.out[unit, self.core, region] = new
                if self.to_other:
                    self.over(unit).start()
                else:
                    self.spread(unit, HALVINGS - 1).start()

        self.each(base, count, one)

    def gather(self, base, count, step):
        units = pl.ds(base, count)
        if step == 0:
            self.await_chunk(DIMS, base, self.total(units, pl.ds(0, self.share)))
            self.each(base, count, lambda unit: self.spread(unit, HALVINGS - 1).start())
        elif step <= HALVINGS:
            k = HALVINGS - step
            self.await_chunk(DIMS + 1 + k, base, self.total(units, pl.ds(0, self.rows >> (k + 1))))

            def one(unit):
                if k > 0:
                    self.spread(unit, k - 1).start()
                if k < 2:
                    self.back(unit, 1 - k).start()

            self.each(base, count, one)
        else:
            self.await_chunk(DIMS + 1 + HALVINGS, base, self.out.at[units, 1 - self.core])

    def drain(self, reduced, gathered):
        def sent(slot, ref):
            pltpu.make_async_copy(ref, ref, self.send_sem.at[slot]).wait()

        for step in range(DIMS):
            size = self.rows >> (step + 1) if step < HALVINGS else self.share
            sent(step, self.kept.at[pl.ds(0, reduced), pl.ds(0, size)])
        if self.to_other:
            sent(DIMS, self.kept.at[pl.ds(0, reduced), pl.ds(0, self.share)])
        if gathered:
            for k in range(HALVINGS):
                sent(DIMS + 1 + k, self.total(pl.ds(0, gathered), pl.ds(0, self.rows >> (k + 1))))
            sent(DIMS + 1 + HALVINGS, self.total(pl.ds(0, gathered)))


def family_scratch(units, reduced, groups, rows, dtype):
    share = rows >> HALVINGS
    chunks = pl.cdiv(units, DIMS)
    return [
        pltpu.VMEM((reduced, rows, LANES), dtype),
        pltpu.VMEM((reduced, rows - share + (DIMS - HALVINGS) * share, LANES), dtype),
        pltpu.SemaphoreType.DMA((groups,)),
        pltpu.SemaphoreType.DMA((groups,)),
        pltpu.SemaphoreType.DMA((SLOTS,)),
        pltpu.SemaphoreType.DMA((chunks, SLOTS)),
    ]


FAMILIES = ((25, 15, 13, 1024, BF16), (DIMS, DIMS, 1, PROJ_ROWS, BF16), (1, 1, 1, SMALL_ROWS, F32))
TOWER_UNIT = 12
IN_UNIT = 13
SPLIT = 15
TINY_ROWS = 24


PLAN_FIRST = (
    ("ins", 1, 6), ("back", 0, 1), ("sum", 3, 0), ("front",), ("sum", 4, 0), ("sum", 3, 1), ("send_p",), ("take_p",),
    ("sum", 4, 1), ("sum", 3, 2), ("sum_p", 0), ("sum", 4, 2), ("sum", 3, 3), ("sum", 4, 3), ("sum_p", 1),
    ("sum", 3, 4), ("sum", 4, 4), ("seq", 0, 1), ("sum_p", 2), ("seq", 1, 2), ("sum_p", 3), ("weights",), ("tiny", 0),
    ("sum_p", 4), ("tiny", 1), ("tiny", 2), ("all_p", 1), ("tiny", 3), ("all_p", 2), ("tiny", 4), ("all_p", 3),
    ("tiny", 5), ("all_p", 4), ("tiny", 6),
)
PLAN_SECOND = (
    ("send_t", 0), ("send_o", 0), ("send_o", 4), ("send_o", 1), ("take_t", 0), ("back", 0, 1), ("send_o", 2),
    ("send_o", 3), ("take_o", 0), ("take_o", 4), ("take_o", 1), ("send_o", 5), ("send_i", 0), ("take_o", 2),
    ("take_o", 3), ("back", 1, 3), ("take_i", 0), ("take_o", 5), ("back", 3, 6), ("sum", 0, 0), ("sum", 1, 0),
    ("front",), ("sum", 2, 0), ("sum", 0, 1), ("sum", 1, 1), ("sum", 2, 1), ("sum", 0, 2), ("sum", 1, 2),
    ("sum", 2, 2), ("sum", 0, 3), ("send_v",), ("sum", 1, 3), ("sum", 2, 3), ("take_v",), ("sum", 0, 4),
    ("sum", 1, 4), ("sum", 2, 4), ("all", 0, 1), ("all", 1, 1), ("sum_v", 0), ("all", 3, 0), ("all", 2, 1),
    ("all", 0, 2), ("all", 4, 0), ("all", 1, 2), ("all", 3, 1), ("sum_v", 1), ("sum_v", 2), ("all", 2, 2),
    ("sum_v", 3), ("all", 4, 1), ("all", 1, 3), ("sum_v", 4), ("all", 0, 3), ("all", 3, 2), ("all", 4, 2),
    ("all", 1, 4), ("all_v", 1), ("all", 3, 3), ("all", 2, 3), ("all_v", 2), ("all", 4, 3), ("all_v", 3),
    ("all", 0, 4), ("all", 2, 4), ("all", 3, 4), ("all_v", 4), ("all", 4, 4),
)


def exact(left, right):
    return jnp.dot(left, right, precision=lax.Precision.HIGHEST, preferred_element_type=F32)


def exact_cols(left, right):
    return lax.dot_general(
        left, right, (((1,), (1,)), ((), ())), precision=lax.Precision.HIGHEST, preferred_element_type=F32
    )


def exact_rows(left, right):
    return lax.dot_general(
        left, right, (((0,), (0,)), ((), ())), precision=lax.Precision.HIGHEST, preferred_element_type=F32
    )


def product(left, right):
    return jnp.dot(left, right, preferred_element_type=F32)


def contract_rows(left, right):
    return lax.dot_general(left, right, (((0,), (0,)), ((), ())), preferred_element_type=F32)


def contract_cols(left, right):
    return lax.dot_general(left, right, (((1,), (1,)), ((), ())), preferred_element_type=F32)


def split(value, terms):
    out = []
    for _ in range(terms):
        out.append(value.astype(BF16))
        value = value - out[-1].astype(F32)
    return out


def sigmoid(v):
    return 1.0 / (1.0 + jnp.exp(-v))


ROOT = 0.7978845608028654
CUBE = 0.044715


def gelu_both(v):
    square = v * v
    bent = jnp.tanh(v * (ROOT + ROOT * CUBE * square))
    half = 0.5 + 0.5 * bent
    value = v * half
    slope = half + value * (1.0 - half) * (2.0 * ROOT + 6.0 * ROOT * CUBE * square)
    return value, slope


def column_sum(array):
    return jnp.sum(array, axis=0, keepdims=True)


def row_sum(array):
    return jnp.sum(array, axis=1, keepdims=True)


def lanes(shape):
    return lax.broadcasted_iota(jnp.int32, shape, 1)


def lane_match(rows, columns, period, shift=0):
    place = lax.broadcasted_iota(jnp.int32, (rows, columns), 1) - shift
    if period:
        place = place % period
    return (place == lax.broadcasted_iota(jnp.int32, (rows, columns), 0)).astype(F32)


def kernel(
    lengths,
    domains,
    validity,
    cotangent,
    w_query,
    w_key,
    w_value,
    b_proj,
    norm_gain,
    norm_shift,
    gate_turned,
    b_in,
    b_out,
    tower_bias,
    tower_out,
    tower_end,
    fields_hbm,
    w_proj_hbm,
    tower_in_hbm,
    behaviour_hbm,
    w_in_hbm,
    w_out_hbm,
    big_out,
    proj_out,
    small_out,
    tiny_out,
    pred_all,
    d_fields,
    d_seq,
    fields,
    tower_in,
    behaviour,
    w_in,
    w_out,
    groups,
    probe_w,
    value_w,
    pooled_w,
    back_w,
    target_w,
    proj_turned,
    gate_rows,
    info,
    joined,
    activation,
    proj_slope,
    normed,
    standard,
    active,
    slope,
    expert,
    d_expert,
    d_normed,
    d_residual,
    mixing,
    d_mixing,
    gates,
    residual_low,
    d_tower,
    d_proj_low,
    pooled_rows,
    d_value_rows,
    d_probe_rows,
    small,
    tiny,
    tiny_arrived,
    load_sem,
    tiny_send,
    tiny_recv,
    *family_refs,
):
    section = lax.axis_index("section")
    core = coords()[3]

    barrier = pltpu.get_barrier_semaphore()
    for dim in range(DIMS):
        pl.semaphore_signal(barrier, inc=1, device_id=neighbour(dim), device_id_type=MESH)
    for other in (sibling(), cross()):
        pl.semaphore_signal(barrier, inc=1, device_id=other, device_id_type=MESH)

    seq_copy = pltpu.make_async_copy(behaviour_hbm, behaviour, load_sem.at[2])

    load_in = pltpu.make_async_copy(w_in_hbm, w_in, load_sem.at[0])
    load_out = pltpu.make_async_copy(w_out_hbm, w_out, load_sem.at[1])
    load_fields = pltpu.make_async_copy(fields_hbm, fields, load_sem.at[3])
    load_tower = pltpu.make_async_copy(tower_in_hbm, tower_in, load_sem.at[4])
    cut = FIELDS - EMBED
    load_proj = [
        pltpu.make_async_copy(w_proj_hbm.at[pl.ds(cut, EMBED)], proj_turned.at[pl.ds(0, EMBED)], load_sem.at[5]),
        pltpu.make_async_copy(w_proj_hbm.at[pl.ds(0, cut)], proj_turned.at[pl.ds(EMBED, cut)], load_sem.at[6]),
    ]

    tile = lane_match(EMBED, SPAN, EMBED)

    def prepare():
        seq_copy.start()
        load_fields.start()
        for copy in load_proj:
            copy.start()
        load_in.start()
        load_out.start()
        load_tower.start()
        group = lax.broadcasted_iota(jnp.int32, (SPAN, SPAN), 0) // EMBED
        groups[...] = (group == lanes((SPAN, SPAN)) // EMBED).astype(F32).astype(BF16)
        eye = lane_match(EMBED, LANES, 0)
        probe_w[...] = exact(w_query[...], exact_rows(w_key[...], tile))
        value_w[...] = exact_rows(tile, exact(w_value[...], eye))
        pooled_w[...] = exact_rows(tile, eye)
        back_w[...] = exact_rows(w_value[...], tile)
        target_w[...] = exact_rows(tile, exact(exact_cols(w_key[...], w_query[...]), eye))
        rows = [lengths[...].astype(F32), domains[...].astype(F32), validity[...].astype(F32), cotangent[...]]
        info[...] = jnp.transpose(jnp.concatenate(rows + [jnp.zeros((4, ROWS), F32)], axis=0))
        gate_rows[...] = jnp.zeros_like(gate_rows)
        gate_rows[:7] = gate_turned[...]
        small[...] = jnp.zeros_like(small)
        tiny[0] = jnp.zeros((TINY_ROWS, LANES), F32)
        seq_copy.wait()
        load_fields.wait()

    def group_sum(value, terms):
        count, width = value.shape
        stacked = jnp.concatenate(split(value, terms), axis=0)
        sums = product(stacked, groups[:width, :width])
        return sum(sums[i * count : (i + 1) * count] for i in range(terms))

    def narrow_sum(pieces):
        wide = sum(pieces[:-1])
        return jnp.concatenate([wide[:, :LANES] + pieces[-1], wide[:, LANES:]], axis=1)

    def stretch(rows, at, width):
        return behaviour[rows, at : at + width].astype(F32)

    def attention(rows):
        target = fields[rows, 0:LANES].astype(F32)[:, :EMBED]
        probe = exact(target, probe_w[...])
        length = info[rows, 0:1]
        scores = []
        for at, width in PIECES:
            sums = group_sum(stretch(rows, at, width) * probe[:, :width], 3)
            place = ((lanes((1, width)) + at) // EMBED).astype(F32)
            scores.append(jnp.where(place < length, 0.5 * sums, -1e30))
        peak = scores[0]
        for piece in scores[1:-1]:
            peak = jnp.maximum(peak, piece)
        peak = jnp.maximum(jnp.max(peak, axis=1, keepdims=True), jnp.max(scores[-1], axis=1, keepdims=True))
        raised = [jnp.exp(piece - peak) for piece in scores]
        scale = float(EMBED) / row_sum(narrow_sum(raised))
        return probe, [piece * scale for piece in raised]

    def pool(rows, attn):
        return narrow_sum([w * stretch(rows, at, width) for w, (at, width) in zip(attn, PIECES)])

    def attention_forward(block, _):
        rows = pl.ds(pl.multiple_of(block * BLOCK, BLOCK), BLOCK)
        _, attn = attention(rows)
        value = exact(pool(rows, attn), value_w[...])
        joined[rows, LANES:] = fields[rows, LANES:]
        head = fields[rows, :LANES]
        joined[rows, :LANES] = jnp.where(lanes(head.shape) < EMBED, value.astype(BF16), head)
        return 0

    def gate_columns():
        return [gates[:, i : i + 1] for i in range(6)]

    def front_forward():
        for copy in load_proj:
            copy.wait()
        projected = product(joined[...], proj_turned[...]) + b_proj[...]
        act, slope_proj = gelu_both(projected)
        activation[...] = act.astype(BF16)
        act = act.astype(BF16).astype(F32)
        proj_slope[...] = slope_proj
        centred = act - row_sum(act) * (1.0 / HIDDEN)
        scale = lax.rsqrt(row_sum(centred * centred) * (1.0 / HIDDEN) + EPSILON)
        standard[...] = centred * scale
        normed[...] = (centred * scale * norm_gain[...] + norm_shift[...]).astype(BF16)

        logits = contract_cols(normed[...], gate_rows[...])
        in_first = info[:, 1:2] == 0.0
        level = sigmoid(logits[:, 6:7])
        shared_a = sigmoid(logits[:, 0:1] - logits[:, 1:2])
        shared_b = sigmoid(logits[:, 1:2] - logits[:, 0:1])
        lead = jnp.where(in_first, logits[:, 2:3] - logits[:, 3:4], logits[:, 4:5] - logits[:, 5:6])
        chosen_a, chosen_b = sigmoid(lead), sigmoid(-lead)
        zero = jnp.zeros_like(level)
        columns = [
            level * shared_a,
            level * shared_b,
            jnp.where(in_first, (1.0 - level) * chosen_a, zero),
            jnp.where(in_first, (1.0 - level) * chosen_b, zero),
            jnp.where(in_first, zero, (1.0 - level) * chosen_a),
            jnp.where(in_first, zero, (1.0 - level) * chosen_b),
        ]
        place = lanes((ROWS, 8))
        mixing[...] = sum(jnp.where(place == i, column, 0.0) for i, column in enumerate(columns))
        held = (scale, level, shared_a, shared_b, chosen_a, chosen_b)
        gates[...] = sum(jnp.where(place == i, column, 0.0) for i, column in enumerate(held))
        d_residual[...] = jnp.zeros_like(d_residual)

    def expert_forward(e, _):
        pre = product(normed[...], w_in[e]) + b_in[pl.ds(e, 1)]
        out, grade = gelu_both(pre)
        active[e] = out.astype(BF16)
        slope[e] = grade.astype(BF16)
        rows = product(active[e], w_out[e]) + b_out[pl.ds(e, 1)]
        expert[e] = rows.astype(BF16)
        weight = row_sum(jnp.where(lanes((ROWS, 8)) == e, mixing[...], 0.0))
        d_residual[...] += weight * rows
        return 0

    def tower_both():
        load_tower.wait()
        branch = d_residual[...]
        residual = activation[...].astype(F32) + branch
        in_first = info[:, 1:2] == 0.0
        valid = info[:, 2:3]
        residual_low[...] = residual.astype(BF16)
        tower_act, tower_slope = gelu_both(product(residual_low[...], tower_in[...]) + tower_bias[...])
        chosen = jnp.where(in_first, 0, 1) == lanes((ROWS, HIDDEN)) // 256
        ends = tower_end[...]
        end = jnp.where(in_first, ends[:, 0:1], ends[:, 1:2])
        predict = sigmoid(row_sum(jnp.where(chosen, tower_act * tower_out[...], 0.0)) + end)
        d_logit = info[:, 3:4] * valid * predict * (1.0 - predict)
        spread_logit = jnp.where(chosen, d_logit, 0.0)
        d_tower[...] = (spread_logit * tower_out[...] * tower_slope).astype(BF16)
        small[3:4] = column_sum(d_tower[...].astype(F32))
        small[4:5] = column_sum(tower_act * spread_logit)
        spots = lanes((1, HIDDEN))
        parts = (
            column_sum(jnp.where(in_first, d_logit, 0.0)),
            column_sum(jnp.where(in_first, 0.0, d_logit)),
            column_sum(valid * row_sum(residual * residual)),
            column_sum(valid * row_sum(branch * branch)),
            column_sum(valid),
        )
        small[5:6] = sum(jnp.where(spots == i, part, 0.0) for i, part in enumerate(parts))
        wide = jnp.transpose(jnp.broadcast_to(predict, (ROWS, LANES)))
        pred_all[0] = wide[:8, :LANES]
        pred_all[1] = wide[:8, LANES:]
        d_residual[...] = contract_cols(d_tower[...], tower_in[...])

    def spread_residual(e, _):
        weight = row_sum(jnp.where(lanes((ROWS, 8)) == e, mixing[...], 0.0))
        low = (weight * d_residual[...]).astype(BF16)
        d_expert[e] = low
        small[pl.ds(32 + e, 1)] = column_sum(low.astype(F32))
        inner = row_sum(expert[e].astype(F32) * d_residual[...])
        d_mixing[...] = jnp.where(lanes((ROWS, 8)) == e, inner, d_mixing[...])
        return 0

    def expert_backward(e, _):
        grade = contract_cols(d_expert[e], w_out[e]) * slope[e].astype(F32)
        low = grade.astype(BF16)
        slope[e] = low
        sums = column_sum(low.astype(F32))
        small[pl.ds(16 + e, 1)] = sums[:, :512]
        small[pl.ds(24 + e, 1)] = sums[:, 512:]
        d_normed[...] += contract_cols(low, w_in[e])
        return 0

    def front_backward():
        scale, level, shared_a, shared_b, chosen_a, chosen_b = gate_columns()
        in_first = info[:, 1:2] == 0.0
        grads = [d_mixing[:, e : e + 1] for e in range(EXPERTS)]
        grad_a = jnp.where(in_first, grads[2], grads[4])
        grad_b = jnp.where(in_first, grads[3], grads[5])
        d_level = grads[0] * shared_a + grads[1] * shared_b - grad_a * chosen_a - grad_b * chosen_b
        d_shared = level * shared_a * shared_b * (grads[0] - grads[1])
        d_lead = (1.0 - level) * chosen_a * chosen_b * (grad_a - grad_b)
        zero = jnp.zeros_like(d_lead)
        d_first = jnp.where(in_first, d_lead, zero)
        d_second = jnp.where(in_first, zero, d_lead)
        columns = (d_shared, -d_shared, d_first, -d_first, d_second, -d_second, d_level * level * (1.0 - level))
        place = lanes((ROWS, LANES))
        d_logits = sum(jnp.where(place == i, column, 0.0) for i, column in enumerate(columns)).astype(BF16)
        small[8:16] = jnp.transpose(contract_rows(normed[...], d_logits))[:8]
        total = d_normed[...] + product(d_logits[:, :16], gate_rows[...])
        std = standard[...]
        small[1:2] = column_sum(total * std)
        small[2:3] = column_sum(total)
        scaled = total * norm_gain[...]
        inner = scaled - row_sum(scaled) * (1.0 / HIDDEN) - std * (row_sum(scaled * std) * (1.0 / HIDDEN))
        d_act = (inner * scale + d_residual[...]).astype(BF16).astype(F32)
        low = (d_act * proj_slope[...]).astype(BF16)
        sums = column_sum(low.astype(F32))
        for i in range(HIDDEN // LANES):
            tiny[0, 16 + i : 17 + i] = sums[:, i * LANES : (i + 1) * LANES]
        d_proj_low[...] = low

    def attention_back(block):
        rows = pl.ds(pl.multiple_of(block * BACK_BLOCK, BACK_BLOCK), BACK_BLOCK)
        probe, attn = attention(rows)
        pooled_rows[rows] = exact(pool(rows, attn), pooled_w[...])
        d_joined = contract_cols(d_proj_low[rows], proj_turned[...])
        head = d_joined[:, :LANES]
        d_value_rows[rows] = head
        d_pooled = exact(head[:, :EMBED], back_w[...])
        d_attn = [group_sum(stretch(rows, at, width) * d_pooled[:, :width], 2) for at, width in PIECES]
        inner = row_sum(narrow_sum([a * d for a, d in zip(attn, d_attn)])) * (1.0 / EMBED)
        pieces = []
        for (at, width), a, d in zip(PIECES, attn, d_attn):
            grade = 0.5 * a * (d - inner)
            pieces.append(grade * stretch(rows, at, width))
            d_seq[rows, at : at + width] = (a * d_pooled[:, :width] + grade * probe[:, :width]).astype(BF16)
        wide = narrow_sum(pieces)
        d_probe_rows[rows] = exact(wide, pooled_w[...])
        d_target = exact(wide, target_w[...])
        d_fields[rows] = d_joined
        d_fields[rows, :LANES] = jnp.where(lanes(head.shape) < EMBED, d_target, head)

    def attention_weights():
        target = fields[:, 0:LANES].astype(F32)[:, :EMBED]
        d_probe = d_probe_rows[...][:, :EMBED]
        query_grad = exact_rows(target, exact(d_probe, w_key[...]))
        key_grad = exact_rows(d_probe, exact(target, w_query[...]))
        value_grad = exact_rows(pooled_rows[...][:, :EMBED], d_value_rows[...][:, :EMBED])
        grads = (query_grad, key_grad, value_grad)
        tiny[0, :EMBED] = sum(exact(g, lane_match(EMBED, LANES, 0, EMBED * i)) for i, g in enumerate(grads))

    def out_halves(e, half):
        grad = contract_rows(active[e], d_expert[e, :, pl.ds(pl.multiple_of(half * 256, 256), 256)])
        return [grad[:, :LANES], grad[:, LANES:]]

    def in_halves(e, half):
        grad = contract_rows(normed[...], slope[e, :, pl.ds(pl.multiple_of(half * 512, 512), 512)])
        columns = [grad[:, i * LANES : (i + 1) * LANES] for i in range(4)]
        return [jnp.concatenate(columns[:2], axis=0), jnp.concatenate(columns[2:], axis=0)]

    def tower_halves(half):
        grad = contract_rows(residual_low[...], d_tower[:, pl.ds(pl.multiple_of(half * 256, 256), 256)])
        return [jnp.concatenate([grad[:, :LANES], grad[:, LANES:]], axis=0)]

    def proj_half(half):
        grad = contract_rows(joined[...], d_proj_low[:, pl.ds(pl.multiple_of(half * 256, 256), 256)])
        columns = []
        for j in range(2):
            column = grad[:, j * LANES : (j + 1) * LANES]
            columns += [column[EMBED:], column[:EMBED]]
        flat = jnp.concatenate(columns, axis=0)
        return [flat[unit * PROJ_ROWS : (unit + 1) * PROJ_ROWS] for unit in range(DIMS)]

    def small_half(half):
        columns = [small[:, pl.ds(pl.multiple_of(half * 256 + j * LANES, LANES), LANES)] for j in range(2)]
        return [jnp.concatenate(columns, axis=0)]

    def tiny_copy(step):
        return pltpu.make_async_remote_copy(
            src_ref=tiny.at[step],
            dst_ref=tiny_arrived.at[step],
            send_sem=tiny_send.at[step],
            recv_sem=tiny_recv.at[step],
            device_id=sibling() if step == DIMS else neighbour(step),
            device_id_type=MESH,
        )

    def tiny_step(step):
        if step:
            tiny_copy(step - 1).wait_recv()
            tiny[step] = tiny[step - 1] + tiny_arrived[step - 1]
        if step <= DIMS:
            tiny_copy(step).start()

    def forward_all():
        prepare()
        lax.fori_loop(0, ROWS // BLOCK, attention_forward, 0)
        front_forward()
        load_in.wait()
        load_out.wait()

        @pl.loop(0, EXPERTS, step=2)
        def _(e):
            expert_forward(e, 0)
            expert_forward(e + 1, 0)

        tower_both()
        d_normed[...] = jnp.zeros_like(d_normed)
        d_mixing[...] = jnp.zeros_like(d_mixing)
        pl.semaphore_wait(barrier, 7)

    here = (
        [which_half(dim) for dim in range(DIMS)],
        [neighbour(dim) for dim in range(DIMS)],
        core,
        sibling(),
        cross(),
    )

    def family(i, first=0, to_other=False, unrolled=False):
        out = (big_out, proj_out, small_out)[i]
        return Family(FAMILIES[i][3], out, family_refs[6 * i : 6 * i + 6], first, here, to_other, unrolled)

    def perform(plan, big, extra):
        def backs(start, end):
            lax.fori_loop(start, end, expert_backward, 0)

        def send_out(e):
            spread_residual(e, 0)
            big.send(e, 2 * e, out_halves(e, 1 - core))

        def ins(start, end):
            @pl.loop(start, end + 1)
            def _(e):
                @pl.when(e < end)
                def _():
                    spread_residual(e, 0)
                    expert_backward(e, 0)
                    big.send(6 + e, IN_UNIT + 2 * e, in_halves(e, 1 - core))

                @pl.when(e > start)
                def _():
                    big.take(5 + e, IN_UNIT + 2 * e - 2, in_halves(e - 1, core))

        work = {
            "send_o": send_out,
            "take_o": lambda e: big.take(e, 2 * e, out_halves(e, core)),
            "ins": ins,
            "send_t": lambda e: big.send(12, TOWER_UNIT, tower_halves(1 - core)),
            "take_t": lambda e: big.take(12, TOWER_UNIT, tower_halves(core)),
            "send_i": lambda e: big.send(6 + e, IN_UNIT + 2 * e, in_halves(e, 1 - core)),
            "take_i": lambda e: big.take(6 + e, IN_UNIT + 2 * e, in_halves(e, core)),
            "back": backs,
            "front": front_backward,
            "sum": lambda c, step: big.reduce(DIMS * c, DIMS, step),
            "all": lambda c, step: big.gather(DIMS * c, DIMS, step),
            **extra,
        }
        for name, *where in plan:
            work[name](*where)

    forward_all()

    @pl.when(section == 0)
    def _():
        spread_residual(0, 0)
        big = family(0, SPLIT, True, True)
        proj = family(1, unrolled=True)
        perform(
            PLAN_FIRST,
            big,
            {
                "seq": lambda start, end: pl.loop(2 * start, 2 * end)(attention_back),
                "weights": attention_weights,
                "send_p": lambda: proj.send(0, 0, proj_half(1 - core)),
                "take_p": lambda: proj.take(0, 0, proj_half(core)),
                "sum_p": lambda step: proj.reduce(0, DIMS, step),
                "all_p": lambda step: proj.gather(0, DIMS, step),
                "tiny": tiny_step,
            },
        )
        big.drain(FAMILIES[0][0] - SPLIT, 0)
        proj.drain(DIMS, DIMS)
        for step in range(DIMS + 1):
            tiny_copy(step).wait_send()
        tiny_out[...] = tiny[DIMS + 1]

    @pl.when(section == 1)
    def _():
        big = family(0, unrolled=True)
        vectors = family(2, unrolled=True)
        perform(
            PLAN_SECOND,
            big,
            {
                "send_v": lambda: vectors.send(0, 0, small_half(1 - core)),
                "take_v": lambda: vectors.take(0, 0, small_half(core)),
                "sum_v": lambda step: vectors.reduce(0, 1, step),
                "all_v": lambda step: vectors.gather(0, 1, step),
            },
        )
        big.drain(SPLIT, FAMILIES[0][0])
        vectors.drain(1, 1)


def run(*args):
    here = pl.BlockSpec(memory_space=pltpu.VMEM)
    far = pl.BlockSpec(memory_space=pl.ANY)

    def keep(*shape, dtype=F32):
        return pltpu.VMEM(shape, dtype)

    scratch = [
        keep(ROWS, FIELDS, dtype=BF16),
        keep(HIDDEN, HIDDEN, dtype=BF16),
        keep(ROWS, SEQ, dtype=BF16),
        keep(EXPERTS, HIDDEN, WIDE, dtype=BF16),
        keep(EXPERTS, WIDE, HIDDEN, dtype=BF16),
        keep(SPAN, SPAN, dtype=BF16),
        keep(EMBED, SPAN),
        keep(SPAN, LANES),
        keep(SPAN, LANES),
        keep(EMBED, SPAN),
        keep(SPAN, LANES),
        keep(FIELDS, HIDDEN, dtype=BF16),
        keep(16, HIDDEN, dtype=BF16),
        keep(ROWS, 8),
        keep(ROWS, FIELDS, dtype=BF16),
        keep(ROWS, HIDDEN, dtype=BF16),
        keep(ROWS, HIDDEN),
        keep(ROWS, HIDDEN, dtype=BF16),
        keep(ROWS, HIDDEN),
        keep(EXPERTS, ROWS, WIDE, dtype=BF16),
        keep(EXPERTS, ROWS, WIDE, dtype=BF16),
        keep(EXPERTS, ROWS, HIDDEN, dtype=BF16),
        keep(EXPERTS, ROWS, HIDDEN, dtype=BF16),
        keep(ROWS, HIDDEN),
        keep(ROWS, HIDDEN),
        keep(ROWS, 8),
        keep(ROWS, 8),
        keep(ROWS, 8),
        keep(ROWS, HIDDEN, dtype=BF16),
        keep(ROWS, HIDDEN, dtype=BF16),
        keep(ROWS, HIDDEN, dtype=BF16),
        keep(ROWS, LANES),
        keep(ROWS, LANES),
        keep(ROWS, LANES),
        keep(64, HIDDEN),
        keep(DIMS + 2, TINY_ROWS, LANES),
        keep(DIMS + 1, TINY_ROWS, LANES),
        pltpu.SemaphoreType.DMA((7,)),
        pltpu.SemaphoreType.DMA((DIMS + 1,)),
        pltpu.SemaphoreType.DMA((DIMS + 1,)),
    ]
    for family in FAMILIES:
        scratch += family_scratch(*family)
    outs = [pltpu.VMEM((units, 2, rows, LANES), dtype) for units, _, _, rows, dtype in FAMILIES]
    outs += [
        pltpu.VMEM((TINY_ROWS, LANES), F32),
        pltpu.VMEM((2, 8, LANES), F32),
        pltpu.VMEM((ROWS, FIELDS), F32),
        pltpu.VMEM((ROWS, SEQ), BF16),
    ]
    return pl.pallas_call(
        kernel,
        out_shape=outs,
        in_specs=[here] * 16 + [far] * 6,
        out_specs=[here] * 7,
        scratch_shapes=scratch,
        compiler_params=pltpu.CompilerParams(
            collective_id=0, has_side_effects=True, vmem_limit_bytes=46 << 20
        ),
        name="rank_and_sum",
    )(*args)


SMALL_SHAPES = ((1, ROWS),) + ((1, 512),) * 5 + ((1, 2),) * 2
SMALL_SHAPES += ((7, 1, 512), (6, 1, 1024), (6, 1, 512)) + ((1, 16, 16),) * 3


def place_kernel(
    big,
    proj_units,
    small,
    tiny,
    pred_all,
    field_rows,
    seq_rows,
    out_grad,
    in_grad,
    field_grad,
    seq_grad,
    proj,
    tower,
    *rest,
):
    count = len(SMALL_SHAPES)
    small_outs, small_stages = rest[:count], rest[count : 2 * count]
    (
        out_stage,
        in_stage,
        seq_stage,
        field_stage,
        proj_stage,
        tower_stage,
        out_sem,
        in_sem,
        other_sem,
        small_sem,
    ) = rest[2 * count :]
    section = lax.axis_index("section")
    second = (section == 1).astype(F32)

    def out_copy(e, slot):
        return pltpu.make_async_copy(out_stage.at[slot], out_grad.at[0, e], out_sem.at[slot])

    def in_copy(e, slot):
        return pltpu.make_async_copy(in_stage.at[slot], in_grad.at[0, e], in_sem.at[slot])

    stages = ((seq_stage, seq_grad), (field_stage, field_grad), (proj_stage, proj), (tower_stage, tower))
    others = [pltpu.make_async_copy(stage, grad.at[0], other_sem.at[i]) for i, (stage, grad) in enumerate(stages)]

    @pl.when(section == 0)
    def _():
        out_stage[0] = jnp.zeros((WIDE, HIDDEN), F32)
        in_stage[0] = jnp.zeros((HIDDEN, WIDE), F32)
        for e in range(EXPERTS):
            pltpu.make_async_copy(out_stage.at[0], out_grad.at[0, e], out_sem.at[2 + e]).start()
            pltpu.make_async_copy(in_stage.at[0], in_grad.at[0, e], in_sem.at[2 + e]).start()
        seq_stage[...] = seq_rows[...].astype(F32)
        others[0].start()
        field_stage[...] = field_rows[...]
        others[1].start()
        for core in range(2):
            flat = jnp.concatenate([proj_units[i, core].astype(F32) for i in range(DIMS)], axis=0)
            for j in range(2):
                at = slice((2 * core + j) * LANES, (2 * core + j + 1) * LANES)
                proj_stage[:, at] = flat[j * FIELDS : (j + 1) * FIELDS]
        others[2].start()
        tower_stage[...] = jnp.zeros_like(tower_stage)
        others[3].start()

    @pl.when(section == 1)
    def _():
        field_stage[...] = jnp.zeros_like(field_stage)
        others[1].start()
        proj_stage[...] = jnp.zeros_like(proj_stage)
        others[2].start()

        @pl.loop(0, EXPERTS)
        def _(e):
            slot = e % 2

            @pl.when(e > 1)
            def _():
                out_copy(e - 2, slot).wait()

            for core in range(2):
                for j in range(2):
                    at = (2 * core + j) * LANES
                    out_stage[slot, :, at : at + LANES] = big[2 * e + j, core].astype(F32)
            out_copy(e, slot).start()

            @pl.when(e > 1)
            def _():
                in_copy(e - 2, slot).wait()

            for core in range(2):
                for j in range(2):
                    for i in range(2):
                        at = (4 * core + 2 * j + i) * LANES
                        rows = slice(i * HIDDEN, (i + 1) * HIDDEN)
                        in_stage[slot, :, at : at + LANES] = big[IN_UNIT + 2 * e + j, core, rows].astype(F32)
            in_copy(e, slot).start()

            @pl.when(e == 0)
            def _():
                seq_stage[...] = jnp.zeros_like(seq_stage)
                others[0].start()

        for core in range(2):
            for j in range(2):
                at = slice((2 * core + j) * LANES, (2 * core + j + 1) * LANES)
                tower_stage[:, at] = big[TOWER_UNIT, core, j * HIDDEN : (j + 1) * HIDDEN].astype(F32)
        others[3].start()

    (
        predictions,
        b_proj,
        gain,
        shift,
        tower_b,
        tower_o,
        tower_e,
        roots,
        gate,
        in_b,
        out_b,
        query,
        key,
        value,
    ) = small_stages
    for j in range(2):
        predictions[:, j * LANES : (j + 1) * LANES] = jnp.where(section == 1, pred_all[j, 0:1], 0.0)

    def rows(start, count):
        found = jnp.concatenate(
            [small[0, core, j * 64 + start : j * 64 + start + count] for core in range(2) for j in range(2)],
            axis=1,
        )
        return jnp.where(section == 1, found, 0.0)

    head = rows(0, 8)
    gain[...] = head[1:2]
    shift[...] = head[2:3]
    tower_b[...] = head[3:4]
    tower_o[...] = head[4:5]
    tower_e[...] = head[5:6, 0:2]
    valid = head[5:6, 4:5]
    squares = head[5:6, 2:4] / (float(HIDDEN) * jnp.maximum(valid, 1.0)) + EPSILON
    roots[...] = jnp.where(valid > 0.0, jnp.sqrt(squares), 0.0) * second
    gate_lines, out_lines = rows(8, 8), rows(32, 8)
    in_lines = jnp.concatenate([rows(16, 8), rows(24, 8)], axis=1)
    for i in range(7):
        gate[i] = gate_lines[i : i + 1]
    for e in range(EXPERTS):
        in_b[e] = in_lines[e : e + 1]
        out_b[e] = out_lines[e : e + 1]
    three = jnp.where(section == 0, tiny[...], 0.0)
    b_proj[...] = jnp.concatenate([three[16 + i : 17 + i] for i in range(4)], axis=1)
    query[0] = three[:EMBED, 0:16]
    key[0] = three[:EMBED, 16:32]
    value[0] = three[:EMBED, 32:48]
    smalls = [
        pltpu.make_async_copy(stage, out, small_sem.at[i])
        for i, (stage, out) in enumerate(zip(small_stages, small_outs))
    ]
    for copy in smalls:
        copy.start()

    @pl.when(section == 0)
    def _():
        for e in range(EXPERTS):
            pltpu.make_async_copy(out_stage.at[0], out_grad.at[0, e], out_sem.at[2 + e]).wait()
            pltpu.make_async_copy(in_stage.at[0], in_grad.at[0, e], in_sem.at[2 + e]).wait()

    @pl.when(section == 1)
    def _():
        for e in (EXPERTS - 2, EXPERTS - 1):
            out_copy(e, e % 2).wait()
            in_copy(e, e % 2).wait()

    for copy in others + smalls:
        copy.wait()


def place(*results):
    here = pl.BlockSpec(memory_space=pltpu.VMEM)
    far = pl.BlockSpec(memory_space=pl.ANY)
    shapes = [(1, 6, 1024, 512), (1, 6, 512, 1024), (1, ROWS, FIELDS), (1, ROWS, SEQ), (1, 640, 512), (1, 512, 512)]
    shapes += SMALL_SHAPES
    return pl.pallas_call(
        place_kernel,
        out_shape=[jax.ShapeDtypeStruct(shape, F32) for shape in shapes],
        in_specs=[here] * 7,
        out_specs=[far] * 20,
        scratch_shapes=[pltpu.VMEM(shape, F32) for shape in SMALL_SHAPES]
        + [
            pltpu.VMEM((2, WIDE, HIDDEN), F32),
            pltpu.VMEM((2, HIDDEN, WIDE), F32),
            pltpu.VMEM((ROWS, SEQ), F32),
            pltpu.VMEM((ROWS, FIELDS), F32),
            pltpu.VMEM((FIELDS, HIDDEN), F32),
            pltpu.VMEM((HIDDEN, HIDDEN), F32),
            pltpu.SemaphoreType.DMA((2 + EXPERTS,)),
            pltpu.SemaphoreType.DMA((2 + EXPERTS,)),
            pltpu.SemaphoreType.DMA((4,)),
            pltpu.SemaphoreType.DMA((len(SMALL_SHAPES),)),
        ],
        compiler_params=pltpu.CompilerParams(vmem_limit_bytes=24 << 20),
        name="place",
    )(*(pltpu.with_memory_space_constraint(result, pltpu.VMEM) for result in results))


def body(
    fields,
    behaviour,
    lengths,
    domains,
    validity,
    cotangent,
    w_query,
    w_key,
    w_value,
    w_proj,
    b_proj,
    norm_gain,
    norm_shift,
    gate_weight,
    w_in,
    b_in,
    w_out,
    b_out,
    tower_in,
    tower_bias,
    tower_out,
    tower_end,
):
    def line(array):
        return array.reshape(1, -1)

    results = run(
        line(lengths),
        line(domains),
        line(validity),
        line(cotangent),
        w_query,
        w_key,
        w_value,
        line(b_proj),
        line(norm_gain),
        line(norm_shift),
        gate_weight.T,
        b_in,
        b_out,
        line(tower_bias),
        line(tower_out),
        line(tower_end),
        fields,
        w_proj,
        tower_in,
        behaviour,
        w_in,
        w_out,
    )
    (
        out_grad,
        in_grad,
        field_grad,
        seq_grad,
        proj,
        tower,
        predictions,
        b_proj_grad,
        gain,
        shift,
        tower_b,
        tower_o,
        tower_e,
        roots,
        gate,
        in_b,
        out_b,
        query,
        key,
        value,
    ) = place(*results)
    return (
        predictions,
        field_grad,
        seq_grad,
        query,
        key,
        value,
        proj,
        b_proj_grad,
        gain,
        shift,
        gate.transpose(1, 2, 0),
        in_grad,
        in_b.transpose(1, 0, 2),
        out_grad,
        out_b.transpose(1, 0, 2),
        tower,
        tower_b,
        tower_o,
        tower_e,
        roots,
    )


def solution(mesh):
    each = (P("dp", None), P("dp", None), P("dp"), P("dp"), P("dp"), P("dp"))
    ranks = (2, 3, 3, 3, 3, 3, 3, 2, 2, 2, 3, 4, 3, 4, 3, 3, 2, 2, 2, 2)
    outs = tuple(
        P("section", "dp", *(None,) * (rank - 2)) if i < 3 else P("section", *(None,) * (rank - 1))
        for i, rank in enumerate(ranks)
    )
    return jax.shard_map(
        body, mesh=mesh, in_specs=each + (P(),) * 16, out_specs=outs, check_vma=False
    )
```
